32 devices in a mesh: dp: 8 (over y, x, core), seq: 4 (over z).
Axes of the slice: x: 2, y: 2, z: 4, core: 2. Of those that a mesh axis runs over, the one named last changes fastest.
Arguments:
- hidden_in: bfloat16 [16, 1024, 768], P('dp', 'seq'), may hold values from -6 to 6
- seq_len: int32 [16], P('dp'), may hold values from 64 to 1024, as said below
- bucket: int32 [16], P('dp'), may hold values from 0 to 2, as said below
- in_weight: bfloat16 [768, 2304], P('dp'), may hold values from -0.21875 to 0.21875
- in_bias: float32 [2304], replicated, may hold values from -3 to 3
- short_taps: float32 [3, 2304], replicated, may hold values from -3.5 to 3.5
- cond_taps: float32 [3, 768], replicated, may hold values from -3.5 to 3.5
- mode_residue: float32 [4, 768], replicated, may hold values from -3.5 to 3.5
- mode_rate: float32 [4, 768], replicated, may hold values from 0.0001 to 0.02
- out_weight: bfloat16 [768, 768], P('dp'), may hold values from -0.21875 to 0.21875
- out_bias: float32 [768], replicated, may hold values from -3 to 3
- norm1_gain: float32 [768], replicated, may hold values from 0.5 to 1.5
- norm1_bias: float32 [768], replicated, may hold values from -1.75 to 1.75
- gate_weight: bfloat16 [768, 3072], P('dp'), may hold values from -0.21875 to 0.21875
- up_weight: bfloat16 [768, 3072], P('dp'), may hold values from -0.21875 to 0.21875
- down_weight: bfloat16 [3072, 768], P('dp'), may hold values from -0.109375 to 0.109375
- down_bias: float32 [768], replicated, may hold values from -3 to 3
- norm2_gain: float32 [768], replicated, may hold values from 0.5 to 1.5
- norm2_bias: float32 [768], replicated, may hold values from -1.75 to 1.75
- out_cotangent: bfloat16 [16, 1024, 768], P('dp', 'seq'), may hold values from -6 to 6
Outputs:
- layer_out: bfloat16 [16, 1024, 768], P('dp', 'seq')
- grad_hidden: bfloat16 [16, 1024, 768], P('dp', 'seq')
- grad_in_weight: float32 [768, 2304], P('dp')
- grad_in_bias: float32 [2304], replicated
- grad_short_taps: float32 [3, 2304], replicated
- grad_cond_taps: float32 [3, 768], replicated
- grad_mode_residue: float32 [4, 768], replicated
- grad_mode_rate: float32 [4, 768], replicated
- grad_out_weight: float32 [768, 768], P('dp')
- grad_out_bias: float32 [768], replicated
- grad_norm1_gain: float32 [768], replicated
- grad_norm1_bias: float32 [768], replicated
- grad_gate_weight: float32 [768, 3072], P('dp')
- grad_up_weight: float32 [768, 3072], P('dp')
- grad_down_weight: float32 [3072, 768], P('dp')
- grad_down_bias: float32 [768], replicated
- grad_norm2_gain: float32 [768], replicated
- grad_norm2_bias: float32 [768], replicated
The draws below stay inside these ranges and needn't reach their ends.
Inputs may be any that keep to these rules, and one draw needn't show every extreme that they name: Of the 2 rows 2 * i to 2 * i + 1, one has bucket 2. seq_len[r] lies between 1024 * 2**bucket[r] // 16 and 1024 * 2**bucket[r] // 4; of the 2 rows 2 * i to 2 * i + 1, one has length 1024.
All inputs are finite; a program needn't handle non-finite values.
Results may differ from the reference program's by a relative error of at most 0.019.
Values may be sent and summed in bfloat16 or wider, within the bound.
No kernel may reach another device: no remote copies, remote signals or barrier semaphores. Data moves between devices by JAX's collectives and lax.ppermute only.
A program may use at most 512 MiB of HBM per device.

```python
import math
import jax
import jax.numpy as jnp
from jax import lax

D = 768
FF = 3072
MODES = 4
LMAX = 1024
ROW_DEV = 2
ROWS = 16


def rows_layout(key):
    kind_key, pick_key, size_key = jax.random.split(jax.random.fold_in(key, 11), 3)
    drawn_kind = jax.random.randint(kind_key, (ROWS,), 0, 3)
    chosen = jax.random.randint(pick_key, (ROWS // ROW_DEV,), 0, ROW_DEV)
    rows_all = jnp.arange(ROWS)
    forced = rows_all % ROW_DEV == jnp.repeat(chosen, ROW_DEV)
    kind_rows = jnp.where(forced, 2, drawn_kind).astype(jnp.int32)
    capacity = LMAX // 4 * jnp.left_shift(jnp.int32(1), kind_rows)
    lower_len = capacity // 4
    size_rows = jax.random.randint(size_key, (ROWS,), lower_len, capacity + 1)
    size_rows = jnp.where(forced, LMAX, size_rows).astype(jnp.int32)
    return (kind_rows, size_rows)


def draw_bucket(key, part):
    return rows_layout(key)[0]


def draw_seq_len(key, part):
    return rows_layout(key)[1]


def draw_mode_rate(key, part):
    key = jax.random.fold_in(key, 23)
    low_end = math.log(0.0001)
    high_end = math.log(0.02)
    uniform_draw = jax.random.uniform(key, (MODES, D), jnp.float32)
    return jnp.exp(low_end + (high_end - low_end) * uniform_draw)


def steps_of(own_key, shape, pieces, least, top_value):
    gain = 1.0
    for dim, blocks in pieces:
        draws = jax.random.uniform(jax.random.fold_in(jax.random.fold_in(own_key, 6), dim), (blocks,), jnp.float32, least / len(pieces), top_value / len(pieces))
        gain = gain * jnp.repeat(jnp.exp(draws), shape[dim] // blocks).reshape((-1,) + (1,) * (len(shape) - 1 - dim))
    return gain


def gaussian(key, dims, scale, bound, pieces=(), kind=jnp.bfloat16):
    entries = jax.random.normal(key, dims, jnp.float32) * scale
    if len(pieces) > 0:
        entries = steps_of(key, dims, pieces, -0.22, 0.18) * entries
    return jnp.clip(entries, min=-bound, max=bound).astype(kind)


def setup_inputs(seed: int = 0) -> dict:
    key_of = jax.random.split(jax.random.key(seed), 21)
    hidden_in = gaussian(key_of[0], (ROWS, LMAX, D), 1.0, 6.0, ((0, 8), (1, 4)))
    seq_len = draw_seq_len(jax.random.fold_in(key_of[20], 71), 0)
    bucket = draw_bucket(jax.random.fold_in(key_of[20], 71), 0)
    in_weight = gaussian(key_of[3], (D, 3 * D), D ** -0.5, 0.21875, ((0, 8),))
    in_bias = gaussian(key_of[4], (3 * D,), 0.5, 3.0, (), jnp.float32)
    short_taps = gaussian(key_of[5], (3, 3 * D), 0.6, 3.5, (), jnp.float32)
    cond_taps = gaussian(key_of[6], (3, D), 0.6, 3.5, (), jnp.float32)
    mode_residue = gaussian(key_of[7], (MODES, D), 0.6, 3.5, (), jnp.float32)
    mode_rate = draw_mode_rate(jax.random.fold_in(key_of[20], 71), 0)
    out_weight = gaussian(key_of[9], (D, D), D ** -0.5, 0.21875, ((0, 8),))
    out_bias = gaussian(key_of[10], (D,), 0.5, 3.0, (), jnp.float32)
    norm1_gain = jnp.clip(1.0 + 0.1 * jax.random.normal(key_of[11], (D,), jnp.float32), 0.5, 1.5)
    norm1_bias = gaussian(key_of[12], (D,), 0.3, 1.75, (), jnp.float32)
    gate_weight = gaussian(key_of[13], (D, FF), D ** -0.5, 0.21875, ((0, 8),))
    up_weight = gaussian(key_of[14], (D, FF), D ** -0.5, 0.21875, ((0, 8),))
    down_weight = gaussian(key_of[15], (FF, D), FF ** -0.5, 0.109375, ((0, 8),))
    down_bias = gaussian(key_of[16], (D,), 0.5, 3.0, (), jnp.float32)
    norm2_gain = jnp.clip(1.0 + 0.1 * jax.random.normal(key_of[17], (D,), jnp.float32), 0.5, 1.5)
    norm2_bias = gaussian(key_of[18], (D,), 0.3, 1.75, (), jnp.float32)
    out_cotangent = gaussian(key_of[19], (ROWS, LMAX, D), 1.0, 6.0, ((0, 8), (1, 4)))
    return dict(hidden_in=hidden_in, seq_len=seq_len, bucket=bucket, in_weight=in_weight, in_bias=in_bias, short_taps=short_taps, cond_taps=cond_taps, mode_residue=mode_residue, mode_rate=mode_rate, out_weight=out_weight, out_bias=out_bias, norm1_gain=norm1_gain, norm1_bias=norm1_bias, gate_weight=gate_weight, up_weight=up_weight, down_weight=down_weight, down_bias=down_bias, norm2_gain=norm2_gain, norm2_bias=norm2_bias, out_cotangent=out_cotangent)


@jax.custom_vjp
def low(v):
    return lax.optimization_barrier(v.astype(jnp.bfloat16)).astype(jnp.float32)

@jax.custom_vjp
def low_back(v):
    return v

def low_keep(v):
    return (low(v), None)

def low_pass(kept, grad):
    return (grad,)

def back_keep(v):
    return (v, None)

def back_low(kept, grad):
    return (low(grad),)
low.defvjp(low_keep, low_pass)
low_back.defvjp(back_keep, back_low)

def layer_norm(values, gain_vec, shifts):
    centre = values - lax.optimization_barrier(jnp.mean(values, axis=-1, keepdims=True))
    spread = lax.optimization_barrier(jnp.mean(centre * centre, axis=-1, keepdims=True))
    return centre * lax.rsqrt(spread + 1e-05) * gain_vec + shifts

def product(left_side, right_side):
    return jnp.dot(left_side, right_side, precision=lax.Precision.HIGHEST, preferred_element_type=jnp.float32)

def depthwise(signal, kernel_taps):
    padded = jnp.pad(signal, ((1, 1), (0, 0)))
    return kernel_taps[0] * padded[:-2] + kernel_taps[1] * padded[1:-1] + kernel_taps[2] * padded[2:]

def long_kernel(mode_residue, mode_rate, factor):
    lag_steps = jnp.arange(LMAX).astype(jnp.float32)
    decays = mode_rate * factor
    weight = mode_residue * jnp.sqrt(1.0 - jnp.exp(-2.0 * decays))
    return lax.optimization_barrier(jnp.sum(weight[:, None, :] * jnp.exp(-decays[:, None, :] * lag_steps[None, :, None]), axis=0))

def causal_conv(source, kernel_rows):
    fft_length = 2 * LMAX
    spectrum = jnp.fft.rfft(source, n=fft_length, axis=0) * jnp.fft.rfft(kernel_rows, n=fft_length, axis=0)
    return jnp.fft.irfft(spectrum, n=fft_length, axis=0)[:LMAX]

def layer_row(tokens_row, row_mask, factor, params):
    in_weight, in_bias, short_taps, cond_taps, mode_residue, mode_rate, out_weight, out_bias, norm1_gain, norm1_bias, gate_weight, up_weight, down_weight, down_bias, norm2_gain, norm2_bias = params
    keep_rows = row_mask[:, None]
    model_width = tokens_row.shape[1]
    projected = low_back(product(tokens_row, in_weight) + in_bias)
    rounded = low(projected * keep_rows)
    shorted = depthwise(rounded, short_taps)
    key_part = depthwise(shorted[:, model_width:2 * model_width], cond_taps)
    mixed_in = low_back(jnp.concatenate([shorted[:, :model_width], key_part, shorted[:, 2 * model_width:]], axis=1))
    queries = mixed_in[:, :model_width]
    source = mixed_in[:, model_width:2 * model_width] * mixed_in[:, 2 * model_width:] * keep_rows
    long_out = causal_conv(source, long_kernel(mode_residue, mode_rate, factor))
    gated_out = low(queries * long_out * keep_rows)
    mixer_out = low_back(product(gated_out, out_weight) + out_bias)
    normed_one = layer_norm(tokens_row + mixer_out, norm1_gain, norm1_bias)
    first_low = low(normed_one)
    gate_pre = low_back(product(first_low, gate_weight))
    up_pre = low_back(product(first_low, up_weight))
    active = low(jax.nn.gelu(gate_pre, approximate=True) * up_pre)
    feed_out = low_back(product(active, down_weight) + down_bias)
    return layer_norm(normed_one + feed_out, norm2_gain, norm2_bias) * keep_rows

def reference(hidden_in, seq_len, bucket, in_weight, in_bias, short_taps, cond_taps, mode_residue, mode_rate, out_weight, out_bias, norm1_gain, norm1_bias, gate_weight, up_weight, down_weight, down_bias, norm2_gain, norm2_bias, out_cotangent):
    params = (in_weight.astype(jnp.float32), in_bias, short_taps, cond_taps, mode_residue, mode_rate, out_weight.astype(jnp.float32), out_bias, norm1_gain, norm1_bias, gate_weight.astype(jnp.float32), up_weight.astype(jnp.float32), down_weight.astype(jnp.float32), down_bias, norm2_gain, norm2_bias)
    positions = jnp.arange(LMAX).astype(jnp.int32)
    row_masks = (positions[None, :] < seq_len[:, None].astype(jnp.int32)).astype(jnp.float32)
    factors = jnp.where(bucket == 0, 4.0, jnp.where(bucket == 1, 2.0, 1.0)).astype(jnp.float32)

    def one_row(totals, inputs):
        tokens_row, row_mask, factor, cotangent = inputs

        def forward(data, weights):
            return layer_row(data, row_mask, factor, weights)
        result, pullback = jax.vjp(forward, tokens_row.astype(jnp.float32), params)
        data_grad, weight_grads = pullback(cotangent.astype(jnp.float32))
        totals = jax.tree.map(lambda total_part, grad_part: total_part + grad_part, totals, weight_grads)
        return (totals, (result.astype(jnp.bfloat16), data_grad.astype(jnp.bfloat16)))
    zero_grads = jax.tree.map(jnp.zeros_like, params)
    totals, (outputs, input_grads) = lax.scan(one_row, zero_grads, (hidden_in, row_masks, factors, out_cotangent))
    grad_in_weight, grad_in_bias, grad_short, grad_cond, grad_residue, grad_rate, grad_out_weight, grad_out_bias, grad_gain_one, grad_shift_one, grad_gate, grad_up, grad_down, grad_down_bias, grad_gain_two, grad_shift_two = totals
    return (outputs, input_grads, grad_in_weight, grad_in_bias, grad_short, grad_cond, grad_residue, grad_rate, grad_out_weight, grad_out_bias, grad_gain_one, grad_shift_one, grad_gate, grad_up, grad_down, grad_down_bias, grad_gain_two, grad_shift_two)
```

```python
import jax
import jax.numpy as jnp
from jax import lax
from jax.experimental import pallas as pl
from jax.experimental.pallas import tpu as pltpu
from jax.sharding import PartitionSpec as P

norm_eps = 1e-05
f32 = jnp.float32
bf16 = jnp.bfloat16
segs = 8
lane_block = 256
vmem_cap = 56 * 1024 * 1024


def iota(shape, dim):
    return lax.broadcasted_iota(jnp.int32, shape, dim)


def factor_of(info, rows, r):
    b = info[rows + r]
    return jnp.where(b == 0, 4.0, jnp.where(b == 1, 2.0, 1.0)).astype(f32)


def order_matrix(span):
    seg = span // segs
    o, n = iota((span, span), 0), iota((span, span), 1)
    return (n == (o & (segs - 1)) * seg + lax.shift_right_logical(o, 3)).astype(f32).astype(bf16)


def fill_edges(ext, r, seg, halo, cols):
    n = cols[1]
    c = pl.ds(cols[0], n)
    sub = iota((segs, n), 0)
    for h, (dst, src, shift, edge) in enumerate(
        ((0, seg, 1, 0), (1, seg + 1, 1, 0), (seg + 2, 2, segs - 1, segs - 1), (seg + 3, 3, segs - 1, segs - 1))
    ):
        rolled = pltpu.roll(ext[r, src, :, c], shift, 0)
        ext[r, dst, :, c] = jnp.where(sub == edge, halo[pl.ds(4 * r + h, 1), c], rolled)


def fetch_parts(where, parts, full, sems):
    depth = parts[0].shape[0]
    return [
        pltpu.make_async_copy(
            part, full.at[pl.ds(pl.multiple_of(where[k] * depth, 16), depth)], sems.at[k]
        )
        for k, part in enumerate(parts)
    ]


def start_all(copies):
    for copy in copies:
        copy.start()


def wait_all(copies):
    for copy in copies:
        copy.wait()


def send_parts(where, full, outs, sems, cols=None):
    per, depth = outs[0].shape[0], outs[0].shape[1]
    copies = []
    for k in range(per * len(outs)):
        rows_of = pl.ds(pl.multiple_of(where[k] * depth, 16), depth)
        src, dst = full.at[rows_of], outs[k // per].at[k % per]
        if cols is not None:
            src, dst = full.at[rows_of, cols], outs[k // per].at[k % per, :, cols]
        copies.append(pltpu.make_async_copy(src, dst, sems.at[k]))
    return copies


def enter_kernel(rows, span, seq_count, count, info, where, x, cot, xh, bias, st, ct, rate, *refs):
    parts, refs = refs[:count], refs[count:]
    xp, xpt, cp, ext, q, keys, vals, ends, dev_end, mask, hal, w, sems = refs
    copies = fetch_parts(where, parts, w, sems)
    start_all(copies)
    width = x.shape[2]
    seg = span // segs
    place = info[2 * rows]
    base = place * span
    order = order_matrix(span)
    for r in range(rows):
        moved = jnp.dot(order, x[r], preferred_element_type=f32).astype(bf16)
        xp[pl.ds(r * span, span), :] = moved
        xpt[:, pl.ds(r * span, span)] = moved.T
        cp[pl.ds(r * span, span), :] = jnp.dot(order, cot[r], preferred_element_type=f32).astype(bf16)
        n = iota((span, 128), 0)
        pos = base + (n & (segs - 1)) * seg + lax.shift_right_logical(n, 3)
        mask[pl.ds(r * span, span), :] = (pos < info[r]).astype(f32)
    hn = iota((16, 128), 0)
    hk = hn & 3
    hpos = base + jnp.where(hk < 2, hk - 2, span + hk - 2)
    hlim = jnp.where(lax.shift_right_logical(hn, 2) == 0, info[0], info[1])
    hmask = ((hpos >= 0) & (hpos < hlim)).astype(f32)
    wait_all(copies)

    @pl.loop(0, 3 * width // lane_block)
    def _(t):
        cols = pl.ds(pl.multiple_of(t * lane_block, lane_block), lane_block)
        part = jnp.dot(xp[...], w[:, cols], preferred_element_type=f32) + bias[:, cols]
        rim = jnp.dot(xh[...], w[:, cols], preferred_element_type=f32) + bias[:, cols]
        for s in range(lane_block // 128):
            sub = slice(s * 128, (s + 1) * 128)
            scol = pl.ds(pl.multiple_of(t * lane_block + s * 128, 128), 128)
            low = (part[:, sub] * mask[...]).astype(bf16).astype(f32)
            for r in range(rows):
                ext[r, pl.ds(2, seg), :, scol] = low[r * span : (r + 1) * span].reshape(seg, segs, 128)
            hal[:, scol] = (rim[:, sub] * hmask).astype(bf16).astype(f32)

    sub = iota((segs, lane_block), 0)
    first = (place == 0).astype(f32)
    last = (place == seq_count - 1).astype(f32)
    in_low = 1.0 - first * (sub == 0).astype(f32)
    in_high = 1.0 - last * (sub == segs - 1).astype(f32)
    for r in range(rows):
        factor = factor_of(info, rows, r)
        for t in range(3 * width // lane_block):
            fill_edges(ext, r, seg, hal, (t * lane_block, lane_block))
        for t in range(width // lane_block):
            cq = pl.ds(t * lane_block, lane_block)
            ck = pl.ds(width + t * lane_block, lane_block)
            cv = pl.ds(2 * width + t * lane_block, lane_block)
            modes = rate.shape[0]
            fade = [jnp.exp(-rate[pl.ds(m, 1), cq] * factor) for m in range(modes)]
            far = [jnp.exp(-rate[pl.ds(m, 1), cq] * (factor * seg)) for m in range(modes)]

            def tap3(cols, e):
                return (
                    st[pl.ds(0, 1), cols] * ext[r, e - 1, :, cols]
                    + st[pl.ds(1, 1), cols] * ext[r, e, :, cols]
                    + st[pl.ds(2, 1), cols] * ext[r, e + 1, :, cols]
                )

            def step(j, carry):
                kp_prev, kp_cur, states = carry
                kp_next = tap3(ck, j + 3)
                kp_next = jnp.where(j == seg - 1, kp_next * in_high, kp_next)
                key = (
                    ct[pl.ds(0, 1), cq] * kp_prev
                    + ct[pl.ds(1, 1), cq] * kp_cur
                    + ct[pl.ds(2, 1), cq] * kp_next
                )
                val = tap3(cv, j + 2)
                q[r, j, :, cq] = tap3(cq, j + 2)
                keys[r, j, :, cq] = key
                vals[r, j, :, cq] = val
                live = (base + sub * seg + j < info[r]).astype(f32)
                src = key * val * live
                return (kp_cur, kp_next, tuple(f * h + src for f, h in zip(fade, states)))

            zero = jnp.zeros((segs, lane_block), f32)
            start = (tap3(ck, 1) * in_low, tap3(ck, 2), (zero,) * modes)
            _, _, states = lax.fori_loop(0, seg, step, start)
            for m in range(modes):
                ends[r, m, :, cq] = states[m]
                total = jnp.zeros((1, lane_block), f32)
                for i in range(segs):
                    total = far[m] * total + states[m][i : i + 1]
                dev_end[r, pl.ds(m, 1), cq] = total


def vm(shape, dtype=f32):
    return jax.ShapeDtypeStruct(shape, dtype)


def vmem_specs(n):
    return [pl.BlockSpec(memory_space=pltpu.VMEM)] * n


def smem_spec():
    return [pl.BlockSpec(memory_space=pltpu.SMEM)]


def cost(flops, nbytes):
    return pl.CostEstimate(flops=int(flops), bytes_accessed=int(nbytes), transcendentals=0)


def any_specs(n):
    return [pl.BlockSpec(memory_space=pl.ANY)] * n


def mixer_enter(info, where, hidden, cot, halo, bias, st, ct, rate, parts, seq_count):
    rows, span, width = hidden.shape
    seg, modes, tokens = span // segs, rate.shape[0], rows * span
    body = (rows, seg, segs, width)
    return pl.pallas_call(
        lambda *refs: enter_kernel(rows, span, seq_count, len(parts), *refs),
        out_shape=(
            vm((tokens, width), bf16),
            vm((width, tokens), bf16),
            vm((tokens, width), bf16),
            vm((rows, seg + 4, segs, 3 * width)),
            vm(body),
            vm(body),
            vm(body),
            vm((rows, modes, segs, width)),
            vm((rows, modes, width)),
        ),
        in_specs=smem_spec() * 2 + vmem_specs(7) + any_specs(len(parts)),
        out_specs=tuple(vmem_specs(9)),
        scratch_shapes=[
            pltpu.VMEM((tokens, 128), f32),
            pltpu.VMEM((16, 3 * width), f32),
            pltpu.VMEM((width, 3 * width), bf16),
            pltpu.SemaphoreType.DMA((len(parts),)),
        ],
        compiler_params=pltpu.CompilerParams(vmem_limit_bytes=vmem_cap),
        cost_estimate=cost(2 * tokens * width * width * 3, 20e6),
        name="mixer_enter",
    )(info, where, hidden, cot, halo, bias, st, ct, rate, *parts)


def carry_in(parts, fade_span):
    total = parts[0]
    scale = fade_span
    for p in parts[1:]:
        total = total + scale * p
        scale = scale * fade_span
    return total


def settle_kernel(rows, span, others, count, info, where, *refs):
    gath, refs = refs[:others], refs[others:]
    parts, refs = refs[:count], refs[count:]
    ends, q, keys, vals, rate, res, xp, ob, long_out, gated_t, carry_out, n1, s1, gsc, wo, sems = refs
    copies = fetch_parts(where, parts, wo, sems)
    start_all(copies)
    seg = span // segs
    width = q.shape[3]
    modes = rate.shape[0]
    base = info[2 * rows] * span
    sub = iota((segs, lane_block), 0)
    for r in range(rows):
        factor = factor_of(info, rows, r)
        for t in range(width // lane_block):
            c = pl.ds(t * lane_block, lane_block)
            fade, mix, start = [], [], []
            for m in range(modes):
                d = rate[pl.ds(m, 1), c] * factor
                fade.append(jnp.exp(-d))
                mix.append(res[pl.ds(m, 1), c] * jnp.sqrt(1.0 - jnp.exp(-2.0 * d)))
                far = jnp.exp(-d * seg)
                cur = carry_in([g[r, pl.ds(m, 1), c] for g in gath], jnp.exp(-d * span))
                tile = jnp.zeros((segs, lane_block), f32)
                end = ends[r, m, :, c]
                for i in range(segs):
                    tile = jnp.where(sub == i, cur, tile)
                    cur = far * cur + end[i : i + 1]
                carry_out[r, m, :, c] = tile
                start.append(tile)

            def step(j, states):
                live = (base + sub * seg + j < info[r]).astype(f32)
                src = keys[r, j, :, c] * vals[r, j, :, c] * live
                states = tuple(f * h + src for f, h in zip(fade, states))
                out = mix[0] * states[0]
                for m in range(1, modes):
                    out = out + mix[m] * states[m]
                long_out[r, j, :, c] = out
                gsc[r, j, :, c] = q[r, j, :, c] * out * live
                return states

            lax.fori_loop(0, seg, step, tuple(start))
    wait_all(copies)
    for r in range(rows):
        tok = pl.ds(r * span, span)
        low = gsc[r].reshape(span, width).astype(bf16)
        gated_t[:, tok] = low.T
        n1[tok, :] = xp[tok, :].astype(f32) + jnp.dot(low, wo[...], preferred_element_type=f32) + ob[...]

    @pl.loop(0, rows * span // 16)
    def _(k):
        tok = pl.ds(pl.multiple_of(k * 16, 16), 16)
        v = n1[tok, :]
        centre = v - jnp.mean(v, axis=-1, keepdims=True)
        inv = lax.rsqrt(jnp.mean(centre * centre, axis=-1, keepdims=True) + norm_eps)
        n1[tok, :] = centre * inv
        s1[tok, :] = jnp.broadcast_to(inv, (16, 128))


def mixer_settle(info, where, gath, ends, q, keys, vals, rate, res, xp, ob, parts):
    rows, seg, _, width = q.shape
    span = seg * segs
    tokens, modes = rows * span, rate.shape[0]
    return pl.pallas_call(
        lambda *refs: settle_kernel(rows, span, len(gath), len(parts), *refs),
        out_shape=(
            vm(q.shape),
            vm((width, tokens), bf16),
            vm(ends.shape),
            vm((tokens, width)),
            vm((tokens, 128)),
        ),
        in_specs=smem_spec() * 2 + vmem_specs(len(gath)) + any_specs(len(parts)) + vmem_specs(8),
        out_specs=tuple(vmem_specs(5)),
        scratch_shapes=[
            pltpu.VMEM(q.shape, f32),
            pltpu.VMEM((width, width), bf16),
            pltpu.SemaphoreType.DMA((len(parts),)),
        ],
        compiler_params=pltpu.CompilerParams(vmem_limit_bytes=vmem_cap),
        cost_estimate=cost(2 * tokens * width * width, 12e6),
        name="mixer_settle",
    )(info, where, *gath, *parts, ends, q, keys, vals, rate, res, xp, ob)


def gelu_kernel(count, where, n1, gain, shift, *refs):
    gate_parts, up_parts, refs = refs[:count], refs[count : 2 * count], refs[2 * count :]
    low_t, act, act_t, pull, gel, wg, wu, low, gs, us, sems = refs
    tile = act.shape[1]
    i = pl.program_id(0)

    @pl.when(i == 0)
    def _():
        gate_copies = fetch_parts(where, gate_parts, wg, sems.at[0])
        up_copies = fetch_parts(where, up_parts, wu, sems.at[1])
        start_all(gate_copies)
        start_all(up_copies)
        low[...] = (n1[...] * gain[...] + shift[...]).astype(bf16)
        low_t[...] = low[...].T
        wait_all(gate_copies)
        wait_all(up_copies)

    cols = pl.ds(pl.multiple_of(i * tile, tile), tile)
    gs[...] = jnp.dot(low[...], wg[:, cols], preferred_element_type=f32)
    us[...] = jnp.dot(low[...], wu[:, cols], preferred_element_type=f32)
    scale = 0.7978845608028654

    @pl.loop(0, act.shape[0] // 16)
    def _(k):
        tok = pl.ds(pl.multiple_of(k * 16, 16), 16)
        g, u = gs[tok, :], us[tok, :]
        sq = g * g
        th = jnp.tanh(g * (scale + (scale * 0.044715) * sq))
        half = 0.5 + 0.5 * th
        gelu = g * half
        slope = half + (0.5 * g) * (1.0 - th * th) * (scale + (3.0 * scale * 0.044715) * sq)
        act[tok, :] = (gelu * u).astype(bf16)
        pull[tok, :] = (u * slope).astype(bf16)
        gel[tok, :] = gelu.astype(bf16)

    act_t[...] = act[...].T


def feed_gelu(where, n1, gain, shift, gate_parts, up_parts, hidden):
    tokens, width = n1.shape
    tile = 512
    block = pl.BlockSpec((tokens, tile), lambda i: (0, i))
    count = len(gate_parts)

    def fixed(shape):
        return pl.BlockSpec(shape, lambda i: (0,) * len(shape))

    return pl.pallas_call(
        lambda *refs: gelu_kernel(count, *refs),
        grid=(hidden // tile,),
        out_shape=(
            vm((width, tokens), bf16),
            vm((tokens, hidden), bf16),
            vm((hidden, tokens), bf16),
            vm((tokens, hidden), bf16),
            vm((tokens, hidden), bf16),
        ),
        in_specs=smem_spec()
        + [fixed((tokens, width)), fixed((1, width)), fixed((1, width))]
        + any_specs(2 * count),
        out_specs=(
            fixed((width, tokens)),
            block,
            pl.BlockSpec((tile, tokens), lambda i: (i, 0)),
            block,
            block,
        ),
        scratch_shapes=[
            pltpu.VMEM((width, hidden), bf16),
            pltpu.VMEM((width, hidden), bf16),
            pltpu.VMEM((tokens, width), bf16),
            pltpu.VMEM((tokens, tile), f32),
            pltpu.VMEM((tokens, tile), f32),
            pltpu.SemaphoreType.DMA((2, count)),
        ],
        compiler_params=pltpu.CompilerParams(vmem_limit_bytes=vmem_cap),
        cost_estimate=cost(4 * tokens * width * hidden, 24e6),
        name="feed_gelu",
    )(where, n1, gain, shift, *gate_parts, *up_parts)


def row_mean(v):
    return jnp.mean(v, axis=-1, keepdims=True)


def fold(v):
    return v[:8] + v[8:]


def down_kernel(rows, span, count, outs, info, where, slots, *refs):
    parts, refs = refs[:count], refs[count:]
    act, act_t, n1, gain1, shift1, bias, gain2, shift2, cp = refs[:9]
    layer, pre2, feed, sums = refs[9:13]
    dws, refs = refs[13 : 13 + outs], refs[13 + outs :]
    wd, acc, low, dw, sems, out_sems = refs
    copies = fetch_parts(where, parts, wd, sems)
    start_all(copies)
    hidden, width = wd.shape
    wait_all(copies)
    for t in range(width // lane_block):
        c = pl.ds(t * lane_block, lane_block)
        acc[:, c] = jnp.dot(act[...], wd[:, c], preferred_element_type=f32)
    zero = jnp.zeros((8, width), f32)
    base = info[2 * rows] * span
    seg = span // segs

    def step(k, loop):
        tok = pl.ds(pl.multiple_of(k * 16, 16), 16)
        n = iota((16, width), 0) + k * 16
        r = lax.shift_right_logical(n, span.bit_length() - 1)
        n = n & (span - 1)
        pos = base + (n & (segs - 1)) * seg + lax.shift_right_logical(n, 3)
        limit = jnp.where(k * 16 >= span, info[1], info[0])
        keep = (pos < limit).astype(f32)
        v = n1[tok, :] * gain1[...] + shift1[...] + acc[tok, :] + bias[...]
        centre = v - row_mean(v)
        inv = lax.rsqrt(row_mean(centre * centre) + norm_eps)
        n2 = centre * inv
        low[tok, :] = ((n2 * gain2[...] + shift2[...]) * keep).astype(bf16)
        top = cp[tok, :].astype(f32) * keep
        e = top * gain2[...]
        grad = inv * (e - row_mean(e) - n2 * row_mean(e * n2))
        pre2[tok, :] = grad
        cut = grad.astype(bf16)
        feed[tok, :] = cut
        return (
            loop[0] + fold(cut.astype(f32)),
            loop[1] + fold(top * n2),
            loop[2] + fold(top),
        )

    totals = lax.fori_loop(0, rows * span // 16, step, (zero, zero, zero))
    for k in range(3):
        sums[pl.ds(k, 1), :] = jnp.sum(totals[k], axis=0, keepdims=True)
    o, n = iota((span, span), 0), iota((span, span), 1)
    back = (o == (n & (segs - 1)) * seg + lax.shift_right_logical(n, 3)).astype(f32).astype(bf16)
    block = 512
    for b in range(hidden // block):
        c = pl.ds(b * block, block)
        dw[c, :] = jnp.dot(act_t[c, :], feed[...], preferred_element_type=f32).astype(bf16)
    sends = send_parts(slots, dw, dws, out_sems)
    start_all(sends)
    for r in range(rows):
        layer[r] = jnp.dot(back, low[pl.ds(r * span, span), :], preferred_element_type=f32).astype(bf16)
    wait_all(sends)


def feed_down(info, where, slots, act, act_t, n1, gain1, shift1, bias, gain2, shift2, cp, parts, rows, dw_shapes):
    tokens, width = n1.shape
    span, hidden = tokens // rows, act.shape[1]
    count, outs = len(parts), len(dw_shapes)
    return pl.pallas_call(
        lambda *refs: down_kernel(rows, span, count, outs, *refs),
        out_shape=(
            vm((rows, span, width), bf16),
            vm((tokens, width)),
            vm((tokens, width), bf16),
            vm((8, width)),
        )
        + tuple(vm(s, bf16) for s in dw_shapes),
        in_specs=smem_spec() * 3 + any_specs(count) + vmem_specs(9),
        out_specs=tuple(vmem_specs(4)) + tuple(any_specs(outs)),
        scratch_shapes=[
            pltpu.VMEM((hidden, width), bf16),
            pltpu.VMEM((tokens, width), f32),
            pltpu.VMEM((tokens, width), bf16),
            pltpu.VMEM((hidden, width), bf16),
            pltpu.SemaphoreType.DMA((count,)),
            pltpu.SemaphoreType.DMA((outs * dw_shapes[0][0],)),
        ],
        compiler_params=pltpu.CompilerParams(vmem_limit_bytes=vmem_cap),
        cost_estimate=cost(4 * tokens * width * hidden, 24e6),
        name="feed_down",
    )(info, where, slots, *parts, act, act_t, n1, gain1, shift1, bias, gain2, shift2, cp)


def contract_last(a, b):
    return lax.dot_general(a, b, (((1,), (1,)), ((), ())), preferred_element_type=f32)


def inner_kernel(count, outs, where, slots, *refs):
    down, gate, up = (refs[k * count : (k + 1) * count] for k in range(3))
    refs = refs[3 * count :]
    feed, low_t, pre2, pull, gel = refs[:5]
    first = refs[5]
    dgs, dus = refs[6 : 6 + outs], refs[6 + outs : 6 + 2 * outs]
    wd, wg, wu, dg, du, sems, out_sems = refs[6 + 2 * outs :]
    i, steps = pl.program_id(0), pl.num_programs(0)
    tile = pull.shape[1]

    def weights(which):
        return [
            copy
            for k, parts, full in ((0, down, wd), (1, gate, wg), (2, up, wu))
            if k in which
            for copy in fetch_parts(where, parts, full, sems.at[k])
        ]

    @pl.when(i == 0)
    def _():
        start_all(weights((0, 1, 2)))
        first[...] = pre2[...]
        wait_all(weights((0,)))

    cols = pl.ds(pl.multiple_of(i * tile, tile), tile)
    act = contract_last(feed[...], wd[cols, :])
    g = (act * pull[...].astype(f32)).astype(bf16)
    u = (act * gel[...].astype(f32)).astype(bf16)
    dg[:, cols] = jnp.dot(low_t[...], g, preferred_element_type=f32).astype(bf16)
    du[:, cols] = jnp.dot(low_t[...], u, preferred_element_type=f32).astype(bf16)

    @pl.when(i == 0)
    def _():
        wait_all(weights((1, 2)))

    first[...] += contract_last(g, wg[:, cols]) + contract_last(u, wu[:, cols])

    @pl.when(i == steps - 1)
    def _():
        sends = send_parts(slots, dg, dgs, out_sems.at[0]) + send_parts(slots, du, dus, out_sems.at[1])
        start_all(sends)
        wait_all(sends)


def feed_inner(where, slots, down, gate, up, feed, low_t, pre2, pull, gel, dw_shapes):
    tokens, width = pre2.shape
    hidden = pull.shape[1]
    tile = 384
    count, outs = len(down), len(dw_shapes)
    block = pl.BlockSpec((tokens, tile), lambda i: (0, i))

    def fixed(shape):
        return pl.BlockSpec(shape, lambda i: (0,) * len(shape))

    return pl.pallas_call(
        lambda *refs: inner_kernel(count, outs, *refs),
        grid=(hidden // tile,),
        out_shape=(vm((tokens, width)),) + tuple(vm(s, bf16) for s in dw_shapes * 2),
        in_specs=smem_spec() * 2
        + any_specs(3 * count)
        + [fixed((tokens, width)), fixed((width, tokens)), fixed((tokens, width)), block, block],
        out_specs=(fixed((tokens, width)),) + tuple(any_specs(2 * outs)),
        scratch_shapes=[
            pltpu.VMEM((hidden, width), bf16),
            pltpu.VMEM((width, hidden), bf16),
            pltpu.VMEM((width, hidden), bf16),
            pltpu.VMEM((width, hidden), bf16),
            pltpu.VMEM((width, hidden), bf16),
            pltpu.SemaphoreType.DMA((3, count)),
            pltpu.SemaphoreType.DMA((2, outs * dw_shapes[0][0])),
        ],
        compiler_params=pltpu.CompilerParams(vmem_limit_bytes=vmem_cap),
        cost_estimate=cost(10 * tokens * width * hidden, 32e6),
        name="feed_inner",
    )(where, slots, *down, *gate, *up, feed, low_t, pre2, pull, gel)


def back_kernel(rows, span, count, outs, info, where, slots, *refs):
    parts, refs = refs[:count], refs[count:]
    first, n1, s1, gain, gated_t, q, rate = refs[:7]
    pre1, gg, ends, dev_end, sums = refs[7:12]
    dws = refs[12 : 12 + outs]
    wo, mix, dw, sems, out_sems = refs[12 + outs :]
    copies = fetch_parts(where, parts, wo, sems)
    start_all(copies)
    seg = span // segs
    width, modes = q.shape[3], rate.shape[0]
    base = info[2 * rows] * span
    zero = jnp.zeros((8, width), f32)

    def norm_step(k, loop):
        tok = pl.ds(pl.multiple_of(k * 16, 16), 16)
        top, n = first[tok, :], n1[tok, :]
        e = top * gain[...]
        grad = s1[tok, 0:1] * (e - row_mean(e) - n * row_mean(e * n))
        pre1[tok, :] = grad
        cut = grad.astype(bf16)
        mix[tok, :] = cut
        return (
            loop[0] + fold(cut.astype(f32)),
            loop[1] + fold(top * n),
            loop[2] + fold(top),
        )

    totals = lax.fori_loop(0, rows * span // 16, norm_step, (zero, zero, zero))
    for k in range(3):
        sums[pl.ds(k, 1), :] = jnp.sum(totals[k], axis=0, keepdims=True)
    dw[...] = jnp.dot(gated_t[...], mix[...], preferred_element_type=f32).astype(bf16)
    sends = send_parts(slots, dw, dws, out_sems)
    start_all(sends)
    wait_all(copies)
    for r in range(rows):
        gg[r] = contract_last(mix[pl.ds(r * span, span), :], wo[...]).reshape(seg, segs, width)
    sub = iota((segs, lane_block), 0)
    for r in range(rows):
        factor = factor_of(info, rows, r)
        for t in range(width // lane_block):
            c = pl.ds(t * lane_block, lane_block)
            fade = [jnp.exp(-rate[pl.ds(m, 1), c] * factor) for m in range(modes)]
            far = [jnp.exp(-rate[pl.ds(m, 1), c] * (factor * seg)) for m in range(modes)]

            def step(k, states):
                j = seg - 1 - k
                live = (base + sub * seg + j < info[r]).astype(f32)
                grad = gg[r, j, :, c] * live
                gg[r, j, :, c] = grad
                g = grad * q[r, j, :, c]
                return tuple(f * h + g for f, h in zip(fade, states))

            blank = jnp.zeros((segs, lane_block), f32)
            states = lax.fori_loop(0, seg, step, (blank,) * modes)
            for m in range(modes):
                ends[r, m, :, c] = states[m]
                total = jnp.zeros((1, lane_block), f32)
                for i in reversed(range(segs)):
                    total = far[m] * total + states[m][i : i + 1]
                dev_end[r, pl.ds(m, 1), c] = total
    wait_all(sends)


def mixer_back(info, where, slots, parts, first, n1, s1, gain, gated_t, q, rate, dw_shapes):
    rows, seg, _, width = q.shape
    modes = rate.shape[0]
    tokens = rows * seg * segs
    count, outs = len(parts), len(dw_shapes)
    return pl.pallas_call(
        lambda *refs: back_kernel(rows, seg * segs, count, outs, *refs),
        out_shape=(
            vm((tokens, width)),
            vm(q.shape),
            vm((rows, modes, segs, width)),
            vm((rows, modes, width)),
            vm((8, width)),
        )
        + tuple(vm(s, bf16) for s in dw_shapes),
        in_specs=smem_spec() * 3 + any_specs(count) + vmem_specs(7),
        out_specs=tuple(vmem_specs(5)) + tuple(any_specs(outs)),
        scratch_shapes=[
            pltpu.VMEM((width, width), bf16),
            pltpu.VMEM((tokens, width), bf16),
            pltpu.VMEM((width, width), bf16),
            pltpu.SemaphoreType.DMA((count,)),
            pltpu.SemaphoreType.DMA((outs * dw_shapes[0][0],)),
        ],
        compiler_params=pltpu.CompilerParams(vmem_limit_bytes=vmem_cap),
        cost_estimate=cost(4 * tokens * width * width, 12e6),
        name="mixer_back",
    )(info, where, slots, *parts, first, n1, s1, gain, gated_t, q, rate)


def source_kernel(rows, span, others, info, *refs):
    gath = refs[:others]
    (ends, carry, gg, q, long_out, keys, vals, rate, res, gm, rim, gres, grate, hist) = refs[others:]
    seg = span // segs
    width, modes = q.shape[3], rate.shape[0]
    base = info[2 * rows] * span
    sub = iota((segs, lane_block), 0)
    for t in range(width // lane_block):
        c = pl.ds(t * lane_block, lane_block)
        sum_res = [jnp.zeros((1, lane_block), f32) for _ in range(modes)]
        sum_rate = [jnp.zeros((1, lane_block), f32) for _ in range(modes)]
        for r in range(rows):
            factor = factor_of(info, rows, r)
            fade, mix, start, root, ebb = [], [], [], [], []
            for m in range(modes):
                d = rate[pl.ds(m, 1), c] * factor
                fade.append(jnp.exp(-d))
                ebb.append(jnp.exp(-2.0 * d))
                root.append(jnp.sqrt(1.0 - ebb[m]))
                mix.append(res[pl.ds(m, 1), c] * root[m])
                far = jnp.exp(-d * seg)
                cur = carry_in([g[r, pl.ds(m, 1), c] for g in gath], jnp.exp(-d * span))
                tile = jnp.zeros((segs, lane_block), f32)
                end = ends[r, m, :, c]
                for i in reversed(range(segs)):
                    tile = jnp.where(sub == i, cur, tile)
                    cur = far * cur + end[i : i + 1]
                start.append(tile)

            def ahead(j, loop):
                states, sums = loop
                live = (base + sub * seg + j < info[r]).astype(f32)
                src = keys[r, j, :, c] * vals[r, j, :, c] * live
                g = gg[r, j, :, c] * q[r, j, :, c]
                past = tuple(f * h for f, h in zip(fade, states))
                for m in range(modes):
                    hist[m, j] = past[m]
                states = tuple(p + src for p in past)
                return (states, tuple(s + g * h for s, h in zip(sums, states)))

            zero = jnp.zeros((segs, lane_block), f32)
            init = tuple(carry[r, m, :, c] for m in range(modes))
            _, with_state = lax.fori_loop(0, seg, ahead, (init, (zero,) * modes))

            def behind(k, loop):
                states, sums = loop
                j = seg - 1 - k
                live = (base + sub * seg + j < info[r]).astype(f32)
                grad = gg[r, j, :, c]
                g = grad * q[r, j, :, c]
                states = tuple(f * h + g for f, h in zip(fade, states))
                gs = mix[0] * states[0]
                for m in range(1, modes):
                    gs = gs + mix[m] * states[m]
                gs = gs * live
                for b, part in enumerate(
                    (grad * long_out[r, j, :, c], gs * vals[r, j, :, c], gs * keys[r, j, :, c])
                ):
                    gm[r, j + 2, :, pl.ds(b * width + t * lane_block, lane_block)] = part.astype(bf16).astype(f32)
                return (states, tuple(s + h * hist[m, j] for m, (s, h) in enumerate(zip(sums, states))))

            _, with_lag = lax.fori_loop(0, seg, behind, (tuple(start), (zero,) * modes))
            for m in range(modes):
                u = jnp.sum(with_state[m], axis=0, keepdims=True)
                v = jnp.sum(with_lag[m], axis=0, keepdims=True)
                sum_res[m] = sum_res[m] + root[m] * u
                sum_rate[m] = sum_rate[m] + factor * res[pl.ds(m, 1), c] * (ebb[m] / root[m] * u - root[m] * v)
        for m in range(modes):
            gres[pl.ds(m, 1), c] = sum_res[m]
            grate[pl.ds(m, 1), c] = sum_rate[m]
    for r in range(rows):
        for h, (j, i) in enumerate(((0, 0), (1, 0), (seg - 2, segs - 1), (seg - 1, segs - 1))):
            rim[pl.ds(4 * r + h, 1), :] = gm[r, j + 2, pl.ds(i, 1), :]


def mixer_source(info, gath, ends, carry, gg, q, long_out, keys, vals, rate, res):
    rows, seg, _, width = q.shape
    modes = rate.shape[0]
    return pl.pallas_call(
        lambda *refs: source_kernel(rows, seg * segs, len(gath), *refs),
        out_shape=(
            vm((rows, seg + 4, segs, 3 * width)),
            vm((4 * rows, 3 * width)),
            vm((modes, width)),
            vm((modes, width)),
        ),
        in_specs=smem_spec() + vmem_specs(9 + len(gath)),
        out_specs=tuple(vmem_specs(4)),
        scratch_shapes=[pltpu.VMEM((modes, seg, segs, lane_block), f32)],
        compiler_params=pltpu.CompilerParams(vmem_limit_bytes=vmem_cap),
        cost_estimate=cost(1e6, 16e6),
        name="mixer_source",
    )(info, *gath, ends, carry, gg, q, long_out, keys, vals, rate, res)


def taps_kernel(rows, span, seq_count, count, outs, info, where, slots, gm_in, *refs):
    parts, refs = refs[:count], refs[count:]
    halo, ext, st, ct, xpt, pre1, hidden_grad, gshort, gcond, gbias = refs[:10]
    dws, refs = refs[10 : 10 + outs], refs[10 + outs :]
    gsc, gm, gp, w, dw, low, sem, sems, out_sems = refs
    seg = span // segs
    fetch = pltpu.make_async_copy(gm_in, gm, sem)
    fetch.start()
    copies = fetch_parts(where, parts, w, sems)
    start_all(copies)
    fetch.wait()
    width = ct.shape[1]
    place = info[2 * rows]
    base = place * span
    sub = iota((segs, lane_block), 0)
    in_low = 1.0 - (place == 0).astype(f32) * (sub == 0).astype(f32)
    in_high = 1.0 - (place == seq_count - 1).astype(f32) * (sub == segs - 1).astype(f32)
    zero = jnp.zeros((segs, lane_block), f32)
    for r in range(rows):
        for t in range(3 * width // lane_block):
            fill_edges(gm, r, seg, halo, (t * lane_block, lane_block))
    for block in range(3):
        for t in range(width // lane_block):
            at = block * width + t * lane_block
            c = pl.ds(at, lane_block)
            cc = pl.ds(t * lane_block, lane_block)
            sums = tuple(zero for _ in range(4))
            csums = tuple(zero for _ in range(3))
            for r in range(rows):

                def tap3(e):
                    return (
                        st[pl.ds(0, 1), c] * ext[r, e - 1, :, c]
                        + st[pl.ds(1, 1), c] * ext[r, e, :, c]
                        + st[pl.ds(2, 1), c] * ext[r, e + 1, :, c]
                    )

                def back3(e):
                    return (
                        ct[pl.ds(0, 1), cc] * gm[r, e + 1, :, c]
                        + ct[pl.ds(1, 1), cc] * gm[r, e, :, c]
                        + ct[pl.ds(2, 1), cc] * gm[r, e - 1, :, c]
                    )

                def grad_at(e):
                    return back3(e) if block == 1 else gm[r, e, :, c]

                def step(j, loop):
                    prev, cur, kp_prev, kp_cur, sums, csums = loop
                    nxt = grad_at(j + 3)
                    if block == 1:
                        nxt = jnp.where(j == seg - 1, nxt * in_high, nxt)
                        kp_next = tap3(j + 3)
                        kp_next = jnp.where(j == seg - 1, kp_next * in_high, kp_next)
                        own = gm[r, j + 2, :, c]
                        csums = tuple(s + own * k for s, k in zip(csums, (kp_prev, kp_cur, kp_next)))
                    else:
                        kp_next = kp_cur
                    live = (base + sub * seg + j < info[r]).astype(f32)
                    full = (
                        st[pl.ds(0, 1), c] * nxt + st[pl.ds(1, 1), c] * cur + st[pl.ds(2, 1), c] * prev
                    ) * live
                    full = full.astype(bf16).astype(f32)
                    gsc[r, j] = full
                    sums = (
                        sums[0] + cur * ext[r, j + 1, :, c],
                        sums[1] + cur * ext[r, j + 2, :, c],
                        sums[2] + cur * ext[r, j + 3, :, c],
                        sums[3] + full,
                    )
                    return (cur, nxt, kp_cur, kp_next, sums, csums)

                if block == 1:
                    start = (grad_at(1) * in_low, grad_at(2), tap3(1) * in_low, tap3(2), sums, csums)
                else:
                    start = (grad_at(1), grad_at(2), zero, zero, sums, csums)
                _, _, _, _, sums, csums = lax.fori_loop(0, seg, step, start)
                gp[pl.ds(r * span, span), c] = gsc[r].reshape(span, lane_block).astype(bf16)
            for k in range(3):
                gshort[pl.ds(k, 1), c] = jnp.sum(sums[k], axis=0, keepdims=True)
            gbias[:, c] = jnp.sum(sums[3], axis=0, keepdims=True)
            if block == 1:
                for k in range(3):
                    gcond[pl.ds(k, 1), cc] = jnp.sum(csums[k], axis=0, keepdims=True)


    for t in range(3 * width // 768):
        c = pl.ds(t * 768, 768)
        dw[:, c] = jnp.dot(xpt[...], gp[:, c], preferred_element_type=f32).astype(bf16)
    sends = send_parts(slots, dw, dws, out_sems)
    start_all(sends)
    wait_all(copies)
    low[...] = (contract_last(gp[...], w[...]) + pre1[...]).astype(bf16)
    o, n = iota((span, span), 0), iota((span, span), 1)
    back = (o == (n & (segs - 1)) * seg + lax.shift_right_logical(n, 3)).astype(f32).astype(bf16)
    for r in range(rows):
        moved = jnp.dot(back, low[pl.ds(r * span, span), :], preferred_element_type=f32)
        hidden_grad[r] = moved.astype(bf16)
    wait_all(sends)


def mixer_taps(info, where, slots, gm, parts, halo, ext, st, ct, xpt, pre1, seq_count, dw_shapes):
    rows, padded, _, wide = ext.shape
    seg, width = padded - 4, wide // 3
    tokens = rows * seg * segs
    count, outs = len(parts), len(dw_shapes)
    return pl.pallas_call(
        lambda *refs: taps_kernel(rows, seg * segs, seq_count, count, outs, *refs),
        out_shape=(
            vm((rows, seg * segs, width), bf16),
            vm((3, wide)),
            vm((3, width)),
            vm((1, wide)),
        )
        + tuple(vm(s, bf16) for s in dw_shapes),
        in_specs=smem_spec() * 3 + any_specs(1 + count) + vmem_specs(6),
        out_specs=tuple(vmem_specs(4)) + tuple(any_specs(outs)),
        scratch_shapes=[
            pltpu.VMEM((rows, seg, segs, lane_block), f32),
            pltpu.VMEM(gm.shape, f32),
            pltpu.VMEM((tokens, wide), bf16),
            pltpu.VMEM((width, wide), bf16),
            pltpu.VMEM((width, wide), bf16),
            pltpu.VMEM((tokens, width), bf16),
            pltpu.SemaphoreType.DMA,
            pltpu.SemaphoreType.DMA((count,)),
            pltpu.SemaphoreType.DMA((outs * dw_shapes[0][0],)),
        ],
        compiler_params=pltpu.CompilerParams(vmem_limit_bytes=vmem_cap),
        cost_estimate=cost(4 * tokens * width * wide, 20e6),
        name="mixer_taps",
    )(info, where, slots, gm, *parts, halo, ext, st, ct, xpt, pre1)


def chip_pairs(count):
    first = [(d, d ^ (2 if d % 2 == 0 else 4)) for d in range(count)]
    second = [(d, d ^ (4 if d % 2 == 0 else 2)) for d in range(count)]
    core = [(d, d ^ 1) for d in range(count)]
    return core, first, second


def gather_shards(shard):
    core, first, second = chip_pairs(8)
    p1 = lax.ppermute(shard, "dp", first)
    p2 = lax.ppermute(shard, "dp", second)
    p3 = lax.ppermute(p1, "dp", second)
    near = [shard, p1, p2, p3]
    return near + [lax.ppermute(p, "dp", core) for p in near]


def shard_order(me):
    even = (me & 1) == 0
    f = jnp.where(even, 2, 4)
    g = jnp.where(even, 4, 2)
    near = [me, me ^ f, me ^ g, me ^ 6]
    far = [me ^ 1, me ^ 1 ^ g, me ^ 1 ^ f, me ^ 7]
    return jnp.stack(near + far).astype(jnp.int32)


def slot_order(me):
    even = (me & 1) == 0
    f = jnp.where(even, 2, 4)
    g = jnp.where(even, 4, 2)
    mine = [me, me ^ g, me ^ f, me ^ 6]
    theirs = [me ^ 1, me ^ 1 ^ f, me ^ 1 ^ g, me ^ 7]
    return jnp.stack(mine + theirs).astype(jnp.int32)


def scatter_sum(mine, theirs):
    core, first, second = chip_pairs(8)
    got = lax.ppermute(theirs, "dp", core)
    send = (mine[2:].astype(f32) + got[2:].astype(f32)).astype(bf16)
    got1 = lax.ppermute(send, "dp", first)
    keep = mine[:2].astype(f32) + got[:2].astype(f32) + got1.astype(f32)
    got2 = lax.ppermute(keep[1].astype(bf16), "dp", second)
    return (keep[0] + got2.astype(f32)).astype(bf16)


def line_sum(own):
    odd = (lax.axis_index("seq") & 1) == 1
    half = own.shape[0] // 2
    low, high = own[:half], own[half:]
    keep, send = jnp.where(odd, high, low), jnp.where(odd, low, high)
    near = [(i, i ^ 1) for i in range(4)]
    h1 = lax.ppermute(send, "seq", near)
    part = (keep.astype(f32) + h1.astype(f32)).astype(bf16)
    h2 = lax.ppermute(part, "seq", [(i, i ^ 2) for i in range(4)])
    total = (part.astype(f32) + h2.astype(f32)).astype(bf16)
    h3 = lax.ppermute(total, "seq", near)
    return jnp.concatenate([jnp.where(odd, h3, total), jnp.where(odd, total, h3)]).astype(f32)


def small_sum(flat):
    for bit in (1, 2, 4):
        flat = flat + lax.ppermute(flat, "dp", [(d, d ^ bit) for d in range(8)])
    for bit in (1, 2):
        flat = flat + lax.ppermute(flat, "seq", [(d, d ^ bit) for d in range(4)])
    return flat


def local(
    hidden_in,
    seq_len,
    bucket,
    in_weight,
    in_bias,
    short_taps,
    cond_taps,
    mode_residue,
    mode_rate,
    out_weight,
    out_bias,
    norm1_gain,
    norm1_bias,
    gate_weight,
    up_weight,
    down_weight,
    down_bias,
    norm2_gain,
    norm2_bias,
    out_cotangent,
):
    rows, span, width = hidden_in.shape
    tokens, seg = rows * span, span // segs
    dp_count, seq_count = lax.axis_size("dp"), lax.axis_size("seq")
    me, place = lax.axis_index("dp"), lax.axis_index("seq")
    info = jnp.concatenate([seq_len, bucket, place[None]]).astype(jnp.int32)
    chips = dp_count == 8
    up_line = [(i, i + 1) for i in range(seq_count - 1)]
    down_line = [(i + 1, i) for i in range(seq_count - 1)]

    def rims(low, high):
        before = lax.ppermute(high, "seq", up_line)
        after = lax.ppermute(low, "seq", down_line)
        return jnp.concatenate([before, after], axis=1).reshape(rows * 4, -1)

    def whole(shard):
        if not chips:
            return [lax.all_gather(shard, "dp", axis=0, tiled=True)]
        return gather_shards(shard)

    def dw_shapes(shard):
        depth, wide = shard.shape
        return ((4, depth, wide),) * 2 if chips else ((1, depth * dp_count, wide),)

    def line(vec):
        return vec[None]

    where = shard_order(me) if chips else jnp.zeros((1,), jnp.int32)
    slots = slot_order(me) if chips else where
    halo = rims(hidden_in[:, :2], hidden_in[:, span - 2 :])
    halo = jnp.pad(halo, ((0, 16 - rows * 4), (0, 0)))
    in_parts = whole(in_weight)
    out_parts = whole(out_weight)
    gate_parts = whole(gate_weight)
    up_parts = whole(up_weight)
    down_parts = whole(down_weight)

    xp, xpt, cp, ext, q, keys, vals, ends, dev_end = mixer_enter(
        info, where, hidden_in, out_cotangent, halo, line(in_bias), short_taps, cond_taps, mode_rate,
        in_parts, seq_count,
    )
    gath = [
        lax.ppermute(dev_end, "seq", [(i, i + k) for i in range(seq_count - k)])
        for k in range(1, seq_count)
    ]
    long_out, gated_t, carry, n1, s1 = mixer_settle(
        info, where, gath, ends, q, keys, vals, mode_rate, mode_residue, xp, line(out_bias), out_parts
    )
    low_t, act, act_t, pull, gel = feed_gelu(
        where, n1, line(norm1_gain), line(norm1_bias), gate_parts, up_parts, gate_weight.shape[1]
    )
    layer_out, pre2, feed, sums_two, *g_down = feed_down(
        info, where, slots, act, act_t, n1, line(norm1_gain), line(norm1_bias), line(down_bias),
        line(norm2_gain), line(norm2_bias), cp, down_parts, rows, dw_shapes(down_weight),
    )
    first, *g_inner = feed_inner(
        where, slots, down_parts, gate_parts, up_parts, feed, low_t, pre2, pull, gel, dw_shapes(gate_weight)
    )
    g_gate, g_up = g_inner[: len(g_inner) // 2], g_inner[len(g_inner) // 2 :]
    pre1, gg, back_ends, back_dev, sums_one, *g_out = mixer_back(
        info, where, slots, out_parts, first, n1, s1, line(norm1_gain), gated_t, q, mode_rate,
        dw_shapes(out_weight),
    )
    back_gath = [
        lax.ppermute(back_dev, "seq", [(i + k, i) for i in range(seq_count - k)])
        for k in range(1, seq_count)
    ]
    gm, rim, g_res, g_rate = mixer_source(
        info, back_gath, back_ends, carry, gg, q, long_out, keys, vals, mode_rate, mode_residue
    )
    rim = rim.astype(bf16).reshape(rows, 4, 3 * width)
    g_halo = rims(rim[:, :2], rim[:, 2:]).astype(f32)
    grad_hidden, g_short, g_cond, g_in_bias, *g_in = mixer_taps(
        info, where, slots, gm, in_parts, g_halo, ext, short_taps, cond_taps, xpt, pre1, seq_count,
        dw_shapes(in_weight),
    )

    small = (g_in_bias[0], g_short, g_cond, g_res, g_rate, sums_one[:3], sums_two[:3])
    flat = jnp.concatenate([s.reshape(-1, width) for s in small])
    if chips and seq_count == 4:
        flat = small_sum(flat)
    else:
        flat = lax.psum(flat, ("dp", "seq"))
    sums, at = [], 0
    for s in small:
        n = s.size // width
        sums.append(flat[at : at + n].reshape(s.shape))
        at += n

    def share(grad):
        if chips:
            own = scatter_sum(*grad)
        else:
            own = lax.psum_scatter(grad[0][0], "dp", scatter_dimension=0, tiled=True)
        if seq_count == 4:
            return line_sum(own)
        return lax.psum(own, "seq").astype(f32)

    share_down, share_gate, share_up, share_out, share_in = map(share, (g_down, g_gate, g_up, g_out, g_in))
    return (
        layer_out, grad_hidden, share_in, sums[0], sums[1], sums[2], sums[3], sums[4], share_out,
        sums[5][0], sums[5][1], sums[5][2], share_gate, share_up, share_down, sums[6][0], sums[6][1],
        sums[6][2],
    )


def solution(mesh):
    split, weight, full = P("dp", "seq", None), P("dp", None), P()
    in_specs = (
        split, P("dp"), P("dp"), weight, full, full, full, full, full, weight,
        full, full, full, weight, weight, weight, full, full, full, split,
    )
    out_specs = (
        split, split, weight, full, full, full, full, full, weight, full,
        full, full, weight, weight, weight, full, full, full,
    )
    return jax.shard_map(local, mesh=mesh, in_specs=in_specs, out_specs=out_specs, check_vma=False)
```

```python
import jax
import jax.numpy as jnp
from jax import lax
from jax.experimental import pallas as pl
from jax.experimental.pallas import tpu as pltpu
from jax.sharding import PartitionSpec as P

norm_eps = 1e-05
f32 = jnp.float32
bf16 = jnp.bfloat16
segs = 8
lane_block = 256
vmem_cap = 58 * 1024 * 1024


def iota(shape, dim):
    return lax.broadcasted_iota(jnp.int32, shape, dim)


def factor_of(info, rows, r):
    b = info[rows + r]
    return jnp.where(b == 0, 4.0, jnp.where(b == 1, 2.0, 1.0)).astype(f32)


def order_matrix(span):
    seg = span // segs
    o, n = iota((span, span), 0), iota((span, span), 1)
    return (n == (o & (segs - 1)) * seg + lax.shift_right_logical(o, 3)).astype(f32).astype(bf16)


def fill_edges(ext, r, seg, halo, cols):
    n = cols[1]
    c = pl.ds(cols[0], n)
    sub = iota((segs, n), 0)
    for h, (dst, src, shift, edge) in enumerate(
        ((0, seg, 1, 0), (1, seg + 1, 1, 0), (seg + 2, 2, segs - 1, segs - 1), (seg + 3, 3, segs - 1, segs - 1))
    ):
        rolled = pltpu.roll(ext[r, src, :, c], shift, 0)
        ext[r, dst, :, c] = jnp.where(sub == edge, halo[pl.ds(4 * r + h, 1), c], rolled)


def fetch_parts(where, parts, full, sems, at=0, cols=None):
    depth, wide = parts[0].shape[0], full.shape[1] if cols is None else cols.size
    copies = []
    for k, part in enumerate(parts):
        src = part if part.shape[1] == wide else part.at[:, pl.ds(at, wide)]
        dst = full.at[pl.ds(pl.multiple_of(where[k] * depth, 8), depth)]
        if cols is not None:
            dst = full.at[pl.ds(pl.multiple_of(where[k] * depth, 8), depth), cols]
        copies.append(pltpu.make_async_copy(src, dst, sems.at[k]))
    return copies


def start_all(copies):
    for copy in copies:
        copy.start()


def wait_all(copies):
    for copy in copies:
        copy.wait()


def send_parts(where, full, outs, sems, cols=None, into=None):
    per, depth = outs[0].shape[0], outs[0].shape[1]
    copies = []
    for k in range(per * len(outs)):
        rows_of = pl.ds(pl.multiple_of(where[k] * depth, 8), depth)
        src, dst = full.at[rows_of], outs[k // per].at[k % per]
        if cols is not None:
            src, dst = full.at[rows_of, cols], outs[k // per].at[k % per, :, cols]
        if into is not None:
            dst = outs[k // per].at[k % per, :, into]
        copies.append(pltpu.make_async_copy(src, dst, sems.at[k]))
    return copies


def join_rims(rows, before, after, rim):
    rim[...] = jnp.zeros_like(rim)
    low, high = before[...].astype(f32), after[...].astype(f32)
    for r in range(rows):
        for k in range(2):
            rim[pl.ds(4 * r + k, 1), :] = low[2 * r + k : 2 * r + k + 1]
            rim[pl.ds(4 * r + 2 + k, 1), :] = high[2 * r + k : 2 * r + k + 1]


def enter_kernel(rows, span, seq_count, count, info, where, x, cot, before, after, bias, st, ct, rate, *refs):
    parts, refs = refs[:count], refs[count:]
    xp, xpt, cp, ext, q, keys, vals, ends, dev_end, mask, hal, xh, w, sems = refs
    copies = fetch_parts(where, parts, w, sems)
    start_all(copies)
    width = x.shape[2]
    seg = span // segs
    place = info[2 * rows]
    base = place * span
    order = order_matrix(span)
    for r in range(rows):
        moved = jnp.dot(order, x[r], preferred_element_type=f32).astype(bf16)
        xp[pl.ds(r * span, span), :] = moved
        xpt[:, pl.ds(r * span, span)] = moved.T
        cp[pl.ds(r * span, span), :] = jnp.dot(order, cot[r], preferred_element_type=f32).astype(bf16)
        n = iota((span, 128), 0)
        pos = base + (n & (segs - 1)) * seg + lax.shift_right_logical(n, 3)
        mask[pl.ds(r * span, span), :] = (pos < info[r]).astype(f32)
    join_rims(rows, before, after, xh)
    edge_rows = xh[...].astype(bf16)
    hn = iota((16, 128), 0)
    hk = hn & 3
    hpos = base + jnp.where(hk < 2, hk - 2, span + hk - 2)
    hlim = jnp.where(lax.shift_right_logical(hn, 2) == 0, info[0], info[1])
    hmask = ((hpos >= 0) & (hpos < hlim)).astype(f32)
    wait_all(copies)

    @pl.loop(0, 3 * width // lane_block)
    def _(t):
        cols = pl.ds(pl.multiple_of(t * lane_block, lane_block), lane_block)
        part = jnp.dot(xp[...], w[:, cols], preferred_element_type=f32) + bias[:, cols]
        rim = jnp.dot(edge_rows, w[:, cols], preferred_element_type=f32) + bias[:, cols]
        for s in range(lane_block // 128):
            sub = slice(s * 128, (s + 1) * 128)
            scol = pl.ds(pl.multiple_of(t * lane_block + s * 128, 128), 128)
            low = (part[:, sub] * mask[...]).astype(bf16).astype(f32)
            for r in range(rows):
                ext[r, pl.ds(2, seg), :, scol] = low[r * span : (r + 1) * span].reshape(seg, segs, 128)
            hal[:, scol] = (rim[:, sub] * hmask).astype(bf16).astype(f32)

    sub = iota((segs, lane_block), 0)
    first = (place == 0).astype(f32)
    last = (place == seq_count - 1).astype(f32)
    in_low = 1.0 - first * (sub == 0).astype(f32)
    in_high = 1.0 - last * (sub == segs - 1).astype(f32)
    for r in range(rows):
        factor = factor_of(info, rows, r)
        for t in range(3 * width // lane_block):
            fill_edges(ext, r, seg, hal, (t * lane_block, lane_block))
        for t in range(width // lane_block):
            cq = pl.ds(t * lane_block, lane_block)
            ck = pl.ds(width + t * lane_block, lane_block)
            cv = pl.ds(2 * width + t * lane_block, lane_block)
            modes = rate.shape[0]
            fade = [jnp.exp(-rate[pl.ds(m, 1), cq] * factor) for m in range(modes)]
            far = [jnp.exp(-rate[pl.ds(m, 1), cq] * (factor * seg)) for m in range(modes)]

            def tap3(cols, e):
                return (
                    st[pl.ds(0, 1), cols] * ext[r, e - 1, :, cols]
                    + st[pl.ds(1, 1), cols] * ext[r, e, :, cols]
                    + st[pl.ds(2, 1), cols] * ext[r, e + 1, :, cols]
                )

            def step(j, carry):
                kp_prev, kp_cur, states = carry
                kp_next = tap3(ck, j + 3)
                kp_next = jnp.where(j == seg - 1, kp_next * in_high, kp_next)
                key = (
                    ct[pl.ds(0, 1), cq] * kp_prev
                    + ct[pl.ds(1, 1), cq] * kp_cur
                    + ct[pl.ds(2, 1), cq] * kp_next
                )
                val = tap3(cv, j + 2)
                q[r, j, :, cq] = tap3(cq, j + 2)
                keys[r, j, :, cq] = key
                vals[r, j, :, cq] = val
                live = (base + sub * seg + j < info[r]).astype(f32)
                src = key * val * live
                return (kp_cur, kp_next, tuple(f * h + src for f, h in zip(fade, states)))

            zero = jnp.zeros((segs, lane_block), f32)
            start = (tap3(ck, 1) * in_low, tap3(ck, 2), (zero,) * modes)
            _, _, states = lax.fori_loop(0, seg, step, start, unroll=4)
            for m in range(modes):
                ends[r, m, :, cq] = states[m]
                total = jnp.zeros((1, lane_block), f32)
                for i in range(segs):
                    total = far[m] * total + states[m][i : i + 1]
                dev_end[r, pl.ds(m, 1), cq] = total


def vm(shape, dtype=f32):
    return jax.ShapeDtypeStruct(shape, dtype)


def vmem_specs(n):
    return [pl.BlockSpec(memory_space=pltpu.VMEM)] * n


def smem_spec():
    return [pl.BlockSpec(memory_space=pltpu.SMEM)]


def spent(us):
    return pl.CostEstimate(flops=int(us * 1.1e9), bytes_accessed=1_000_000, transcendentals=0)


def any_specs(n):
    return [pl.BlockSpec(memory_space=pl.ANY)] * n


def hbm_specs(n):
    return [pl.BlockSpec(memory_space=pltpu.HBM)] * n


def mixer_enter(info, where, hidden, cot, before, after, bias, st, ct, rate, parts, seq_count):
    rows, span, width = hidden.shape
    seg, modes, tokens = span // segs, rate.shape[0], rows * span
    body = (rows, seg, segs, width)
    return pl.pallas_call(
        lambda *refs: enter_kernel(rows, span, seq_count, len(parts), *refs),
        out_shape=(
            vm((tokens, width), bf16),
            vm((width, tokens), bf16),
            vm((tokens, width), bf16),
            vm((rows, seg + 4, segs, 3 * width)),
            vm(body),
            vm(body),
            vm(body),
            vm((rows, modes, segs, width)),
            vm((rows, modes, width)),
        ),
        in_specs=smem_spec() * 2 + vmem_specs(8) + hbm_specs(len(parts)),
        out_specs=tuple(vmem_specs(9)),
        scratch_shapes=[
            pltpu.VMEM((tokens, 128), f32),
            pltpu.VMEM((16, 3 * width), f32),
            pltpu.VMEM((16, width), f32),
            pltpu.VMEM((width, 3 * width), bf16),
            pltpu.SemaphoreType.DMA((len(parts),)),
        ],
        compiler_params=pltpu.CompilerParams(vmem_limit_bytes=vmem_cap),
        cost_estimate=spent(1),
        name="mixer_enter",
    )(info, where, hidden, cot, before, after, bias, st, ct, rate, *parts)


def carry_in(parts, fade_span):
    total = parts[0]
    scale = fade_span
    for p in parts[1:]:
        total = total + scale * p
        scale = scale * fade_span
    return total


def settle_kernel(rows, span, others, count, info, where, *refs):
    gath, refs = refs[:others], refs[others:]
    parts, refs = refs[:count], refs[count:]
    ends, q, keys, vals, rate, res, xp, ob, gain, shift, long_out, gated_t, carry_out, n1, s1, low, low_t, gsc, wo, sems = refs
    copies = fetch_parts(where, parts, wo, sems, parts[0].shape[1] - wo.shape[1])
    start_all(copies)
    seg = span // segs
    width = q.shape[3]
    modes = rate.shape[0]
    base = info[2 * rows] * span
    sub = iota((segs, lane_block), 0)
    for r in range(rows):
        factor = factor_of(info, rows, r)
        for t in range(width // lane_block):
            c = pl.ds(t * lane_block, lane_block)
            fade, mix, start = [], [], []
            for m in range(modes):
                d = rate[pl.ds(m, 1), c] * factor
                fade.append(jnp.exp(-d))
                mix.append(res[pl.ds(m, 1), c] * jnp.sqrt(1.0 - jnp.exp(-2.0 * d)))
                far = jnp.exp(-d * seg)
                cur = carry_in([g[r, pl.ds(m, 1), c] for g in gath], jnp.exp(-d * span))
                tile = jnp.zeros((segs, lane_block), f32)
                end = ends[r, m, :, c]
                for i in range(segs):
                    tile = jnp.where(sub == i, cur, tile)
                    cur = far * cur + end[i : i + 1]
                carry_out[r, m, :, c] = tile
                start.append(tile)

            def step(j, states):
                live = (base + sub * seg + j < info[r]).astype(f32)
                src = keys[r, j, :, c] * vals[r, j, :, c] * live
                states = tuple(f * h + src for f, h in zip(fade, states))
                out = mix[0] * states[0]
                for m in range(1, modes):
                    out = out + mix[m] * states[m]
                long_out[r, j, :, c] = out
                gsc[r, j, :, c] = q[r, j, :, c] * out * live
                return states

            lax.fori_loop(0, seg, step, tuple(start), unroll=4)
    wait_all(copies)
    for r in range(rows):
        tok = pl.ds(r * span, span)
        cut = gsc[r].reshape(span, width).astype(bf16)
        gated_t[:, tok] = cut.T
        n1[tok, :] = xp[tok, :].astype(f32) + jnp.dot(cut, wo[...], preferred_element_type=f32) + ob[...]

    @pl.loop(0, rows * span // 16, unroll=4)
    def _(k):
        tok = pl.ds(pl.multiple_of(k * 16, 16), 16)
        v = n1[tok, :]
        centre = v - jnp.mean(v, axis=-1, keepdims=True)
        inv = lax.rsqrt(jnp.mean(centre * centre, axis=-1, keepdims=True) + norm_eps)
        n = centre * inv
        n1[tok, :] = n
        s1[tok, :] = jnp.broadcast_to(inv, (16, 128))
        low[tok, :] = (n * gain[...] + shift[...]).astype(bf16)

    low_t[...] = low[...].T


def mixer_settle(info, where, gath, ends, q, keys, vals, rate, res, xp, ob, gain, shift, parts):
    rows, seg, _, width = q.shape
    span = seg * segs
    tokens, modes = rows * span, rate.shape[0]
    return pl.pallas_call(
        lambda *refs: settle_kernel(rows, span, len(gath), len(parts), *refs),
        out_shape=(
            vm(q.shape),
            vm((width, tokens), bf16),
            vm(ends.shape),
            vm((tokens, width)),
            vm((tokens, 128)),
            vm((tokens, width), bf16),
            vm((width, tokens), bf16),
        ),
        in_specs=smem_spec() * 2 + vmem_specs(len(gath)) + hbm_specs(len(parts)) + vmem_specs(10),
        out_specs=tuple(vmem_specs(7)),
        scratch_shapes=[
            pltpu.VMEM(q.shape, f32),
            pltpu.VMEM((width, width), bf16),
            pltpu.SemaphoreType.DMA((len(parts),)),
        ],
        compiler_params=pltpu.CompilerParams(vmem_limit_bytes=vmem_cap),
        cost_estimate=spent(1),
        name="mixer_settle",
    )(info, where, *gath, *parts, ends, q, keys, vals, rate, res, xp, ob, gain, shift)


def row_mean(v):
    return jnp.mean(v, axis=-1, keepdims=True)


def fold(v):
    return v[:8] + v[8:]


def contract_last(a, b):
    return lax.dot_general(a, b, (((1,), (1,)), ((), ())), preferred_element_type=f32)


hidden_tile = 512


def core_kernel(rows, span, count, outs, info, where, slots, *refs):
    w_parts, d_parts, o_parts, refs = refs[:count], refs[count : 2 * count], refs[2 * count : 3 * count], refs[3 * count :]
    low_h, low_th, gated_th, n1_h, s1_h, cp_h, q_h, gain1, shift1, bias, gain2, shift2, rate, layer = refs[:14]
    refs = refs[14:]
    down_out, first_out, second_out, refs = refs[:outs], refs[outs : 2 * outs], refs[2 * outs : 3 * outs], refs[3 * outs :]
    pre1_h, gg_h, ends, dev_end, sums_two, sums_one, w, wd, wo, act, pull, gel, low, low_t, gated_t = refs[:15]
    n1, s1, cp, q, acc, first, feed, out_low, mix, gs, us, dd, dwg, dwu, dwo = refs[15:30]
    in_sems, w_sems, d_sems, o_sems, dd_sems, dw_sems, end_sems = refs[30:]
    hidden, width = wd.shape
    tile, seg, modes = hidden_tile, span // segs, rate.shape[0]
    tiles, tokens = hidden // tile, rows * span
    base = info[2 * rows] * span

    def bring(k, src, dst):
        return pltpu.make_async_copy(src, dst, in_sems.at[k])

    w_in = [
        [
            copy
            for k, at in enumerate((t * tile, hidden + t * tile))
            for copy in fetch_parts(where, w_parts, w, w_sems.at[k, t], at, pl.ds(at, tile))
        ]
        for t in range(tiles)
    ]
    d_in = fetch_parts(where, d_parts, wd, d_sems)
    o_in = fetch_parts(where, o_parts, wo, o_sems, o_parts[0].shape[1] - width)
    low_in = bring(0, low_h, low)
    norm_in = [bring(1, n1_h, n1), bring(2, cp_h, cp)]
    late_in = [bring(3, low_th, low_t), bring(4, s1_h, s1), bring(5, q_h, q), bring(6, gated_th, gated_t)]
    start_all([low_in] + w_in[0] + w_in[1])
    low_in.wait()
    scale = 0.7978845608028654
    for t in range(tiles):
        if t + 2 < tiles:
            start_all(w_in[t + 2])
        if t == 1:
            start_all(d_in)
        if t == 3:
            start_all(norm_in)
        wait_all(w_in[t])
        cols, up_cols = pl.ds(t * tile, tile), pl.ds(hidden + t * tile, tile)
        gs[...] = jnp.dot(low[...], w[:, cols], preferred_element_type=f32)
        us[...] = jnp.dot(low[...], w[:, up_cols], preferred_element_type=f32)

        @pl.loop(0, tokens // 16, unroll=2)
        def _(k):
            tok = pl.ds(pl.multiple_of(k * 16, 16), 16)
            g, u = gs[tok, :], us[tok, :]
            sq = g * g
            th = jnp.tanh(g * (scale + (scale * 0.044715) * sq))
            side = 0.5 + 0.5 * th
            gelu = g * side
            slope = side + (0.5 * g) * (1.0 - th * th) * (scale + (3.0 * scale * 0.044715) * sq)
            act[tok, cols] = (gelu * u).astype(bf16)
            pull[tok, cols] = (u * slope).astype(bf16)
            gel[tok, cols] = gelu.astype(bf16)

    wait_all(d_in)
    for t in range(width // lane_block):
        c = pl.ds(t * lane_block, lane_block)
        acc[:, c] = jnp.dot(act[...], wd[:, c], preferred_element_type=f32)
    zero = jnp.zeros((8, width), f32)
    wait_all(norm_in)
    start_all(late_in + o_in)

    def outer_norm(k, loop):
        tok = pl.ds(pl.multiple_of(k * 16, 16), 16)
        n = iota((16, width), 0) + k * 16
        n = n & (span - 1)
        pos = base + (n & (segs - 1)) * seg + lax.shift_right_logical(n, 3)
        limit = jnp.where(k * 16 >= span, info[1], info[0])
        keep = (pos < limit).astype(f32)
        v = n1[tok, :] * gain1[...] + shift1[...] + acc[tok, :] + bias[...]
        centre = v - row_mean(v)
        inv = lax.rsqrt(row_mean(centre * centre) + norm_eps)
        n2 = centre * inv
        out_low[tok, :] = ((n2 * gain2[...] + shift2[...]) * keep).astype(bf16)
        top = cp[tok, :].astype(f32) * keep
        e = top * gain2[...]
        grad = inv * (e - row_mean(e) - n2 * row_mean(e * n2))
        first[tok, :] = grad
        cut = grad.astype(bf16)
        feed[tok, :] = cut
        return (
            loop[0] + fold(cut.astype(f32)),
            loop[1] + fold(top * n2),
            loop[2] + fold(top),
        )

    totals = lax.fori_loop(0, tokens // 16, outer_norm, (zero, zero, zero), unroll=4)
    for k in range(3):
        sums_two[pl.ds(k, 1), :] = jnp.sum(totals[k], axis=0, keepdims=True)

    blocks = 8
    span_d = hidden // blocks
    d_sends = []
    for k in range(blocks):
        if k >= 2:
            d_sends[k - 2].wait()
        which = k if outs == 1 else slots[k]
        c = pl.ds(pl.multiple_of(which * span_d, 128), span_d)
        dd[k % 2] = jnp.dot(act[:, c].T, feed[...], preferred_element_type=f32).astype(bf16)
        per = down_out[0].shape[0]
        dst = down_out[0].at[0, pl.ds(k * span_d, span_d)] if outs == 1 else down_out[k // per].at[k % per]
        d_sends.append(pltpu.make_async_copy(dd.at[k % 2], dst, dd_sems.at[k]))
        d_sends[k].start()
    o, n = iota((span, span), 0), iota((span, span), 1)
    back = (o == (n & (segs - 1)) * seg + lax.shift_right_logical(n, 3)).astype(f32).astype(bf16)
    for r in range(rows):
        layer[r] = jnp.dot(back, out_low[pl.ds(r * span, span), :], preferred_element_type=f32).astype(bf16)
    wait_all(late_in)
    sends = []
    half_tiles = tiles // 2
    for t in range(tiles):
        cols, up_cols = pl.ds(t * tile, tile), pl.ds(hidden + t * tile, tile)
        grad = contract_last(feed[...], wd[cols, :])
        g = (grad * pull[:, cols].astype(f32)).astype(bf16)
        u = (grad * gel[:, cols].astype(f32)).astype(bf16)
        if t >= 2:
            wait_all(sends[t - 2])
        dwg[t % 2] = jnp.dot(low_t[...], g, preferred_element_type=f32).astype(bf16)
        dwu[t % 2] = jnp.dot(low_t[...], u, preferred_element_type=f32).astype(bf16)
        into, at, own = (first_out, 0, t) if t < half_tiles else (second_out, width, t - half_tiles)
        g_at, u_at = at + own * tile, at + (half_tiles + own) * tile
        sends.append(
            send_parts(slots, dwg.at[t % 2], into, dw_sems.at[0, t], None, pl.ds(g_at, tile))
            + send_parts(slots, dwu.at[t % 2], into, dw_sems.at[1, t], None, pl.ds(u_at, tile))
        )
        start_all(sends[t])
        first[...] += contract_last(g, w[:, cols]) + contract_last(u, w[:, up_cols])

    def put(k, src, dst):
        return pltpu.make_async_copy(src, dst, end_sems.at[k])

    def inner_norm(k, loop):
        tok = pl.ds(pl.multiple_of(k * 16, 16), 16)
        top, n = first[tok, :], n1[tok, :]
        e = top * gain1[...]
        grad = s1[tok, 0:1] * (e - row_mean(e) - n * row_mean(e * n))
        acc[tok, :] = grad
        cut = grad.astype(bf16)
        mix[tok, :] = cut
        return (
            loop[0] + fold(cut.astype(f32)),
            loop[1] + fold(top * n),
            loop[2] + fold(top),
        )

    totals = lax.fori_loop(0, tokens // 16, inner_norm, (zero, zero, zero), unroll=4)
    finals = [put(0, acc, pre1_h)]
    finals[0].start()
    for k in range(3):
        sums_one[pl.ds(k, 1), :] = jnp.sum(totals[k], axis=0, keepdims=True)
    dwo[...] = jnp.dot(gated_t[...], mix[...], preferred_element_type=f32).astype(bf16)
    o_sends = send_parts(slots, dwo, second_out, dw_sems.at[2, 0], None, pl.ds(0, width))
    start_all(o_sends)
    wait_all(o_in)
    for t in range(width // lane_block):
        c = pl.ds(t * lane_block, lane_block)
        first[:, c] = contract_last(mix[...], wo[c, :])
    sub = iota((segs, lane_block), 0)
    for r in range(rows):
        factor = factor_of(info, rows, r)
        for t in range(width // lane_block):
            c = pl.ds(t * lane_block, lane_block)
            fade = [jnp.exp(-rate[pl.ds(m, 1), c] * factor) for m in range(modes)]
            far = [jnp.exp(-rate[pl.ds(m, 1), c] * (factor * seg)) for m in range(modes)]

            def step(k, states):
                j = seg - 1 - k
                live = (base + sub * seg + j < info[r]).astype(f32)
                tok = pl.ds(pl.multiple_of(r * span + j * segs, segs), segs)
                grad = first[tok, c] * live
                first[tok, c] = grad
                g = grad * q[r, j, :, c]
                return tuple(f * h + g for f, h in zip(fade, states))

            blank = jnp.zeros((segs, lane_block), f32)
            states = lax.fori_loop(0, seg, step, (blank,) * modes, unroll=4)
            for m in range(modes):
                ends[r, m, :, c] = states[m]
                total = jnp.zeros((1, lane_block), f32)
                for i in reversed(range(segs)):
                    total = far[m] * total + states[m][i : i + 1]
                dev_end[r, pl.ds(m, 1), c] = total
    finals.append(put(1, first, gg_h))
    finals[1].start()
    for copies in [d_sends[-2:]] + sends[-2:] + [o_sends, finals]:
        wait_all(copies)


def feed_core(
    info, where, slots, w_parts, d_parts, o_parts, low, low_t, gated_t, n1, s1, cp, q, gain1, shift1, bias,
    gain2, shift2, rate, down_shapes, first_shapes, second_shapes,
):
    tokens, width = n1.shape
    rows, seg = q.shape[:2]
    modes, count, outs = rate.shape[0], len(w_parts), len(first_shapes)
    hidden, tile, pieces = w_parts[0].shape[1] // 2, hidden_tile, first_shapes[0][0] * outs
    shapes = tuple(down_shapes) + tuple(first_shapes) + tuple(second_shapes)
    return pl.pallas_call(
        lambda *refs: core_kernel(rows, seg * segs, count, outs, *refs),
        out_shape=(vm((rows, seg * segs, width), bf16),)
        + tuple(vm(s, bf16) for s in shapes)
        + (
            vm((tokens, width)),
            vm((tokens, width)),
            vm((rows, modes, segs, width)),
            vm((rows, modes, width)),
            vm((8, width)),
            vm((8, width)),
        ),
        in_specs=smem_spec() * 3 + hbm_specs(3 * count + 7) + vmem_specs(6),
        out_specs=tuple(vmem_specs(1) + hbm_specs(3 * outs + 2) + vmem_specs(4)),
        scratch_shapes=[
            pltpu.VMEM((width, 2 * hidden), bf16),
            pltpu.VMEM((hidden, width), bf16),
            pltpu.VMEM((width, width), bf16),
            pltpu.VMEM((tokens, hidden), bf16),
            pltpu.VMEM((tokens, hidden), bf16),
            pltpu.VMEM((tokens, hidden), bf16),
            pltpu.VMEM((tokens, width), bf16),
            pltpu.VMEM((width, tokens), bf16),
            pltpu.VMEM((width, tokens), bf16),
            pltpu.VMEM((tokens, width), f32),
            pltpu.VMEM((tokens, 128), f32),
            pltpu.VMEM((tokens, width), bf16),
            pltpu.VMEM(q.shape, f32),
            pltpu.VMEM((tokens, width), f32),
            pltpu.VMEM((tokens, width), f32),
            pltpu.VMEM((tokens, width), bf16),
            pltpu.VMEM((tokens, width), bf16),
            pltpu.VMEM((tokens, width), bf16),
            pltpu.VMEM((tokens, tile), f32),
            pltpu.VMEM((tokens, tile), f32),
            pltpu.VMEM((2, hidden // 8, width), bf16),
            pltpu.VMEM((2, width, tile), bf16),
            pltpu.VMEM((2, width, tile), bf16),
            pltpu.VMEM((width, width), bf16),
            pltpu.SemaphoreType.DMA((7,)),
            pltpu.SemaphoreType.DMA((2, hidden // tile, count)),
            pltpu.SemaphoreType.DMA((count,)),
            pltpu.SemaphoreType.DMA((count,)),
            pltpu.SemaphoreType.DMA((8,)),
            pltpu.SemaphoreType.DMA((3, hidden // tile, pieces)),
            pltpu.SemaphoreType.DMA((2,)),
        ],
        compiler_params=pltpu.CompilerParams(vmem_limit_bytes=vmem_cap),
        cost_estimate=spent(1),
        name="feed_core",
    )(
        info, where, slots, *w_parts, *d_parts, *o_parts, low, low_t, gated_t, n1, s1, cp, q, gain1, shift1,
        bias, gain2, shift2, rate,
    )


def split_rims(rows, seg, at, rim, low, high):
    for r in range(rows):
        for k in range(2):
            rim[pl.ds(2 * r + k, 1), :] = at(r, k, pl.ds(0, 1))
            rim[pl.ds(2 * (rows + r) + k, 1), :] = at(r, seg - 2 + k, pl.ds(segs - 1, 1))
    low[...] = rim[: 2 * rows].astype(bf16)
    high[...] = rim[2 * rows : 4 * rows].astype(bf16)


def source_kernel(rows, span, others, info, *refs):
    gath = refs[:others]
    ends, carry, rate, res, refs = *refs[others : others + 4], refs[others + 4 :]
    streams, refs = refs[:5], refs[5:]
    gm_h, rim_low, rim_high, gres, grate, gg, q, long_out, keys, vals, gm, hist, rim, in_sems, out_sems = refs
    seg = span // segs
    width, modes = q.shape[3], rate.shape[0]
    blocks = width // lane_block
    ins = [
        [
            pltpu.make_async_copy(
                src.at[:, :, :, pl.ds(t * lane_block, lane_block)],
                dst.at[:, :, :, pl.ds(t * lane_block, lane_block)],
                in_sems.at[t, k],
            )
            for k, (src, dst) in enumerate(zip(streams, (gg, q, long_out, keys, vals)))
        ]
        for t in range(blocks)
    ]
    sends = [
        [
            pltpu.make_async_copy(
                gm.at[:, :, :, pl.ds(b * width + t * lane_block, lane_block)],
                gm_h.at[:, pl.ds(2, seg), :, pl.ds(b * width + t * lane_block, lane_block)],
                out_sems.at[t, b],
            )
            for b in range(3)
        ]
        for t in range(blocks)
    ]
    for t in range(blocks):
        start_all(ins[t])
    base = info[2 * rows] * span
    sub = iota((segs, lane_block), 0)
    for t in range(blocks):
        wait_all(ins[t])
        c = pl.ds(t * lane_block, lane_block)
        sum_res = [jnp.zeros((1, lane_block), f32) for _ in range(modes)]
        sum_rate = [jnp.zeros((1, lane_block), f32) for _ in range(modes)]
        for r in range(rows):
            factor = factor_of(info, rows, r)
            fade, mix, start, root, ebb = [], [], [], [], []
            for m in range(modes):
                d = rate[pl.ds(m, 1), c] * factor
                fade.append(jnp.exp(-d))
                ebb.append(jnp.exp(-2.0 * d))
                root.append(jnp.sqrt(1.0 - ebb[m]))
                mix.append(res[pl.ds(m, 1), c] * root[m])
                far = jnp.exp(-d * seg)
                cur = carry_in([g[r, pl.ds(m, 1), c] for g in gath], jnp.exp(-d * span))
                tile = jnp.zeros((segs, lane_block), f32)
                end = ends[r, m, :, c]
                for i in reversed(range(segs)):
                    tile = jnp.where(sub == i, cur, tile)
                    cur = far * cur + end[i : i + 1]
                start.append(tile)

            def ahead(j, loop):
                states, sums = loop
                live = (base + sub * seg + j < info[r]).astype(f32)
                src = keys[r, j, :, c] * vals[r, j, :, c] * live
                g = gg[r, j, :, c] * q[r, j, :, c]
                past = tuple(f * h for f, h in zip(fade, states))
                for m in range(modes):
                    hist[m, j] = past[m]
                states = tuple(p + src for p in past)
                return (states, tuple(s + g * h for s, h in zip(sums, states)))

            zero = jnp.zeros((segs, lane_block), f32)
            init = tuple(carry[r, m, :, c] for m in range(modes))
            _, with_state = lax.fori_loop(0, seg, ahead, (init, (zero,) * modes), unroll=4)

            def behind(k, loop):
                states, sums = loop
                j = seg - 1 - k
                live = (base + sub * seg + j < info[r]).astype(f32)
                grad = gg[r, j, :, c]
                g = grad * q[r, j, :, c]
                states = tuple(f * h + g for f, h in zip(fade, states))
                gs = mix[0] * states[0]
                for m in range(1, modes):
                    gs = gs + mix[m] * states[m]
                gs = gs * live
                for b, part in enumerate(
                    (grad * long_out[r, j, :, c], gs * vals[r, j, :, c], gs * keys[r, j, :, c])
                ):
                    gm[r, j, :, pl.ds(b * width + t * lane_block, lane_block)] = part.astype(bf16).astype(f32)
                return (states, tuple(s + h * hist[m, j] for m, (s, h) in enumerate(zip(sums, states))))

            _, with_lag = lax.fori_loop(0, seg, behind, (tuple(start), (zero,) * modes), unroll=4)
            for m in range(modes):
                u = jnp.sum(with_state[m], axis=0, keepdims=True)
                v = jnp.sum(with_lag[m], axis=0, keepdims=True)
                sum_res[m] = sum_res[m] + root[m] * u
                sum_rate[m] = sum_rate[m] + factor * res[pl.ds(m, 1), c] * (ebb[m] / root[m] * u - root[m] * v)
        for m in range(modes):
            gres[pl.ds(m, 1), c] = sum_res[m]
            grate[pl.ds(m, 1), c] = sum_rate[m]
        start_all(sends[t])
    split_rims(rows, seg, lambda r, j, i: gm[r, j, i, :], rim, rim_low, rim_high)
    for t in range(blocks):
        wait_all(sends[t])


def mixer_source(info, gath, ends, carry, gg, q, long_out, keys, vals, rate, res):
    rows, seg, _, width = q.shape
    modes = rate.shape[0]
    return pl.pallas_call(
        lambda *refs: source_kernel(rows, seg * segs, len(gath), *refs),
        out_shape=(
            vm((rows, seg + 4, segs, 3 * width)),
            vm((2 * rows, 3 * width), bf16),
            vm((2 * rows, 3 * width), bf16),
            vm((modes, width)),
            vm((modes, width)),
        ),
        in_specs=smem_spec() + vmem_specs(4 + len(gath)) + hbm_specs(5),
        out_specs=tuple(hbm_specs(1) + vmem_specs(4)),
        scratch_shapes=[pltpu.VMEM(q.shape, f32)] * 5
        + [
            pltpu.VMEM((rows, seg, segs, 3 * width), f32),
            pltpu.VMEM((modes, seg, segs, lane_block), f32),
            pltpu.VMEM((4 * rows, 3 * width), f32),
            pltpu.SemaphoreType.DMA((width // lane_block, 5)),
            pltpu.SemaphoreType.DMA((width // lane_block, 3)),
        ],
        compiler_params=pltpu.CompilerParams(vmem_limit_bytes=vmem_cap),
        cost_estimate=spent(1),
        name="mixer_source",
    )(info, *gath, ends, carry, rate, res, gg, q, long_out, keys, vals)


def taps_blocks(rows, span, seq_count, info, gm, halo, ext, st, ct, gp, put, gsc, ready, done):
    seg = span // segs
    width = ct.shape[1]
    place = info[2 * rows]
    base = place * span
    sub = iota((segs, lane_block), 0)
    in_low = 1.0 - (place == 0).astype(f32) * (sub == 0).astype(f32)
    in_high = 1.0 - (place == seq_count - 1).astype(f32) * (sub == segs - 1).astype(f32)
    zero = jnp.zeros((segs, lane_block), f32)
    for block in range(3):
        for t in range(width // lane_block):
            ready(block * (width // lane_block) + t)
            for r in range(rows):
                fill_edges(gm, r, seg, halo, (block * width + t * lane_block, lane_block))
            c = pl.ds(block * width + t * lane_block, lane_block)
            lanes = pl.ds(t * lane_block, lane_block)
            sums = tuple(zero for _ in range(4))
            csums = tuple(zero for _ in range(3))
            for r in range(rows):

                def tap3(e):
                    return (
                        st[pl.ds(0, 1), c] * ext[r, e - 1, :, c]
                        + st[pl.ds(1, 1), c] * ext[r, e, :, c]
                        + st[pl.ds(2, 1), c] * ext[r, e + 1, :, c]
                    )

                def grad_at(e):
                    if block != 1:
                        return gm[r, e, :, c]
                    return (
                        ct[pl.ds(0, 1), lanes] * gm[r, e + 1, :, c]
                        + ct[pl.ds(1, 1), lanes] * gm[r, e, :, c]
                        + ct[pl.ds(2, 1), lanes] * gm[r, e - 1, :, c]
                    )

                def step(j, loop):
                    prev, cur, kp_prev, kp_cur, sums, csums = loop
                    nxt = grad_at(j + 3)
                    if block == 1:
                        nxt = jnp.where(j == seg - 1, nxt * in_high, nxt)
                        kp_next = tap3(j + 3)
                        kp_next = jnp.where(j == seg - 1, kp_next * in_high, kp_next)
                        own = gm[r, j + 2, :, c]
                        csums = tuple(s + own * k for s, k in zip(csums, (kp_prev, kp_cur, kp_next)))
                    else:
                        kp_next = kp_cur
                    live = (base + sub * seg + j < info[r]).astype(f32)
                    full = (
                        st[pl.ds(0, 1), c] * nxt + st[pl.ds(1, 1), c] * cur + st[pl.ds(2, 1), c] * prev
                    ) * live
                    full = full.astype(bf16).astype(f32)
                    gsc[r, j] = full
                    sums = (
                        sums[0] + cur * ext[r, j + 1, :, c],
                        sums[1] + cur * ext[r, j + 2, :, c],
                        sums[2] + cur * ext[r, j + 3, :, c],
                        sums[3] + full,
                    )
                    return (cur, nxt, kp_cur, kp_next, sums, csums)

                if block == 1:
                    start = (grad_at(1) * in_low, grad_at(2), tap3(1) * in_low, tap3(2), sums, csums)
                else:
                    start = (grad_at(1), grad_at(2), zero, zero, sums, csums)
                _, _, _, _, sums, csums = lax.fori_loop(0, seg, step, start, unroll=4)
                gp[pl.ds(r * span, span), c] = gsc[r].reshape(span, lane_block).astype(bf16)
            for k in range(3):
                put("short", k, block, lanes, jnp.sum(sums[k], axis=0, keepdims=True))
            put("bias", 0, block, lanes, jnp.sum(sums[3], axis=0, keepdims=True))
            if block == 1:
                for k in range(3):
                    put("cond", k, block, lanes, jnp.sum(csums[k], axis=0, keepdims=True))
        done(block)


row_bias, row_short, row_cond, row_res, row_rate, row_one, row_two, small_rows = 0, 3, 12, 15, 19, 23, 26, 32


def small_put(small):
    def put(kind, k, block, lanes, value):
        row = {"bias": row_bias + block, "short": row_short + 3 * k + block, "cond": row_cond + k}[kind]
        small[pl.ds(row, 1), lanes] = value

    return put


def taps_kernel(rows, span, seq_count, count, outs, info, where, slots, *refs):
    parts, refs = refs[:count], refs[count:]
    gm_h, ext_h, xpt_h, pre1_h, before, after, st, ct, gres, grate, sums_one, sums_two = refs[:12]
    hidden_grad, small = refs[12:14]
    dws, refs = refs[14 : 14 + outs], refs[14 + outs :]
    gsc, gm, ext, xpt, pre1, gp, halo, w, dw, low, stream_sems, in_sems, sems, out_sems = refs
    width = ct.shape[1]
    groups = 3 * width // lane_block
    streams = [
        [
            pltpu.make_async_copy(
                src.at[:, :, :, pl.ds(n * lane_block, lane_block)],
                dst.at[:, :, :, pl.ds(n * lane_block, lane_block)],
                stream_sems.at[k, n],
            )
            for k, (src, dst) in enumerate(((gm_h, gm), (ext_h, ext)))
        ]
        for n in range(groups)
    ]
    late = [pltpu.make_async_copy(xpt_h, xpt, in_sems.at[0]), pltpu.make_async_copy(pre1_h, pre1, in_sems.at[1])]
    copies = fetch_parts(where, parts, w, sems)
    for n in range(groups):
        start_all(streams[n])
        if n == 2:
            late[0].start()
    start_all(copies + late[1:])
    small[...] = jnp.zeros_like(small)
    modes = gres.shape[0]
    small[pl.ds(row_res, modes), :] = gres[...]
    small[pl.ds(row_rate, modes), :] = grate[...]
    small[pl.ds(row_one, 3), :] = sums_one[pl.ds(0, 3), :]
    small[pl.ds(row_two, 3), :] = sums_two[pl.ds(0, 3), :]
    join_rims(rows, before, after, halo)
    sends = []

    def done(block):
        c = pl.ds(block * width, width)
        if block == 0:
            late[0].wait()
        dw[:, c] = jnp.dot(xpt[...], gp[:, c], preferred_element_type=f32).astype(bf16)
        sends.extend(send_parts(slots, dw, dws, out_sems.at[block], c))
        start_all(sends[-outs * dws[0].shape[0] :])

    taps_blocks(
        rows, span, seq_count, info, gm, halo, ext, st, ct, gp, small_put(small), gsc,
        lambda n: wait_all(streams[n]), done,
    )
    wait_all(copies + late[1:])
    low[...] = (contract_last(gp[...], w[...]) + pre1[...]).astype(bf16)
    o, n = iota((span, span), 0), iota((span, span), 1)
    seg = span // segs
    back = (o == (n & (segs - 1)) * seg + lax.shift_right_logical(n, 3)).astype(f32).astype(bf16)
    for r in range(rows):
        moved = jnp.dot(back, low[pl.ds(r * span, span), :], preferred_element_type=f32)
        hidden_grad[r] = moved.astype(bf16)
    wait_all(sends)


def mixer_taps(
    info, where, slots, gm, parts, before, after, ext, st, ct, xpt, pre1, gres, grate, sums_one, sums_two,
    seq_count, dw_shapes,
):
    rows, padded, _, wide = ext.shape
    seg, width = padded - 4, wide // 3
    tokens = rows * seg * segs
    count, outs = len(parts), len(dw_shapes)
    return pl.pallas_call(
        lambda *refs: taps_kernel(rows, seg * segs, seq_count, count, outs, *refs),
        out_shape=(vm((rows, seg * segs, width), bf16), vm((small_rows, width)))
        + tuple(vm(s, bf16) for s in dw_shapes),
        in_specs=smem_spec() * 3 + hbm_specs(count + 4) + vmem_specs(8),
        out_specs=tuple(vmem_specs(2)) + tuple(any_specs(outs)),
        scratch_shapes=[
            pltpu.VMEM((rows, seg, segs, lane_block), f32),
            pltpu.VMEM(gm.shape, f32),
            pltpu.VMEM(ext.shape, f32),
            pltpu.VMEM(xpt.shape, bf16),
            pltpu.VMEM(pre1.shape, f32),
            pltpu.VMEM((tokens, wide), bf16),
            pltpu.VMEM((16, wide), f32),
            pltpu.VMEM((width, wide), bf16),
            pltpu.VMEM((width, wide), bf16),
            pltpu.VMEM((tokens, width), bf16),
            pltpu.SemaphoreType.DMA((2, wide // lane_block)),
            pltpu.SemaphoreType.DMA((2,)),
            pltpu.SemaphoreType.DMA((count,)),
            pltpu.SemaphoreType.DMA((3, outs * dw_shapes[0][0])),
        ],
        compiler_params=pltpu.CompilerParams(vmem_limit_bytes=vmem_cap),
        cost_estimate=spent(1),
        name="mixer_taps",
    )(
        info, where, slots, *parts, gm, ext, xpt, pre1, before, after, st, ct, gres, grate, sums_one, sums_two
    )


def chip_pairs(count):
    first = [(d, d ^ (2 if d % 2 == 0 else 4)) for d in range(count)]
    second = [(d, d ^ (4 if d % 2 == 0 else 2)) for d in range(count)]
    core = [(d, d ^ 1) for d in range(count)]
    return core, first, second


def tie(value, *needs):
    return lax.optimization_barrier((value, needs))[0]


def cross(block, pairs):
    return lax.ppermute(block, "dp", pairs)


def shard_order(me):
    even = (me & 1) == 0
    f = jnp.where(even, 2, 4)
    g = jnp.where(even, 4, 2)
    near = [me, me ^ f, me ^ g, me ^ 6]
    far = [me ^ 1, me ^ 1 ^ g, me ^ 1 ^ f, me ^ 7]
    return jnp.stack(near + far).astype(jnp.int32)


def slot_order(me):
    even = (me & 1) == 0
    f = jnp.where(even, 2, 4)
    g = jnp.where(even, 4, 2)
    mine = [me, me ^ g, me ^ f, me ^ 6]
    theirs = [me ^ 1, me ^ 1 ^ f, me ^ 1 ^ g, me ^ 7]
    return jnp.stack(mine + theirs).astype(jnp.int32)


class Gather:
    def __init__(self, shard, name):
        self.shard, self.name = shard, name
        self.core, self.first, self.second = chip_pairs(8)

    def one(self, *needs):
        with jax.named_scope(self.name + "_one"):
            self.p1 = cross(tie(self.shard, *needs), self.first)
        return self.p1

    def two(self, *needs):
        with jax.named_scope(self.name + "_two"):
            self.p2 = cross(tie(self.shard, *needs), self.second)
        return self.p2

    def three(self, *needs):
        with jax.named_scope(self.name + "_three"):
            self.p3 = cross(tie(self.p1, *needs), self.second)
        return self.p3

    def share(self, early=(), late=()):
        near = [self.shard, self.p1, self.p2, self.p3]
        with jax.named_scope(self.name + "_core"):
            sent = [tie(p, *early) for p in near[:3]] + [tie(near[3], *late)]
            self.parts = near + [cross(p, self.core) for p in sent]
        return self.parts


class Scatter:
    steps = 6

    def __init__(self, mine, theirs, name):
        self.mine, self.theirs, self.name, self.at = mine, theirs, name, 0
        self.core, self.first, self.second = chip_pairs(8)
        self.odd = lax.axis_index("seq") & 1
        self.near = [(i, i ^ 1) for i in range(4)]

    def step(self, *needs):
        self.at += 1
        with jax.named_scope(f"{self.name}_s{self.at}"):
            return getattr(self, f"step{self.at}")(needs)

    def step1(self, needs):
        self.sent = tie(self.theirs, *needs)
        self.got = cross(self.sent, self.core)
        return self.got

    def step2(self, needs):
        got = tie(self.got, *needs)
        self.sent = (self.mine[2:].astype(f32) + got[2:].astype(f32)).astype(bf16)
        self.got1 = cross(self.sent, self.first)
        return self.got1

    def step3(self, needs):
        got1 = tie(self.got1, *needs)
        send = self.mine[1].astype(f32) + self.got[1].astype(f32) + got1[1].astype(f32)
        self.sent = send.astype(bf16)
        self.got2 = cross(self.sent, self.second)
        return self.got2

    def own_half(self, got2, high):
        depth, wide = got2.shape[0] // 2, got2.shape[1]

        def cut(block):
            if block.ndim == 2:
                return lax.dynamic_slice(block, (high * depth, 0), (depth, wide)).astype(f32)
            return lax.dynamic_slice(block, (0, high * depth, 0), (1, depth, wide))[0].astype(f32)

        return cut(self.mine) + cut(self.got) + cut(self.got1) + cut(got2)

    def step4(self, needs):
        self.sent = self.own_half(tie(self.got2, *needs), 1 - self.odd).astype(bf16)
        self.h1 = lax.ppermute(self.sent, "seq", self.near)
        return self.h1

    def step5(self, needs):
        part = self.own_half(self.got2, self.odd) + tie(self.h1, *needs).astype(f32)
        self.part = self.sent = part.astype(bf16)
        self.h2 = lax.ppermute(self.part, "seq", [(i, i ^ 2) for i in range(4)])
        return self.h2

    def step6(self, needs):
        self.total = (self.part.astype(f32) + tie(self.h2, *needs).astype(f32)).astype(bf16)
        self.sent = self.total
        self.h3 = lax.ppermute(self.total, "seq", self.near)
        return self.h3

    def result(self):
        odd = self.odd == 1
        low = jnp.where(odd, self.h3, self.total)
        return jnp.concatenate([low, jnp.where(odd, self.total, self.h3)]).astype(f32)


class Total:
    steps = 5

    def __init__(self, flat, name):
        self.flat, self.name, self.at = flat, name, 0

    def step(self, *needs):
        axis, count, bit = (("dp", 8, 1), ("dp", 8, 2), ("dp", 8, 4), ("seq", 4, 1), ("seq", 4, 2))[self.at]
        self.at += 1
        with jax.named_scope(f"{self.name}_s{self.at}"):
            flat = self.sent = tie(self.flat, *needs)
            got = lax.ppermute(flat, axis, [(d, d ^ bit) for d in range(count)])
            self.flat = flat + got
        return got

    def result(self):
        return self.flat


def advance(last, *flows):
    for f in flows:
        f.step(last)
        last = f.sent
    return last


def local(
    hidden_in,
    seq_len,
    bucket,
    in_weight,
    in_bias,
    short_taps,
    cond_taps,
    mode_residue,
    mode_rate,
    out_weight,
    out_bias,
    norm1_gain,
    norm1_bias,
    gate_weight,
    up_weight,
    down_weight,
    down_bias,
    norm2_gain,
    norm2_bias,
    out_cotangent,
):
    rows, span, width = hidden_in.shape
    tokens, seg = rows * span, span // segs
    dp_count, seq_count = lax.axis_size("dp"), lax.axis_size("seq")
    me, place = lax.axis_index("dp"), lax.axis_index("seq")
    info = jnp.concatenate([seq_len, bucket, place[None]]).astype(jnp.int32)
    chips = dp_count == 8 and seq_count == 4
    up_line = [(i, i + 1) for i in range(seq_count - 1)]
    down_line = [(i + 1, i) for i in range(seq_count - 1)]

    def rims(low, high):
        return lax.ppermute(high, "seq", up_line), lax.ppermute(low, "seq", down_line)

    def dw_shapes(depth, wide):
        return ((4, depth, wide),) * 2 if chips else ((1, depth * dp_count, wide),)

    def line(vec):
        return vec[None]

    def states_of(block, sign):
        return [
            lax.ppermute(block, "seq", [(i, i + sign * k) for i in range(seq_count) if 0 <= i + sign * k < seq_count])
            for k in range(1, seq_count)
        ]

    depth, hidden = gate_weight.shape
    half = hidden // 2
    before, after = rims(
        hidden_in[:, :2].reshape(2 * rows, width), hidden_in[:, span - 2 :].reshape(2 * rows, width)
    )
    shards = (
        jnp.concatenate([in_weight, out_weight], axis=1),
        down_weight,
        jnp.concatenate([gate_weight, up_weight], axis=1),
    )
    if chips:
        w_io, w_d, w_f = (Gather(shard, name) for shard, name in zip(shards, ("w_in_out", "w_down", "w_feed")))
        w_io.one()
        w_io.two()
        w_io.three(w_io.p2, before, after, shards[2], info)
        io_parts = w_io.share((w_io.p1,))
        w_d.one(w_io.p3)
        w_d.two(w_io.p3)
    else:
        io_parts, d_parts, f_parts = ([lax.all_gather(shard, "dp", axis=0, tiled=True)] for shard in shards)
    one = jnp.zeros((1,), jnp.int32)
    where = shard_order(me) if chips else one
    slots = slot_order(me) if chips else one

    xp, xpt, cp, ext, q, keys, vals, ends, dev_end = mixer_enter(
        info, where, hidden_in, out_cotangent, before, after, line(in_bias), short_taps, cond_taps, mode_rate,
        io_parts, seq_count,
    )
    gath = states_of(tie(dev_end, w_d.p1, w_d.p2) if chips else dev_end, 1)
    wait = ()
    if chips:
        w_f.one(dev_end, w_d.p1, w_d.p2)
        w_f.two(dev_end, w_d.p1, w_d.p2)
    long_out, gated_t, carry, n1, s1, low, low_t = mixer_settle(
        tie(info, *wait), where, gath, ends, q, keys, vals, mode_rate, mode_residue, xp,
        line(out_bias), line(norm1_gain), line(norm1_bias), io_parts,
    )
    if chips:
        w_d.three(low)
        d_parts = w_d.share((low,), (low,))
        w_f.three(low, w_f.p2)
        f_parts = w_f.share((low,), (low,))
    layer_out, *grads, pre1, gg, back_ends, back_dev, sums_two, sums_one = feed_core(
        info, where, slots, f_parts, d_parts, io_parts, low, low_t, gated_t, n1, s1, cp, q, line(norm1_gain),
        line(norm1_bias), line(down_bias), line(norm2_gain), line(norm2_bias), mode_rate,
        dw_shapes(*down_weight.shape), dw_shapes(depth, hidden), dw_shapes(depth, width + hidden),
    )
    gg = gg.reshape(q.shape)
    back_gath = states_of(back_dev, -1)
    wait = ()
    if chips:
        s_d, s_a, s_b = (
            Scatter(*grads[2 * k : 2 * k + 2], name) for k, name in enumerate(("g_down", "g_feed", "g_out_feed"))
        )
        s_d.step()
        s_a.step()
        s_b.step()
        wait = advance(back_gath, s_d)
    gm, rim_low, rim_high, g_res, g_rate = mixer_source(
        tie(info, wait), back_gath, back_ends, carry, gg, q, long_out, keys, vals, mode_rate, mode_residue
    )
    before, after = rims(rim_low, rim_high)
    if chips:
        wait = advance(rim_low, s_d, s_a)
    grad_hidden, small, *g_in = mixer_taps(
        tie(info, wait), where, slots, gm, io_parts, before, after, ext, short_taps, cond_taps,
        xpt, pre1, g_res, g_rate, sums_one, sums_two, seq_count, dw_shapes(depth, 3 * width),
    )

    if chips:
        s_in = Scatter(*g_in, "g_in")
        s_small = Total(small, "g_small")
        s_in.step()
        order = (
            s_d, s_a, s_b, s_small, s_in, s_d, s_a, s_b, s_small, s_d, s_in, s_a, s_b, s_small, s_a, s_in,
            s_b, s_small, s_in, s_b, s_small, s_in,
        )
        advance(small, *order)
        flow = (s_in, s_small, s_d, s_a, s_b)
        share_in, small, share_down, share_a, share_b = (f.result() for f in flow)
    else:

        def share(grad):
            own = lax.psum_scatter(grad[0], "dp", scatter_dimension=0, tiled=True)
            return lax.psum(own, "seq").astype(f32)

        share_in, share_down, share_a, share_b = map(share, (*g_in, *grads))
        small = lax.psum(small, ("dp", "seq"))
    share_out = share_b[:, :width]
    share_gate = jnp.concatenate([share_a[:, :half], share_b[:, width : width + half]], axis=1)
    share_up = jnp.concatenate([share_a[:, half:], share_b[:, width + half :]], axis=1)
    modes = mode_rate.shape[0]
    return (
        layer_out, grad_hidden, share_in,
        small[row_bias : row_bias + 3].reshape(3 * width),
        small[row_short : row_short + 9].reshape(3, 3 * width),
        small[row_cond : row_cond + 3],
        small[row_res : row_res + modes],
        small[row_rate : row_rate + modes],
        share_out, small[row_one], small[row_one + 1], small[row_one + 2],
        share_gate, share_up, share_down, small[row_two], small[row_two + 1], small[row_two + 2],
    )


def solution(mesh):
    split, weight, full = P("dp", "seq", None), P("dp", None), P()
    in_specs = (
        split, P("dp"), P("dp"), weight, full, full, full, full, full, weight,
        full, full, full, weight, weight, weight, full, full, full, split,
    )
    out_specs = (
        split, split, weight, full, full, full, full, full, weight, full,
        full, full, weight, weight, weight, full, full, full,
    )
    return jax.shard_map(local, mesh=mesh, in_specs=in_specs, out_specs=out_specs, check_vma=False)
```

```python
import jax
import jax.numpy as jnp
from jax import lax
from jax.experimental import pallas as pl
from jax.experimental.pallas import tpu as pltpu
from jax.sharding import PartitionSpec as P

norm_eps = 1e-05
f32 = jnp.float32
bf16 = jnp.bfloat16
segs = 8
lane_block = 256
vmem_cap = 60 * 1024 * 1024


def iota(shape, dim):
    return lax.broadcasted_iota(jnp.int32, shape, dim)


def factor_of(info, rows, r):
    b = info[rows + r]
    return jnp.where(b == 0, 4.0, jnp.where(b == 1, 2.0, 1.0)).astype(f32)


def order_matrix(span):
    seg = span // segs
    o, n = iota((span, span), 0), iota((span, span), 1)
    return (n == (o & (segs - 1)) * seg + lax.shift_right_logical(o, 3)).astype(f32).astype(bf16)


def fill_edges(ext, r, seg, halo, cols):
    n = cols[1]
    c = pl.ds(cols[0], n)
    sub = iota((segs, n), 0)
    for h, (dst, src, shift, edge) in enumerate(
        ((0, seg, 1, 0), (1, seg + 1, 1, 0), (seg + 2, 2, segs - 1, segs - 1), (seg + 3, 3, segs - 1, segs - 1))
    ):
        rolled = pltpu.roll(ext[r, src, :, c], shift, 0)
        ext[r, dst, :, c] = jnp.where(sub == edge, halo[pl.ds(4 * r + h, 1), c], rolled)


def fetch_parts(where, parts, full, sems, at=0, cols=None):
    depth, wide = parts[0].shape[0], full.shape[1] if cols is None else cols.size
    copies = []
    for k, part in enumerate(parts):
        src = part if part.shape[1] == wide else part.at[:, pl.ds(at, wide)]
        dst = full.at[pl.ds(pl.multiple_of(where[k] * depth, 8), depth)]
        if cols is not None:
            dst = full.at[pl.ds(pl.multiple_of(where[k] * depth, 8), depth), cols]
        copies.append(pltpu.make_async_copy(src, dst, sems.at[k]))
    return copies


def start_all(copies):
    for copy in copies:
        copy.start()


def wait_all(copies):
    for copy in copies:
        copy.wait()


def send_parts(where, full, outs, sems, cols=None, into=None):
    per, depth = outs[0].shape[0], outs[0].shape[1]
    copies = []
    for k in range(per * len(outs)):
        rows_of = pl.ds(pl.multiple_of(where[k] * depth, 8), depth)
        src, dst = full.at[rows_of], outs[k // per].at[k % per]
        if cols is not None:
            src, dst = full.at[rows_of, cols], outs[k // per].at[k % per, :, cols]
        if into is not None:
            dst = outs[k // per].at[k % per, :, into]
        copies.append(pltpu.make_async_copy(src, dst, sems.at[k]))
    return copies


def join_rims(rows, before, after, rim):
    rim[...] = jnp.zeros_like(rim)
    low, high = before[...].astype(f32), after[...].astype(f32)
    for r in range(rows):
        for k in range(2):
            rim[pl.ds(4 * r + k, 1), :] = low[2 * r + k : 2 * r + k + 1]
            rim[pl.ds(4 * r + 2 + k, 1), :] = high[2 * r + k : 2 * r + k + 1]


def enter_kernel(rows, span, seq_count, count, info, where, x, cot, before, after, bias, st, ct, rate, *refs):
    parts, refs = refs[:count], refs[count:]
    xp, xpt, cp, ext, q, keys, vals, ends, dev_end, mask, hal, xh, w, sems = refs
    copies = fetch_parts(where, parts, w, sems)
    start_all(copies)
    width = x.shape[2]
    seg = span // segs
    place = info[2 * rows]
    base = place * span
    order = order_matrix(span)
    for r in range(rows):
        moved = jnp.dot(order, x[r], preferred_element_type=f32).astype(bf16)
        xp[pl.ds(r * span, span), :] = moved
        xpt[:, pl.ds(r * span, span)] = moved.T
        cp[pl.ds(r * span, span), :] = jnp.dot(order, cot[r], preferred_element_type=f32).astype(bf16)
        n = iota((span, 128), 0)
        pos = base + (n & (segs - 1)) * seg + lax.shift_right_logical(n, 3)
        mask[pl.ds(r * span, span), :] = (pos < info[r]).astype(f32)
    join_rims(rows, before, after, xh)
    edge_rows = xh[...].astype(bf16)
    hn = iota((16, 128), 0)
    hk = hn & 3
    hpos = base + jnp.where(hk < 2, hk - 2, span + hk - 2)
    hlim = jnp.where(lax.shift_right_logical(hn, 2) == 0, info[0], info[1])
    hmask = ((hpos >= 0) & (hpos < hlim)).astype(f32)
    wait_all(copies)

    @pl.loop(0, 3 * width // lane_block)
    def _(t):
        cols = pl.ds(pl.multiple_of(t * lane_block, lane_block), lane_block)
        part = jnp.dot(xp[...], w[:, cols], preferred_element_type=f32) + bias[:, cols]
        rim = jnp.dot(edge_rows, w[:, cols], preferred_element_type=f32) + bias[:, cols]
        for s in range(lane_block // 128):
            sub = slice(s * 128, (s + 1) * 128)
            scol = pl.ds(pl.multiple_of(t * lane_block + s * 128, 128), 128)
            low = (part[:, sub] * mask[...]).astype(bf16).astype(f32)
            for r in range(rows):
                ext[r, pl.ds(2, seg), :, scol] = low[r * span : (r + 1) * span].reshape(seg, segs, 128)
            hal[:, scol] = (rim[:, sub] * hmask).astype(bf16).astype(f32)

    sub = iota((segs, lane_block), 0)
    first = (place == 0).astype(f32)
    last = (place == seq_count - 1).astype(f32)
    in_low = 1.0 - first * (sub == 0).astype(f32)
    in_high = 1.0 - last * (sub == segs - 1).astype(f32)
    for r in range(rows):
        factor = factor_of(info, rows, r)
        for t in range(3 * width // lane_block):
            fill_edges(ext, r, seg, hal, (t * lane_block, lane_block))
        for t in range(width // lane_block):
            cq = pl.ds(t * lane_block, lane_block)
            ck = pl.ds(width + t * lane_block, lane_block)
            cv = pl.ds(2 * width + t * lane_block, lane_block)
            modes = rate.shape[0]
            fade = [jnp.exp(-rate[pl.ds(m, 1), cq] * factor) for m in range(modes)]
            far = [jnp.exp(-rate[pl.ds(m, 1), cq] * (factor * seg)) for m in range(modes)]

            def tap3(cols, e):
                return (
                    st[pl.ds(0, 1), cols] * ext[r, e - 1, :, cols]
                    + st[pl.ds(1, 1), cols] * ext[r, e, :, cols]
                    + st[pl.ds(2, 1), cols] * ext[r, e + 1, :, cols]
                )

            def step(j, carry):
                kp_prev, kp_cur, states = carry
                kp_next = tap3(ck, j + 3)
                kp_next = jnp.where(j == seg - 1, kp_next * in_high, kp_next)
                key = (
                    ct[pl.ds(0, 1), cq] * kp_prev
                    + ct[pl.ds(1, 1), cq] * kp_cur
                    + ct[pl.ds(2, 1), cq] * kp_next
                )
                val = tap3(cv, j + 2)
                q[r, j, :, cq] = tap3(cq, j + 2)
                keys[r, j, :, cq] = key
                vals[r, j, :, cq] = val
                live = (base + sub * seg + j < info[r]).astype(f32)
                src = key * val * live
                return (kp_cur, kp_next, tuple(f * h + src for f, h in zip(fade, states)))

            zero = jnp.zeros((segs, lane_block), f32)
            start = (tap3(ck, 1) * in_low, tap3(ck, 2), (zero,) * modes)
            _, _, states = lax.fori_loop(0, seg, step, start, unroll=4)
            for m in range(modes):
                ends[r, m, :, cq] = states[m]
                total = jnp.zeros((1, lane_block), f32)
                for i in range(segs):
                    total = far[m] * total + states[m][i : i + 1]
                dev_end[r, pl.ds(m, 1), cq] = total


def vm(shape, dtype=f32):
    return jax.ShapeDtypeStruct(shape, dtype)


def vmem_specs(n):
    return [pl.BlockSpec(memory_space=pltpu.VMEM)] * n


def smem_spec():
    return [pl.BlockSpec(memory_space=pltpu.SMEM)]


def spent(us):
    return pl.CostEstimate(flops=int(us * 1.1e9), bytes_accessed=1_000_000, transcendentals=0)


def any_specs(n):
    return [pl.BlockSpec(memory_space=pl.ANY)] * n


def hbm_specs(n):
    return [pl.BlockSpec(memory_space=pltpu.HBM)] * n


def mixer_enter(info, where, hidden, cot, before, after, bias, st, ct, rate, parts, seq_count):
    rows, span, width = hidden.shape
    seg, modes, tokens = span // segs, rate.shape[0], rows * span
    body = (rows, seg, segs, width)
    return pl.pallas_call(
        lambda *refs: enter_kernel(rows, span, seq_count, len(parts), *refs),
        out_shape=(
            vm((tokens, width), bf16),
            vm((width, tokens), bf16),
            vm((tokens, width), bf16),
            vm((rows, seg + 4, segs, 3 * width)),
            vm(body),
            vm(body),
            vm(body),
            vm((rows, modes, segs, width)),
            vm((rows, modes, width)),
        ),
        in_specs=smem_spec() * 2 + vmem_specs(8) + hbm_specs(len(parts)),
        out_specs=tuple(vmem_specs(9)),
        scratch_shapes=[
            pltpu.VMEM((tokens, 128), f32),
            pltpu.VMEM((16, 3 * width), f32),
            pltpu.VMEM((16, width), f32),
            pltpu.VMEM((width, 3 * width), bf16),
            pltpu.SemaphoreType.DMA((len(parts),)),
        ],
        compiler_params=pltpu.CompilerParams(vmem_limit_bytes=vmem_cap),
        cost_estimate=spent(1),
        name="mixer_enter",
    )(info, where, hidden, cot, before, after, bias, st, ct, rate, *parts)


def carry_in(parts, fade_span):
    total = parts[0]
    scale = fade_span
    for p in parts[1:]:
        total = total + scale * p
        scale = scale * fade_span
    return total


def settle_kernel(rows, span, others, count, info, where, *refs):
    gath, refs = refs[:others], refs[others:]
    parts, refs = refs[:count], refs[count:]
    ends, q, keys, vals, rate, res, xp, vecs, long_out, gated_t, carry_out, n1, s1, low, low_t, gsc, wo, sems = refs
    ob, gain, shift = (vecs.at[pl.ds(k, 1)] for k in range(3))
    copies = fetch_parts(where, parts, wo, sems, parts[0].shape[1] - wo.shape[1])
    start_all(copies)
    seg = span // segs
    width = q.shape[3]
    modes = rate.shape[0]
    base = info[2 * rows] * span
    sub = iota((segs, lane_block), 0)
    for r in range(rows):
        factor = factor_of(info, rows, r)
        for t in range(width // lane_block):
            c = pl.ds(t * lane_block, lane_block)
            fade, mix, start = [], [], []
            for m in range(modes):
                d = rate[pl.ds(m, 1), c] * factor
                fade.append(jnp.exp(-d))
                mix.append(res[pl.ds(m, 1), c] * jnp.sqrt(1.0 - jnp.exp(-2.0 * d)))
                far = jnp.exp(-d * seg)
                cur = carry_in([g[r, pl.ds(m, 1), c] for g in gath], jnp.exp(-d * span))
                tile = jnp.zeros((segs, lane_block), f32)
                end = ends[r, m, :, c]
                for i in range(segs):
                    tile = jnp.where(sub == i, cur, tile)
                    cur = far * cur + end[i : i + 1]
                carry_out[r, m, :, c] = tile
                start.append(tile)

            def step(j, states):
                live = (base + sub * seg + j < info[r]).astype(f32)
                src = keys[r, j, :, c] * vals[r, j, :, c] * live
                states = tuple(f * h + src for f, h in zip(fade, states))
                out = mix[0] * states[0]
                for m in range(1, modes):
                    out = out + mix[m] * states[m]
                long_out[r, j, :, c] = out
                gsc[r, j, :, c] = q[r, j, :, c] * out * live
                return states

            lax.fori_loop(0, seg, step, tuple(start), unroll=4)
    wait_all(copies)
    for r in range(rows):
        tok = pl.ds(r * span, span)
        cut = gsc[r].reshape(span, width).astype(bf16)
        gated_t[:, tok] = cut.T
        n1[tok, :] = xp[tok, :].astype(f32) + jnp.dot(cut, wo[...], preferred_element_type=f32) + ob[...]

    @pl.loop(0, rows * span // 16, unroll=4)
    def _(k):
        tok = pl.ds(pl.multiple_of(k * 16, 16), 16)
        v = n1[tok, :]
        centre = v - jnp.mean(v, axis=-1, keepdims=True)
        inv = lax.rsqrt(jnp.mean(centre * centre, axis=-1, keepdims=True) + norm_eps)
        n = centre * inv
        n1[tok, :] = n
        s1[tok, :] = jnp.broadcast_to(inv, (16, 128))
        low[tok, :] = (n * gain[...] + shift[...]).astype(bf16)

    low_t[...] = low[...].T


def mixer_settle(info, where, gath, ends, q, keys, vals, rate, res, xp, vecs, parts):
    rows, seg, _, width = q.shape
    span = seg * segs
    tokens, modes = rows * span, rate.shape[0]
    return pl.pallas_call(
        lambda *refs: settle_kernel(rows, span, len(gath), len(parts), *refs),
        out_shape=(
            vm(q.shape),
            vm((width, tokens), bf16),
            vm(ends.shape),
            vm((tokens, width)),
            vm((tokens, 128)),
            vm((tokens, width), bf16),
            vm((width, tokens), bf16),
        ),
        in_specs=smem_spec() * 2 + vmem_specs(len(gath)) + hbm_specs(len(parts)) + vmem_specs(8),
        out_specs=tuple(vmem_specs(7)),
        scratch_shapes=[
            pltpu.VMEM(q.shape, f32),
            pltpu.VMEM((width, width), bf16),
            pltpu.SemaphoreType.DMA((len(parts),)),
        ],
        compiler_params=pltpu.CompilerParams(vmem_limit_bytes=vmem_cap),
        cost_estimate=spent(1),
        name="mixer_settle",
    )(info, where, *gath, *parts, ends, q, keys, vals, rate, res, xp, vecs)


def row_mean(v):
    return jnp.mean(v, axis=-1, keepdims=True)


def fold(v):
    return v[:8] + v[8:]


def contract_last(a, b):
    return lax.dot_general(a, b, (((1,), (1,)), ((), ())), preferred_element_type=f32)


hidden_tile = 512


def core_kernel(rows, span, count, outs, info, where, slots, *refs):
    w_parts, o_parts, refs = refs[:count], refs[count : 2 * count], refs[2 * count :]
    if outs == 1:
        d_parts, refs = refs[:1], refs[1:]
    low_h, low_th, gated_th, n1_h, s1_h, cp_h, q_h, vecs, rate, layer = refs[:10]
    refs = refs[10:]
    gain1, shift1, bias, gain2, shift2 = (vecs.at[pl.ds(k, 1)] for k in range(1, 6))
    down_out, first_out, second_out, refs = refs[:outs], refs[outs : 2 * outs], refs[2 * outs : 3 * outs], refs[3 * outs :]
    pre1_h, gg_h, ends, dev_end, sums_two, sums_one, w, wd, wo, act, pull, gel, low, low_t, gated_t = refs[:15]
    n1, s1, cp, q, acc, first, feed, out_low, mix, gs, us, dd, dwg, dwu, dwo = refs[15:30]
    in_sems, w_sems, d_sems, o_sems, dd_sems, dw_sems, end_sems = refs[30:]
    hidden, width = wd.shape
    tile, seg, modes = hidden_tile, span // segs, rate.shape[0]
    tiles, tokens = hidden // tile, rows * span
    base = info[2 * rows] * span

    def bring(k, src, dst):
        return pltpu.make_async_copy(src, dst, in_sems.at[k])

    w_in = [
        [
            copy
            for k, at in enumerate((t * tile, hidden + t * tile))
            for copy in fetch_parts(where, w_parts, w, w_sems.at[k, t], at, pl.ds(at, tile))
        ]
        for t in range(tiles)
    ]
    if outs == 1:
        d_in = fetch_parts(where, d_parts, wd, d_sems.at[0])
    else:
        depth = w_parts[0].shape[0]
        d_in = [
            pltpu.make_async_copy(
                part.at[:, pl.ds(2 * hidden + j * width, width)],
                wd.at[pl.ds(pl.multiple_of(where[k] * (hidden // count) + j * depth, 8), depth)],
                d_sems.at[j, k],
            )
            for k, part in enumerate(w_parts)
            for j in range(hidden // count // depth)
        ]
    o_in = fetch_parts(where, o_parts, wo, o_sems, o_parts[0].shape[1] - width)
    low_in = bring(0, low_h, low)
    norm_in = [bring(1, n1_h, n1), bring(2, cp_h, cp)]
    late_in = [bring(3, low_th, low_t), bring(4, s1_h, s1), bring(5, q_h, q), bring(6, gated_th, gated_t)]
    start_all([low_in] + w_in[0] + w_in[1])
    low_in.wait()
    scale = 0.7978845608028654
    for t in range(tiles):
        if t + 2 < tiles:
            start_all(w_in[t + 2])
        if t == 1:
            start_all(d_in)
        if t == 3:
            start_all(norm_in)
        wait_all(w_in[t])
        cols, up_cols = pl.ds(t * tile, tile), pl.ds(hidden + t * tile, tile)
        gs[...] = jnp.dot(low[...], w[:, cols], preferred_element_type=f32)
        us[...] = jnp.dot(low[...], w[:, up_cols], preferred_element_type=f32)

        @pl.loop(0, tokens // 16, unroll=2)
        def _(k):
            tok = pl.ds(pl.multiple_of(k * 16, 16), 16)
            g, u = gs[tok, :], us[tok, :]
            sq = g * g
            th = jnp.tanh(g * (scale + (scale * 0.044715) * sq))
            side = 0.5 + 0.5 * th
            gelu = g * side
            slope = side + (0.5 * g) * (1.0 - th * th) * (scale + (3.0 * scale * 0.044715) * sq)
            act[tok, cols] = (gelu * u).astype(bf16)
            pull[tok, cols] = (u * slope).astype(bf16)
            gel[tok, cols] = gelu.astype(bf16)

    wait_all(d_in)
    for t in range(width // lane_block):
        c = pl.ds(t * lane_block, lane_block)
        acc[:, c] = jnp.dot(act[...], wd[:, c], preferred_element_type=f32)
    zero = jnp.zeros((8, width), f32)
    wait_all(norm_in)
    start_all(late_in + o_in)

    def outer_norm(k, loop):
        tok = pl.ds(pl.multiple_of(k * 16, 16), 16)
        n = iota((16, width), 0) + k * 16
        n = n & (span - 1)
        pos = base + (n & (segs - 1)) * seg + lax.shift_right_logical(n, 3)
        limit = jnp.where(k * 16 >= span, info[1], info[0])
        keep = (pos < limit).astype(f32)
        v = n1[tok, :] * gain1[...] + shift1[...] + acc[tok, :] + bias[...]
        centre = v - row_mean(v)
        inv = lax.rsqrt(row_mean(centre * centre) + norm_eps)
        n2 = centre * inv
        out_low[tok, :] = ((n2 * gain2[...] + shift2[...]) * keep).astype(bf16)
        top = cp[tok, :].astype(f32) * keep
        e = top * gain2[...]
        grad = inv * (e - row_mean(e) - n2 * row_mean(e * n2))
        first[tok, :] = grad
        cut = grad.astype(bf16)
        feed[tok, :] = cut
        return (
            loop[0] + fold(cut.astype(f32)),
            loop[1] + fold(top * n2),
            loop[2] + fold(top),
        )

    totals = lax.fori_loop(0, tokens // 16, outer_norm, (zero, zero, zero), unroll=4)
    for k in range(3):
        sums_two[pl.ds(k, 1), :] = jnp.sum(totals[k], axis=0, keepdims=True)

    blocks = 8
    span_d = hidden // blocks
    d_sends = []
    for k in range(blocks):
        if k >= 2:
            d_sends[k - 2].wait()
        which = k if outs == 1 else slots[k]
        c = pl.ds(pl.multiple_of(which * span_d, 128), span_d)
        dd[k % 2] = jnp.dot(act[:, c].T, feed[...], preferred_element_type=f32).astype(bf16)
        per = down_out[0].shape[0]
        dst = down_out[0].at[0, pl.ds(k * span_d, span_d)] if outs == 1 else down_out[k // per].at[k % per]
        d_sends.append(pltpu.make_async_copy(dd.at[k % 2], dst, dd_sems.at[k]))
        d_sends[k].start()
    o, n = iota((span, span), 0), iota((span, span), 1)
    back = (o == (n & (segs - 1)) * seg + lax.shift_right_logical(n, 3)).astype(f32).astype(bf16)
    for r in range(rows):
        layer[r] = jnp.dot(back, out_low[pl.ds(r * span, span), :], preferred_element_type=f32).astype(bf16)
    wait_all(late_in)
    sends = []
    half_tiles = tiles // 2
    for t in range(tiles):
        cols, up_cols = pl.ds(t * tile, tile), pl.ds(hidden + t * tile, tile)
        grad = contract_last(feed[...], wd[cols, :])
        g = (grad * pull[:, cols].astype(f32)).astype(bf16)
        u = (grad * gel[:, cols].astype(f32)).astype(bf16)
        if t >= 2:
            wait_all(sends[t - 2])
        dwg[t % 2] = jnp.dot(low_t[...], g, preferred_element_type=f32).astype(bf16)
        dwu[t % 2] = jnp.dot(low_t[...], u, preferred_element_type=f32).astype(bf16)
        into, at, own = (first_out, 0, t) if t < half_tiles else (second_out, width, t - half_tiles)
        g_at, u_at = at + own * tile, at + (half_tiles + own) * tile
        sends.append(
            send_parts(slots, dwg.at[t % 2], into, dw_sems.at[0, t], None, pl.ds(g_at, tile))
            + send_parts(slots, dwu.at[t % 2], into, dw_sems.at[1, t], None, pl.ds(u_at, tile))
        )
        start_all(sends[t])
        first[...] += contract_last(g, w[:, cols]) + contract_last(u, w[:, up_cols])

    def put(k, src, dst):
        return pltpu.make_async_copy(src, dst, end_sems.at[k])

    def inner_norm(k, loop):
        tok = pl.ds(pl.multiple_of(k * 16, 16), 16)
        top, n = first[tok, :], n1[tok, :]
        e = top * gain1[...]
        grad = s1[tok, 0:1] * (e - row_mean(e) - n * row_mean(e * n))
        acc[tok, :] = grad
        cut = grad.astype(bf16)
        mix[tok, :] = cut
        return (
            loop[0] + fold(cut.astype(f32)),
            loop[1] + fold(top * n),
            loop[2] + fold(top),
        )

    totals = lax.fori_loop(0, tokens // 16, inner_norm, (zero, zero, zero), unroll=4)
    finals = [put(0, acc, pre1_h)]
    finals[0].start()
    for k in range(3):
        sums_one[pl.ds(k, 1), :] = jnp.sum(totals[k], axis=0, keepdims=True)
    dwo[...] = jnp.dot(gated_t[...], mix[...], preferred_element_type=f32).astype(bf16)
    o_sends = send_parts(slots, dwo, second_out, dw_sems.at[2, 0], None, pl.ds(0, width))
    start_all(o_sends)
    wait_all(o_in)
    for t in range(width // lane_block):
        c = pl.ds(t * lane_block, lane_block)
        first[:, c] = contract_last(mix[...], wo[c, :])
    sub = iota((segs, lane_block), 0)
    for r in range(rows):
        factor = factor_of(info, rows, r)
        for t in range(width // lane_block):
            c = pl.ds(t * lane_block, lane_block)
            fade = [jnp.exp(-rate[pl.ds(m, 1), c] * factor) for m in range(modes)]
            far = [jnp.exp(-rate[pl.ds(m, 1), c] * (factor * seg)) for m in range(modes)]

            def step(k, states):
                j = seg - 1 - k
                live = (base + sub * seg + j < info[r]).astype(f32)
                tok = pl.ds(pl.multiple_of(r * span + j * segs, segs), segs)
                grad = first[tok, c] * live
                first[tok, c] = grad
                g = grad * q[r, j, :, c]
                return tuple(f * h + g for f, h in zip(fade, states))

            blank = jnp.zeros((segs, lane_block), f32)
            states = lax.fori_loop(0, seg, step, (blank,) * modes, unroll=4)
            for m in range(modes):
                ends[r, m, :, c] = states[m]
                total = jnp.zeros((1, lane_block), f32)
                for i in reversed(range(segs)):
                    total = far[m] * total + states[m][i : i + 1]
                dev_end[r, pl.ds(m, 1), c] = total
    finals.append(put(1, first, gg_h))
    finals[1].start()
    for copies in [d_sends[-2:]] + sends[-2:] + [o_sends, finals]:
        wait_all(copies)


def feed_core(
    info, where, slots, w_parts, d_parts, o_parts, low, low_t, gated_t, n1, s1, cp, q, vecs, rate, down_shapes, first_shapes, second_shapes,
):
    tokens, width = n1.shape
    rows, seg = q.shape[:2]
    modes, count, outs = rate.shape[0], len(w_parts), len(first_shapes)
    hidden, tile, pieces = down_shapes[0][0] * outs * down_shapes[0][1], hidden_tile, first_shapes[0][0] * outs
    shapes = tuple(down_shapes) + tuple(first_shapes) + tuple(second_shapes)
    return pl.pallas_call(
        lambda *refs: core_kernel(rows, seg * segs, count, outs, *refs),
        out_shape=(vm((rows, seg * segs, width), bf16),)
        + tuple(vm(s, bf16) for s in shapes)
        + (
            vm((tokens, width)),
            vm((tokens, width)),
            vm((rows, modes, segs, width)),
            vm((rows, modes, width)),
            vm((8, width)),
            vm((8, width)),
        ),
        in_specs=smem_spec() * 3 + hbm_specs(2 * count + len(d_parts) + 7) + vmem_specs(2),
        out_specs=tuple(vmem_specs(1) + hbm_specs(3 * outs + 2) + vmem_specs(4)),
        scratch_shapes=[
            pltpu.VMEM((width, 2 * hidden), bf16),
            pltpu.VMEM((hidden, width), bf16),
            pltpu.VMEM((width, width), bf16),
            pltpu.VMEM((tokens, hidden), bf16),
            pltpu.VMEM((tokens, hidden), bf16),
            pltpu.VMEM((tokens, hidden), bf16),
            pltpu.VMEM((tokens, width), bf16),
            pltpu.VMEM((width, tokens), bf16),
            pltpu.VMEM((width, tokens), bf16),
            pltpu.VMEM((tokens, width), f32),
            pltpu.VMEM((tokens, 128), f32),
            pltpu.VMEM((tokens, width), bf16),
            pltpu.VMEM(q.shape, f32),
            pltpu.VMEM((tokens, width), f32),
            pltpu.VMEM((tokens, width), f32),
            pltpu.VMEM((tokens, width), bf16),
            pltpu.VMEM((tokens, width), bf16),
            pltpu.VMEM((tokens, width), bf16),
            pltpu.VMEM((tokens, tile), f32),
            pltpu.VMEM((tokens, tile), f32),
            pltpu.VMEM((2, hidden // 8, width), bf16),
            pltpu.VMEM((2, width, tile), bf16),
            pltpu.VMEM((2, width, tile), bf16),
            pltpu.VMEM((width, width), bf16),
            pltpu.SemaphoreType.DMA((7,)),
            pltpu.SemaphoreType.DMA((2, hidden // tile, count)),
            pltpu.SemaphoreType.DMA((hidden // width, count)),
            pltpu.SemaphoreType.DMA((count,)),
            pltpu.SemaphoreType.DMA((8,)),
            pltpu.SemaphoreType.DMA((3, hidden // tile, pieces)),
            pltpu.SemaphoreType.DMA((2,)),
        ],
        compiler_params=pltpu.CompilerParams(vmem_limit_bytes=vmem_cap),
        cost_estimate=spent(1),
        name="feed_core",
    )(
        info, where, slots, *w_parts, *o_parts, *d_parts, low, low_t, gated_t, n1, s1, cp, q, vecs, rate
    )


def split_rims(rows, seg, at, rim, low, high):
    for r in range(rows):
        for k in range(2):
            rim[pl.ds(2 * r + k, 1), :] = at(r, k, pl.ds(0, 1))
            rim[pl.ds(2 * (rows + r) + k, 1), :] = at(r, seg - 2 + k, pl.ds(segs - 1, 1))
    low[...] = rim[: 2 * rows].astype(bf16)
    high[...] = rim[2 * rows : 4 * rows].astype(bf16)


def source_kernel(rows, span, others, info, *refs):
    gath = refs[:others]
    ends, carry, rate, res, refs = *refs[others : others + 4], refs[others + 4 :]
    streams, refs = refs[:5], refs[5:]
    gm_h, rim_low, rim_high, gres, grate, gg, q, long_out, keys, vals, gm, hist, rim, in_sems, out_sems = refs
    seg = span // segs
    width, modes = q.shape[3], rate.shape[0]
    blocks = width // lane_block
    ins = [
        [
            pltpu.make_async_copy(
                src.at[:, :, :, pl.ds(t * lane_block, lane_block)],
                dst.at[:, :, :, pl.ds(t * lane_block, lane_block)],
                in_sems.at[t, k],
            )
            for k, (src, dst) in enumerate(zip(streams, (gg, q, long_out, keys, vals)))
        ]
        for t in range(blocks)
    ]
    sends = [
        [
            pltpu.make_async_copy(
                gm.at[:, :, :, pl.ds(b * width + t * lane_block, lane_block)],
                gm_h.at[:, pl.ds(2, seg), :, pl.ds(b * width + t * lane_block, lane_block)],
                out_sems.at[t, b],
            )
            for b in range(3)
        ]
        for t in range(blocks)
    ]
    for t in range(blocks):
        start_all(ins[t])
    base = info[2 * rows] * span
    sub = iota((segs, lane_block), 0)
    for t in range(blocks):
        wait_all(ins[t])
        c = pl.ds(t * lane_block, lane_block)
        sum_res = [jnp.zeros((1, lane_block), f32) for _ in range(modes)]
        sum_rate = [jnp.zeros((1, lane_block), f32) for _ in range(modes)]
        for r in range(rows):
            factor = factor_of(info, rows, r)
            fade, mix, start, root, ebb = [], [], [], [], []
            for m in range(modes):
                d = rate[pl.ds(m, 1), c] * factor
                fade.append(jnp.exp(-d))
                ebb.append(jnp.exp(-2.0 * d))
                root.append(jnp.sqrt(1.0 - ebb[m]))
                mix.append(res[pl.ds(m, 1), c] * root[m])
                far = jnp.exp(-d * seg)
                cur = carry_in([g[r, pl.ds(m, 1), c] for g in gath], jnp.exp(-d * span))
                tile = jnp.zeros((segs, lane_block), f32)
                end = ends[r, m, :, c]
                for i in reversed(range(segs)):
                    tile = jnp.where(sub == i, cur, tile)
                    cur = far * cur + end[i : i + 1]
                start.append(tile)

            def ahead(j, loop):
                states, sums = loop
                live = (base + sub * seg + j < info[r]).astype(f32)
                src = keys[r, j, :, c] * vals[r, j, :, c] * live
                g = gg[r, j, :, c] * q[r, j, :, c]
                past = tuple(f * h for f, h in zip(fade, states))
                for m in range(modes):
                    hist[m, j] = past[m]
                states = tuple(p + src for p in past)
                return (states, tuple(s + g * h for s, h in zip(sums, states)))

            zero = jnp.zeros((segs, lane_block), f32)
            init = tuple(carry[r, m, :, c] for m in range(modes))
            _, with_state = lax.fori_loop(0, seg, ahead, (init, (zero,) * modes), unroll=4)

            def behind(k, loop):
                states, sums = loop
                j = seg - 1 - k
                live = (base + sub * seg + j < info[r]).astype(f32)
                grad = gg[r, j, :, c]
                g = grad * q[r, j, :, c]
                states = tuple(f * h + g for f, h in zip(fade, states))
                gs = mix[0] * states[0]
                for m in range(1, modes):
                    gs = gs + mix[m] * states[m]
                gs = gs * live
                for b, part in enumerate(
                    (grad * long_out[r, j, :, c], gs * vals[r, j, :, c], gs * keys[r, j, :, c])
                ):
                    gm[r, j, :, pl.ds(b * width + t * lane_block, lane_block)] = part.astype(bf16).astype(f32)
                return (states, tuple(s + h * hist[m, j] for m, (s, h) in enumerate(zip(sums, states))))

            _, with_lag = lax.fori_loop(0, seg, behind, (tuple(start), (zero,) * modes), unroll=4)
            for m in range(modes):
                u = jnp.sum(with_state[m], axis=0, keepdims=True)
                v = jnp.sum(with_lag[m], axis=0, keepdims=True)
                sum_res[m] = sum_res[m] + root[m] * u
                sum_rate[m] = sum_rate[m] + factor * res[pl.ds(m, 1), c] * (ebb[m] / root[m] * u - root[m] * v)
        for m in range(modes):
            gres[pl.ds(m, 1), c] = sum_res[m]
            grate[pl.ds(m, 1), c] = sum_rate[m]
        start_all(sends[t])
    split_rims(rows, seg, lambda r, j, i: gm[r, j, i, :], rim, rim_low, rim_high)
    for t in range(blocks):
        wait_all(sends[t])


def mixer_source(info, gath, ends, carry, gg, q, long_out, keys, vals, rate, res):
    rows, seg, _, width = q.shape
    modes = rate.shape[0]
    return pl.pallas_call(
        lambda *refs: source_kernel(rows, seg * segs, len(gath), *refs),
        out_shape=(
            vm((rows, seg + 4, segs, 3 * width)),
            vm((2 * rows, 3 * width), bf16),
            vm((2 * rows, 3 * width), bf16),
            vm((modes, width)),
            vm((modes, width)),
        ),
        in_specs=smem_spec() + vmem_specs(4 + len(gath)) + hbm_specs(5),
        out_specs=tuple(hbm_specs(1) + vmem_specs(4)),
        scratch_shapes=[pltpu.VMEM(q.shape, f32)] * 5
        + [
            pltpu.VMEM((rows, seg, segs, 3 * width), f32),
            pltpu.VMEM((modes, seg, segs, lane_block), f32),
            pltpu.VMEM((4 * rows, 3 * width), f32),
            pltpu.SemaphoreType.DMA((width // lane_block, 5)),
            pltpu.SemaphoreType.DMA((width // lane_block, 3)),
        ],
        compiler_params=pltpu.CompilerParams(vmem_limit_bytes=vmem_cap),
        cost_estimate=spent(1),
        name="mixer_source",
    )(info, *gath, ends, carry, rate, res, gg, q, long_out, keys, vals)


def taps_blocks(rows, span, seq_count, info, gm, halo, ext, st, ct, gp, put, gsc, ready, done):
    seg = span // segs
    width = ct.shape[1]
    place = info[2 * rows]
    base = place * span
    sub = iota((segs, lane_block), 0)
    in_low = 1.0 - (place == 0).astype(f32) * (sub == 0).astype(f32)
    in_high = 1.0 - (place == seq_count - 1).astype(f32) * (sub == segs - 1).astype(f32)
    zero = jnp.zeros((segs, lane_block), f32)
    for block in range(3):
        for t in range(width // lane_block):
            ready(block * (width // lane_block) + t)
            for r in range(rows):
                fill_edges(gm, r, seg, halo, (block * width + t * lane_block, lane_block))
            c = pl.ds(block * width + t * lane_block, lane_block)
            lanes = pl.ds(t * lane_block, lane_block)
            sums = tuple(zero for _ in range(4))
            csums = tuple(zero for _ in range(3))
            for r in range(rows):

                def tap3(e):
                    return (
                        st[pl.ds(0, 1), c] * ext[r, e - 1, :, c]
                        + st[pl.ds(1, 1), c] * ext[r, e, :, c]
                        + st[pl.ds(2, 1), c] * ext[r, e + 1, :, c]
                    )

                def grad_at(e):
                    if block != 1:
                        return gm[r, e, :, c]
                    return (
                        ct[pl.ds(0, 1), lanes] * gm[r, e + 1, :, c]
                        + ct[pl.ds(1, 1), lanes] * gm[r, e, :, c]
                        + ct[pl.ds(2, 1), lanes] * gm[r, e - 1, :, c]
                    )

                def step(j, loop):
                    prev, cur, kp_prev, kp_cur, sums, csums = loop
                    nxt = grad_at(j + 3)
                    if block == 1:
                        nxt = jnp.where(j == seg - 1, nxt * in_high, nxt)
                        kp_next = tap3(j + 3)
                        kp_next = jnp.where(j == seg - 1, kp_next * in_high, kp_next)
                        own = gm[r, j + 2, :, c]
                        csums = tuple(s + own * k for s, k in zip(csums, (kp_prev, kp_cur, kp_next)))
                    else:
                        kp_next = kp_cur
                    live = (base + sub * seg + j < info[r]).astype(f32)
                    full = (
                        st[pl.ds(0, 1), c] * nxt + st[pl.ds(1, 1), c] * cur + st[pl.ds(2, 1), c] * prev
                    ) * live
                    full = full.astype(bf16).astype(f32)
                    gsc[r, j] = full
                    sums = (
                        sums[0] + cur * ext[r, j + 1, :, c],
                        sums[1] + cur * ext[r, j + 2, :, c],
                        sums[2] + cur * ext[r, j + 3, :, c],
                        sums[3] + full,
                    )
                    return (cur, nxt, kp_cur, kp_next, sums, csums)

                if block == 1:
                    start = (grad_at(1) * in_low, grad_at(2), tap3(1) * in_low, tap3(2), sums, csums)
                else:
                    start = (grad_at(1), grad_at(2), zero, zero, sums, csums)
                _, _, _, _, sums, csums = lax.fori_loop(0, seg, step, start, unroll=4)
                gp[pl.ds(r * span, span), c] = gsc[r].reshape(span, lane_block).astype(bf16)
            for k in range(3):
                put("short", k, block, lanes, jnp.sum(sums[k], axis=0, keepdims=True))
            put("bias", 0, block, lanes, jnp.sum(sums[3], axis=0, keepdims=True))
            if block == 1:
                for k in range(3):
                    put("cond", k, block, lanes, jnp.sum(csums[k], axis=0, keepdims=True))
        done(block)


row_bias, row_short, row_cond, row_res, row_rate, row_one, row_two, small_rows = 0, 3, 12, 15, 19, 23, 26, 32


def small_put(small):
    def put(kind, k, block, lanes, value):
        row = {"bias": row_bias + block, "short": row_short + 3 * k + block, "cond": row_cond + k}[kind]
        small[pl.ds(row, 1), lanes] = value

    return put


def taps_kernel(rows, span, seq_count, count, outs, info, where, slots, *refs):
    parts, refs = refs[:count], refs[count:]
    gm_h, ext_h, xpt_h, pre1_h, before, after, st, ct, gres, grate, sums_one, sums_two = refs[:12]
    hidden_grad, small = refs[12:14]
    dws, refs = refs[14 : 14 + outs], refs[14 + outs :]
    gsc, gm, ext, xpt, pre1, gp, halo, w, dw, low, stream_sems, in_sems, sems, out_sems = refs
    width = ct.shape[1]
    groups = 3 * width // lane_block
    streams = [
        [
            pltpu.make_async_copy(
                src.at[:, :, :, pl.ds(n * lane_block, lane_block)],
                dst.at[:, :, :, pl.ds(n * lane_block, lane_block)],
                stream_sems.at[k, n],
            )
            for k, (src, dst) in enumerate(((gm_h, gm), (ext_h, ext)))
        ]
        for n in range(groups)
    ]
    late = [pltpu.make_async_copy(xpt_h, xpt, in_sems.at[0]), pltpu.make_async_copy(pre1_h, pre1, in_sems.at[1])]
    copies = fetch_parts(where, parts, w, sems)
    for n in range(groups):
        start_all(streams[n])
        if n == 2:
            late[0].start()
    start_all(copies + late[1:])
    small[...] = jnp.zeros_like(small)
    modes = gres.shape[0]
    small[pl.ds(row_res, modes), :] = gres[...]
    small[pl.ds(row_rate, modes), :] = grate[...]
    small[pl.ds(row_one, 3), :] = sums_one[pl.ds(0, 3), :]
    small[pl.ds(row_two, 3), :] = sums_two[pl.ds(0, 3), :]
    join_rims(rows, before, after, halo)
    sends = []

    def done(block):
        c = pl.ds(block * width, width)
        if block == 0:
            late[0].wait()
        dw[:, c] = jnp.dot(xpt[...], gp[:, c], preferred_element_type=f32).astype(bf16)
        sends.extend(send_parts(slots, dw, dws, out_sems.at[block], c))
        start_all(sends[-outs * dws[0].shape[0] :])

    taps_blocks(
        rows, span, seq_count, info, gm, halo, ext, st, ct, gp, small_put(small), gsc,
        lambda n: wait_all(streams[n]), done,
    )
    wait_all(copies + late[1:])
    low[...] = (contract_last(gp[...], w[...]) + pre1[...]).astype(bf16)
    o, n = iota((span, span), 0), iota((span, span), 1)
    seg = span // segs
    back = (o == (n & (segs - 1)) * seg + lax.shift_right_logical(n, 3)).astype(f32).astype(bf16)
    for r in range(rows):
        moved = jnp.dot(back, low[pl.ds(r * span, span), :], preferred_element_type=f32)
        hidden_grad[r] = moved.astype(bf16)
    wait_all(sends)


def mixer_taps(
    info, where, slots, gm, parts, before, after, ext, st, ct, xpt, pre1, gres, grate, sums_one, sums_two,
    seq_count, dw_shapes,
):
    rows, padded, _, wide = ext.shape
    seg, width = padded - 4, wide // 3
    tokens = rows * seg * segs
    count, outs = len(parts), len(dw_shapes)
    return pl.pallas_call(
        lambda *refs: taps_kernel(rows, seg * segs, seq_count, count, outs, *refs),
        out_shape=(vm((rows, seg * segs, width), bf16), vm((small_rows, width)))
        + tuple(vm(s, bf16) for s in dw_shapes),
        in_specs=smem_spec() * 3 + hbm_specs(count + 4) + vmem_specs(8),
        out_specs=tuple(vmem_specs(2)) + tuple(any_specs(outs)),
        scratch_shapes=[
            pltpu.VMEM((rows, seg, segs, lane_block), f32),
            pltpu.VMEM(gm.shape, f32),
            pltpu.VMEM(ext.shape, f32),
            pltpu.VMEM(xpt.shape, bf16),
            pltpu.VMEM(pre1.shape, f32),
            pltpu.VMEM((tokens, wide), bf16),
            pltpu.VMEM((16, wide), f32),
            pltpu.VMEM((width, wide), bf16),
            pltpu.VMEM((width, wide), bf16),
            pltpu.VMEM((tokens, width), bf16),
            pltpu.SemaphoreType.DMA((2, wide // lane_block)),
            pltpu.SemaphoreType.DMA((2,)),
            pltpu.SemaphoreType.DMA((count,)),
            pltpu.SemaphoreType.DMA((3, outs * dw_shapes[0][0])),
        ],
        compiler_params=pltpu.CompilerParams(vmem_limit_bytes=vmem_cap),
        cost_estimate=spent(1),
        name="mixer_taps",
    )(
        info, where, slots, *parts, gm, ext, xpt, pre1, before, after, st, ct, gres, grate, sums_one, sums_two
    )


def chip_pairs(count):
    first = [(d, d ^ (2 if d % 2 == 0 else 4)) for d in range(count)]
    second = [(d, d ^ (4 if d % 2 == 0 else 2)) for d in range(count)]
    core = [(d, d ^ 1) for d in range(count)]
    return core, first, second


def tie(value, *needs):
    return lax.optimization_barrier((value, needs))[0]


def cross(block, pairs):
    return lax.ppermute(block, "dp", pairs)


def shard_order(me):
    even = (me & 1) == 0
    f = jnp.where(even, 2, 4)
    g = jnp.where(even, 4, 2)
    near = [me, me ^ f, me ^ g, me ^ 6]
    far = [me ^ 1, me ^ 1 ^ g, me ^ 1 ^ f, me ^ 7]
    return jnp.stack(near + far).astype(jnp.int32)


def slot_order(me):
    even = (me & 1) == 0
    f = jnp.where(even, 2, 4)
    g = jnp.where(even, 4, 2)
    mine = [me, me ^ g, me ^ f, me ^ 6]
    theirs = [me ^ 1, me ^ 1 ^ f, me ^ 1 ^ g, me ^ 7]
    return jnp.stack(mine + theirs).astype(jnp.int32)


class Gather:
    def __init__(self, shard, name):
        self.shard, self.name = shard, name
        self.core, self.first, self.second = chip_pairs(8)

    def one(self, *needs):
        with jax.named_scope(self.name + "_one"):
            self.p1 = cross(tie(self.shard, *needs), self.first)
        return self.p1

    def two(self, *needs):
        with jax.named_scope(self.name + "_two"):
            self.p2 = cross(tie(self.shard, *needs), self.second)
        return self.p2

    def three(self, *needs):
        with jax.named_scope(self.name + "_three"):
            self.p3 = cross(tie(self.p1, *needs), self.second)
        return self.p3

    def share(self, early=(), late=()):
        near = [self.shard, self.p1, self.p2, self.p3]
        with jax.named_scope(self.name + "_core"):
            sent = [tie(p, *early) for p in near[:3]] + [tie(near[3], *late)]
            self.parts = near + [cross(p, self.core) for p in sent]
        return self.parts


class Scatter:
    steps = 6

    def __init__(self, mine, theirs, name):
        self.mine, self.theirs, self.name, self.at = mine, theirs, name, 0
        self.core, self.first, self.second = chip_pairs(8)
        self.odd = lax.axis_index("seq") & 1
        self.near = [(i, i ^ 1) for i in range(4)]

    def step(self, *needs):
        self.at += 1
        with jax.named_scope(f"{self.name}_s{self.at}"):
            return getattr(self, f"step{self.at}")(needs)

    def step1(self, needs):
        self.sent = tie(self.theirs, *needs)
        self.got = cross(self.sent, self.core)
        return self.got

    def step2(self, needs):
        got = tie(self.got, *needs)
        self.sent = (self.mine[2:].astype(f32) + got[2:].astype(f32)).astype(bf16)
        self.got1 = cross(self.sent, self.first)
        return self.got1

    def step3(self, needs):
        got1 = tie(self.got1, *needs)
        send = self.mine[1].astype(f32) + self.got[1].astype(f32) + got1[1].astype(f32)
        self.sent = send.astype(bf16)
        self.got2 = cross(self.sent, self.second)
        return self.got2

    def own_half(self, got2, high):
        depth, wide = got2.shape[0] // 2, got2.shape[1]

        def cut(block):
            if block.ndim == 2:
                return lax.dynamic_slice(block, (high * depth, 0), (depth, wide)).astype(f32)
            return lax.dynamic_slice(block, (0, high * depth, 0), (1, depth, wide))[0].astype(f32)

        return cut(self.mine) + cut(self.got) + cut(self.got1) + cut(got2)

    def step4(self, needs):
        self.sent = self.own_half(tie(self.got2, *needs), 1 - self.odd).astype(bf16)
        self.h1 = lax.ppermute(self.sent, "seq", self.near)
        return self.h1

    def step5(self, needs):
        part = self.own_half(self.got2, self.odd) + tie(self.h1, *needs).astype(f32)
        self.part = self.sent = part.astype(bf16)
        self.h2 = lax.ppermute(self.part, "seq", [(i, i ^ 2) for i in range(4)])
        return self.h2

    def step6(self, needs):
        self.total = (self.part.astype(f32) + tie(self.h2, *needs).astype(f32)).astype(bf16)
        self.sent = self.total
        self.h3 = lax.ppermute(self.total, "seq", self.near)
        return self.h3

    def result(self):
        odd = self.odd == 1
        low = jnp.where(odd, self.h3, self.total)
        return jnp.concatenate([low, jnp.where(odd, self.total, self.h3)]).astype(f32)


class Total:
    steps = 5

    def __init__(self, flat, name):
        self.flat, self.name, self.at = flat, name, 0

    def step(self, *needs):
        axis, count, bit = (("dp", 8, 1), ("dp", 8, 2), ("dp", 8, 4), ("seq", 4, 1), ("seq", 4, 2))[self.at]
        self.at += 1
        with jax.named_scope(f"{self.name}_s{self.at}"):
            flat = self.sent = tie(self.flat, *needs)
            got = lax.ppermute(flat, axis, [(d, d ^ bit) for d in range(count)])
            self.flat = flat + got
        return got

    def result(self):
        return self.flat


def advance(last, *flows):
    for f in flows:
        f.step(last)
        last = f.sent
    return last


def local(
    hidden_in,
    seq_len,
    bucket,
    in_weight,
    in_bias,
    short_taps,
    cond_taps,
    mode_residue,
    mode_rate,
    out_weight,
    out_bias,
    norm1_gain,
    norm1_bias,
    gate_weight,
    up_weight,
    down_weight,
    down_bias,
    norm2_gain,
    norm2_bias,
    out_cotangent,
):
    rows, span, width = hidden_in.shape
    tokens, seg = rows * span, span // segs
    dp_count, seq_count = lax.axis_size("dp"), lax.axis_size("seq")
    me, place = lax.axis_index("dp"), lax.axis_index("seq")
    info = jnp.concatenate([seq_len, bucket, place[None]]).astype(jnp.int32)
    chips = dp_count == 8 and seq_count == 4
    up_line = [(i, i + 1) for i in range(seq_count - 1)]
    down_line = [(i + 1, i) for i in range(seq_count - 1)]

    def rims(low, high):
        return lax.ppermute(high, "seq", up_line), lax.ppermute(low, "seq", down_line)

    def dw_shapes(depth, wide):
        return ((4, depth, wide),) * 2 if chips else ((1, depth * dp_count, wide),)

    line_in = in_bias[None]
    vecs = jnp.stack([out_bias, norm1_gain, norm1_bias, down_bias, norm2_gain, norm2_bias])

    def states_of(block, sign):
        return [
            lax.ppermute(block, "seq", [(i, i + sign * k) for i in range(seq_count) if 0 <= i + sign * k < seq_count])
            for k in range(1, seq_count)
        ]

    hidden = gate_weight.shape[1]
    depth = gate_weight.shape[0]
    half = hidden // 2
    before, after = rims(
        hidden_in[:, :2].reshape(2 * rows, width), hidden_in[:, span - 2 :].reshape(2 * rows, width)
    )
    shard_io = jnp.concatenate([in_weight, out_weight], axis=1)
    d_parts = ()
    if chips:
        downs = [down_weight[k * depth : (k + 1) * depth] for k in range(hidden // width)]
        shard_f = jnp.concatenate([gate_weight, up_weight, *downs], axis=1)
        w_io, w_f = Gather(shard_io, "w_in_out"), Gather(shard_f, "w_feed_down")
        w_io.one()
        w_io.two()
        w_io.three(w_io.p2, before, after, shard_f, info)
        io_parts = w_io.share((w_io.p1,))
        w_f.one(w_io.p3)
        w_f.two(w_io.p3)
    else:
        shard_f = jnp.concatenate([gate_weight, up_weight], axis=1)
        io_parts, f_parts, d_parts = (
            [lax.all_gather(shard, "dp", axis=0, tiled=True)] for shard in (shard_io, shard_f, down_weight)
        )
    one = jnp.zeros((1,), jnp.int32)
    where = shard_order(me) if chips else one
    slots = slot_order(me) if chips else one

    xp, xpt, cp, ext, q, keys, vals, ends, dev_end = mixer_enter(
        info, where, hidden_in, out_cotangent, before, after, line_in, short_taps, cond_taps, mode_rate,
        io_parts, seq_count,
    )
    gath = states_of(dev_end, 1)
    if chips:
        w_f.three(gath, w_f.p2, vecs)
    long_out, gated_t, carry, n1, s1, low, low_t = mixer_settle(
        info, where, gath, ends, q, keys, vals, mode_rate, mode_residue, xp,
        vecs, io_parts,
    )
    if chips:
        f_parts = w_f.share((gath,), (low,))
    layer_out, *grads, pre1, gg, back_ends, back_dev, sums_two, sums_one = feed_core(
        info, where, slots, f_parts, d_parts, io_parts, low, low_t, gated_t, n1, s1, cp, q, vecs, mode_rate,
        dw_shapes(*down_weight.shape), dw_shapes(depth, hidden), dw_shapes(depth, width + hidden),
    )
    gg = gg.reshape(q.shape)
    back_gath = states_of(back_dev, -1)
    wait = ()
    if chips:
        s_d, s_a, s_b = (
            Scatter(*grads[2 * k : 2 * k + 2], name) for k, name in enumerate(("g_down", "g_feed", "g_out_feed"))
        )
        s_d.step()
        s_a.step(back_gath)
        s_b.step(back_gath)
        wait = advance(back_gath[0], s_d)
    gm, rim_low, rim_high, g_res, g_rate = mixer_source(
        tie(info, wait), back_gath, back_ends, carry, gg, q, long_out, keys, vals, mode_rate, mode_residue
    )
    before, after = rims(rim_low, rim_high)
    if chips:
        wait = advance(rim_low, s_d, s_a)
    grad_hidden, small, *g_in = mixer_taps(
        tie(info, wait), where, slots, gm, io_parts, before, after, ext, short_taps, cond_taps,
        xpt, pre1, g_res, g_rate, sums_one, sums_two, seq_count, dw_shapes(depth, 3 * width),
    )

    if chips:
        s_in = Scatter(*g_in, "g_in")
        s_small = Total(small, "g_small")
        s_in.step()
        order = (
            s_b, s_d, s_a, s_in, s_d, s_d, s_a, s_b, s_in, s_small, s_a, s_b, s_small, s_in, s_a, s_small, s_b,
            s_in, s_small, s_b, s_small, s_in,
        )
        advance(small, *order)
        flow = (s_in, s_small, s_d, s_a, s_b)
        share_in, small, share_down, share_a, share_b = (f.result() for f in flow)
    else:

        def share(grad):
            own = lax.psum_scatter(grad[0], "dp", scatter_dimension=0, tiled=True)
            return lax.psum(own, "seq").astype(f32)

        share_in, share_down, share_a, share_b = map(share, (*g_in, *grads))
        small = lax.psum(small, ("dp", "seq"))
    share_out = share_b[:, :width]
    share_gate = jnp.concatenate([share_a[:, :half], share_b[:, width : width + half]], axis=1)
    share_up = jnp.concatenate([share_a[:, half:], share_b[:, width + half :]], axis=1)
    modes = mode_rate.shape[0]
    return (
        layer_out, grad_hidden, share_in,
        small[row_bias : row_bias + 3].reshape(3 * width),
        small[row_short : row_short + 9].reshape(3, 3 * width),
        small[row_cond : row_cond + 3],
        small[row_res : row_res + modes],
        small[row_rate : row_rate + modes],
        share_out, small[row_one], small[row_one + 1], small[row_one + 2],
        share_gate, share_up, share_down, small[row_two], small[row_two + 1], small[row_two + 2],
    )


def solution(mesh):
    split, weight, full = P("dp", "seq", None), P("dp", None), P()
    in_specs = (
        split, P("dp"), P("dp"), weight, full, full, full, full, full, weight,
        full, full, full, weight, weight, weight, full, full, full, split,
    )
    out_specs = (
        split, split, weight, full, full, full, full, full, weight, full,
        full, full, weight, weight, weight, full, full, full,
    )
    return jax.shard_map(local, mesh=mesh, in_specs=in_specs, out_specs=out_specs, check_vma=False)
```

```python
import jax
import jax.numpy as jnp
from jax import lax
from jax.experimental import pallas as pl
from jax.experimental.pallas import tpu as pltpu
from jax.sharding import PartitionSpec as P

norm_eps = 1e-05
f32 = jnp.float32
bf16 = jnp.bfloat16
segs = 8
lane_block = 256
vmem_cap = 60 * 1024 * 1024


def iota(shape, dim):
    return lax.broadcasted_iota(jnp.int32, shape, dim)


def factor_of(info, rows, r):
    b = info[rows + r]
    return jnp.where(b == 0, 4.0, jnp.where(b == 1, 2.0, 1.0)).astype(f32)


def order_matrix(span):
    seg = span // segs
    o, n = iota((span, span), 0), iota((span, span), 1)
    return (n == (o & (segs - 1)) * seg + lax.shift_right_logical(o, 3)).astype(f32).astype(bf16)


def fill_edges(ext, r, seg, halo, cols):
    n = cols[1]
    c = pl.ds(cols[0], n)
    sub = iota((segs, n), 0)
    for h, (dst, src, shift, edge) in enumerate(
        ((0, seg, 1, 0), (1, seg + 1, 1, 0), (seg + 2, 2, segs - 1, segs - 1), (seg + 3, 3, segs - 1, segs - 1))
    ):
        rolled = pltpu.roll(ext[r, src, :, c], shift, 0)
        ext[r, dst, :, c] = jnp.where(sub == edge, halo[pl.ds(4 * r + h, 1), c], rolled)


def fetch_parts(where, parts, full, sems, at=0, cols=None):
    depth, wide = parts[0].shape[0], full.shape[1] if cols is None else cols.size
    copies = []
    for k, part in enumerate(parts):
        src = part if part.shape[1] == wide else part.at[:, pl.ds(at, wide)]
        dst = full.at[pl.ds(pl.multiple_of(where[k] * depth, 8), depth)]
        if cols is not None:
            dst = full.at[pl.ds(pl.multiple_of(where[k] * depth, 8), depth), cols]
        copies.append(pltpu.make_async_copy(src, dst, sems.at[k]))
    return copies


def start_all(copies):
    for copy in copies:
        copy.start()


def wait_all(copies):
    for copy in copies:
        copy.wait()


def send_parts(where, full, outs, sems, cols=None, into=None):
    per, depth = outs[0].shape[0], outs[0].shape[1]
    copies = []
    for k in range(per * len(outs)):
        rows_of = pl.ds(pl.multiple_of(where[k] * depth, 8), depth)
        src, dst = full.at[rows_of], outs[k // per].at[k % per]
        if cols is not None:
            src, dst = full.at[rows_of, cols], outs[k // per].at[k % per, :, cols]
        if into is not None:
            dst = outs[k // per].at[k % per, :, into]
        copies.append(pltpu.make_async_copy(src, dst, sems.at[k]))
    return copies


def join_rims(rows, before, after, rim):
    rim[...] = jnp.zeros_like(rim)
    low, high = before[...].astype(f32), after[...].astype(f32)
    for r in range(rows):
        for k in range(2):
            rim[pl.ds(4 * r + k, 1), :] = low[2 * r + k : 2 * r + k + 1]
            rim[pl.ds(4 * r + 2 + k, 1), :] = high[2 * r + k : 2 * r + k + 1]


def enter_kernel(rows, span, seq_count, count, info, where, x, cot, before, after, bias, st, ct, rate, *refs):
    parts, refs = refs[:count], refs[count:]
    xp, xpt, cp, ext, q, keys, vals, ends, dev_end, mask, hal, xh, w, sems = refs
    copies = fetch_parts(where, parts, w, sems)
    start_all(copies)
    width = x.shape[2]
    seg = span // segs
    place = info[2 * rows]
    base = place * span
    order = order_matrix(span)
    for r in range(rows):
        moved = jnp.dot(order, x[r], preferred_element_type=f32).astype(bf16)
        xp[pl.ds(r * span, span), :] = moved
        xpt[:, pl.ds(r * span, span)] = moved.T
        cp[pl.ds(r * span, span), :] = jnp.dot(order, cot[r], preferred_element_type=f32).astype(bf16)
        n = iota((span, 128), 0)
        pos = base + (n & (segs - 1)) * seg + lax.shift_right_logical(n, 3)
        mask[pl.ds(r * span, span), :] = (pos < info[r]).astype(f32)
    join_rims(rows, before, after, xh)
    edge_rows = xh[...].astype(bf16)
    hn = iota((16, 128), 0)
    hk = hn & 3
    hpos = base + jnp.where(hk < 2, hk - 2, span + hk - 2)
    hlim = jnp.where(lax.shift_right_logical(hn, 2) == 0, info[0], info[1])
    hmask = ((hpos >= 0) & (hpos < hlim)).astype(f32)
    wait_all(copies)

    @pl.loop(0, 3 * width // lane_block)
    def _(t):
        cols = pl.ds(pl.multiple_of(t * lane_block, lane_block), lane_block)
        part = jnp.dot(xp[...], w[:, cols], preferred_element_type=f32) + bias[:, cols]
        rim = jnp.dot(edge_rows, w[:, cols], preferred_element_type=f32) + bias[:, cols]
        for s in range(lane_block // 128):
            sub = slice(s * 128, (s + 1) * 128)
            scol = pl.ds(pl.multiple_of(t * lane_block + s * 128, 128), 128)
            low = (part[:, sub] * mask[...]).astype(bf16).astype(f32)
            for r in range(rows):
                ext[r, pl.ds(2, seg), :, scol] = low[r * span : (r + 1) * span].reshape(seg, segs, 128)
            hal[:, scol] = (rim[:, sub] * hmask).astype(bf16).astype(f32)

    sub = iota((segs, lane_block), 0)
    first = (place == 0).astype(f32)
    last = (place == seq_count - 1).astype(f32)
    in_low = 1.0 - first * (sub == 0).astype(f32)
    in_high = 1.0 - last * (sub == segs - 1).astype(f32)
    for r in range(rows):
        factor = factor_of(info, rows, r)
        for t in range(3 * width // lane_block):
            fill_edges(ext, r, seg, hal, (t * lane_block, lane_block))
        for t in range(width // lane_block):
            cq = pl.ds(t * lane_block, lane_block)
            ck = pl.ds(width + t * lane_block, lane_block)
            cv = pl.ds(2 * width + t * lane_block, lane_block)
            modes = rate.shape[0]
            fade = [jnp.exp(-rate[pl.ds(m, 1), cq] * factor) for m in range(modes)]
            far = [jnp.exp(-rate[pl.ds(m, 1), cq] * (factor * seg)) for m in range(modes)]

            def tap3(cols, e):
                return (
                    st[pl.ds(0, 1), cols] * ext[r, e - 1, :, cols]
                    + st[pl.ds(1, 1), cols] * ext[r, e, :, cols]
                    + st[pl.ds(2, 1), cols] * ext[r, e + 1, :, cols]
                )

            def step(j, carry):
                kp_prev, kp_cur, states = carry
                kp_next = tap3(ck, j + 3)
                kp_next = jnp.where(j == seg - 1, kp_next * in_high, kp_next)
                key = (
                    ct[pl.ds(0, 1), cq] * kp_prev
                    + ct[pl.ds(1, 1), cq] * kp_cur
                    + ct[pl.ds(2, 1), cq] * kp_next
                )
                val = tap3(cv, j + 2)
                q[r, j, :, cq] = tap3(cq, j + 2)
                keys[r, j, :, cq] = key
                vals[r, j, :, cq] = val
                live = (base + sub * seg + j < info[r]).astype(f32)
                src = key * val * live
                return (kp_cur, kp_next, tuple(f * h + src for f, h in zip(fade, states)))

            zero = jnp.zeros((segs, lane_block), f32)
            start = (tap3(ck, 1) * in_low, tap3(ck, 2), (zero,) * modes)
            _, _, states = lax.fori_loop(0, seg, step, start, unroll=4)
            for m in range(modes):
                ends[r, m, :, cq] = states[m]
                total = jnp.zeros((1, lane_block), f32)
                for i in range(segs):
                    total = far[m] * total + states[m][i : i + 1]
                dev_end[r, pl.ds(m, 1), cq] = total


def vm(shape, dtype=f32):
    return jax.ShapeDtypeStruct(shape, dtype)


def vmem_specs(n):
    return [pl.BlockSpec(memory_space=pltpu.VMEM)] * n


def smem_spec():
    return [pl.BlockSpec(memory_space=pltpu.SMEM)]


def spent(us):
    return pl.CostEstimate(flops=int(us * 1.1e9), bytes_accessed=1_000_000, transcendentals=0)


def any_specs(n):
    return [pl.BlockSpec(memory_space=pl.ANY)] * n


def hbm_specs(n):
    return [pl.BlockSpec(memory_space=pltpu.HBM)] * n


def mixer_enter(info, where, hidden, cot, before, after, bias, st, ct, rate, parts, seq_count):
    rows, span, width = hidden.shape
    seg, modes, tokens = span // segs, rate.shape[0], rows * span
    body = (rows, seg, segs, width)
    return pl.pallas_call(
        lambda *refs: enter_kernel(rows, span, seq_count, len(parts), *refs),
        out_shape=(
            vm((tokens, width), bf16),
            vm((width, tokens), bf16),
            vm((tokens, width), bf16),
            vm((rows, seg + 4, segs, 3 * width)),
            vm(body),
            vm(body),
            vm(body),
            vm((rows, modes, segs, width)),
            vm((rows, modes, width)),
        ),
        in_specs=smem_spec() * 2 + vmem_specs(8) + hbm_specs(len(parts)),
        out_specs=tuple(vmem_specs(9)),
        scratch_shapes=[
            pltpu.VMEM((tokens, 128), f32),
            pltpu.VMEM((16, 3 * width), f32),
            pltpu.VMEM((16, width), f32),
            pltpu.VMEM((width, 3 * width), bf16),
            pltpu.SemaphoreType.DMA((len(parts),)),
        ],
        compiler_params=pltpu.CompilerParams(vmem_limit_bytes=vmem_cap),
        cost_estimate=spent(1),
        name="mixer_enter",
    )(info, where, hidden, cot, before, after, bias, st, ct, rate, *parts)


def carry_in(parts, fade_span):
    total = parts[0]
    scale = fade_span
    for p in parts[1:]:
        total = total + scale * p
        scale = scale * fade_span
    return total


def settle_kernel(rows, span, others, count, info, where, *refs):
    gath, refs = refs[:others], refs[others:]
    parts, refs = refs[:count], refs[count:]
    ends, q, keys, vals, rate, res, xp, vecs, long_out, gated_t, carry_out, n1, s1, low, low_t, gsc, wo, sems = refs
    ob, gain, shift = (vecs.at[pl.ds(k, 1)] for k in range(3))
    copies = fetch_parts(where, parts, wo, sems, parts[0].shape[1] - wo.shape[1])
    start_all(copies)
    seg = span // segs
    width = q.shape[3]
    modes = rate.shape[0]
    base = info[2 * rows] * span
    sub = iota((segs, lane_block), 0)
    for r in range(rows):
        factor = factor_of(info, rows, r)
        for t in range(width // lane_block):
            c = pl.ds(t * lane_block, lane_block)
            fade, mix, start = [], [], []
            for m in range(modes):
                d = rate[pl.ds(m, 1), c] * factor
                fade.append(jnp.exp(-d))
                mix.append(res[pl.ds(m, 1), c] * jnp.sqrt(1.0 - jnp.exp(-2.0 * d)))
                far = jnp.exp(-d * seg)
                cur = carry_in([g[r, pl.ds(m, 1), c] for g in gath], jnp.exp(-d * span))
                tile = jnp.zeros((segs, lane_block), f32)
                end = ends[r, m, :, c]
                for i in range(segs):
                    tile = jnp.where(sub == i, cur, tile)
                    cur = far * cur + end[i : i + 1]
                carry_out[r, m, :, c] = tile
                start.append(tile)

            def step(j, states):
                live = (base + sub * seg + j < info[r]).astype(f32)
                src = keys[r, j, :, c] * vals[r, j, :, c] * live
                states = tuple(f * h + src for f, h in zip(fade, states))
                out = mix[0] * states[0]
                for m in range(1, modes):
                    out = out + mix[m] * states[m]
                long_out[r, j, :, c] = out
                gsc[r, j, :, c] = q[r, j, :, c] * out * live
                return states

            lax.fori_loop(0, seg, step, tuple(start), unroll=4)
    wait_all(copies)
    for r in range(rows):
        tok = pl.ds(r * span, span)
        cut = gsc[r].reshape(span, width).astype(bf16)
        gated_t[:, tok] = cut.T
        n1[tok, :] = xp[tok, :].astype(f32) + jnp.dot(cut, wo[...], preferred_element_type=f32) + ob[...]

    @pl.loop(0, rows * span // 16, unroll=4)
    def _(k):
        tok = pl.ds(pl.multiple_of(k * 16, 16), 16)
        v = n1[tok, :]
        centre = v - jnp.mean(v, axis=-1, keepdims=True)
        inv = lax.rsqrt(jnp.mean(centre * centre, axis=-1, keepdims=True) + norm_eps)
        n = centre * inv
        n1[tok, :] = n
        s1[tok, :] = jnp.broadcast_to(inv, (16, 128))
        low[tok, :] = (n * gain[...] + shift[...]).astype(bf16)

    low_t[...] = low[...].T


def mixer_settle(info, where, gath, ends, q, keys, vals, rate, res, xp, vecs, parts):
    rows, seg, _, width = q.shape
    span = seg * segs
    tokens, modes = rows * span, rate.shape[0]
    return pl.pallas_call(
        lambda *refs: settle_kernel(rows, span, len(gath), len(parts), *refs),
        out_shape=(
            vm(q.shape),
            vm((width, tokens), bf16),
            vm(ends.shape),
            vm((tokens, width)),
            vm((tokens, 128)),
            vm((tokens, width), bf16),
            vm((width, tokens), bf16),
        ),
        in_specs=smem_spec() * 2 + vmem_specs(len(gath)) + hbm_specs(len(parts)) + vmem_specs(8),
        out_specs=tuple(vmem_specs(7)),
        scratch_shapes=[
            pltpu.VMEM(q.shape, f32),
            pltpu.VMEM((width, width), bf16),
            pltpu.SemaphoreType.DMA((len(parts),)),
        ],
        compiler_params=pltpu.CompilerParams(vmem_limit_bytes=vmem_cap),
        cost_estimate=spent(1),
        name="mixer_settle",
    )(info, where, *gath, *parts, ends, q, keys, vals, rate, res, xp, vecs)


def row_mean(v):
    return jnp.mean(v, axis=-1, keepdims=True)


def fold(v):
    return v[:8] + v[8:]


def contract_last(a, b):
    return lax.dot_general(a, b, (((1,), (1,)), ((), ())), preferred_element_type=f32)


hidden_tile = 512


def core_kernel(rows, span, count, outs, info, where, slots, *refs):
    w_parts, o_parts, refs = refs[:count], refs[count : 2 * count], refs[2 * count :]
    if outs == 1:
        d_parts, refs = refs[:1], refs[1:]
    low_h, low_th, gated_th, n1_h, s1_h, cp_h, q_h, vecs, rate, layer = refs[:10]
    refs = refs[10:]
    gain1, shift1, bias, gain2, shift2 = (vecs.at[pl.ds(k, 1)] for k in range(1, 6))
    down_out, first_out, second_out, refs = refs[:outs], refs[outs : 2 * outs], refs[2 * outs : 3 * outs], refs[3 * outs :]
    pre1_h, gg_h, ends, dev_end, sums_two, sums_one, w, wd, wo, act, pull, gel, low, low_t, gated_t = refs[:15]
    n1, s1, cp, q, acc, first, feed, out_low, mix, gs, us, dd, dwg, dwu, dwo = refs[15:30]
    in_sems, w_sems, d_sems, o_sems, dd_sems, dw_sems, end_sems = refs[30:]
    hidden, width = wd.shape
    tile, seg, modes = hidden_tile, span // segs, rate.shape[0]
    tiles, tokens = hidden // tile, rows * span
    base = info[2 * rows] * span

    def bring(k, src, dst):
        return pltpu.make_async_copy(src, dst, in_sems.at[k])

    w_in = [
        [
            copy
            for k, at in enumerate((t * tile, hidden + t * tile))
            for copy in fetch_parts(where, w_parts, w, w_sems.at[k, t], at, pl.ds(at, tile))
        ]
        for t in range(tiles)
    ]
    if outs == 1:
        d_in = fetch_parts(where, d_parts, wd, d_sems.at[0])
    else:
        depth = w_parts[0].shape[0]
        d_in = [
            pltpu.make_async_copy(
                part.at[:, pl.ds(2 * hidden + j * width, width)],
                wd.at[pl.ds(pl.multiple_of(where[k] * (hidden // count) + j * depth, 8), depth)],
                d_sems.at[j, k],
            )
            for k, part in enumerate(w_parts)
            for j in range(hidden // count // depth)
        ]
    o_in = fetch_parts(where, o_parts, wo, o_sems, o_parts[0].shape[1] - width)
    low_in = bring(0, low_h, low)
    norm_in = [bring(1, n1_h, n1), bring(2, cp_h, cp)]
    late_in = [bring(3, low_th, low_t), bring(4, s1_h, s1), bring(5, q_h, q), bring(6, gated_th, gated_t)]
    start_all([low_in] + w_in[0] + w_in[1])
    low_in.wait()
    scale = 0.7978845608028654
    for t in range(tiles):
        if t + 2 < tiles:
            start_all(w_in[t + 2])
        if t == 1:
            start_all(d_in)
        if t == 3:
            start_all(norm_in)
        wait_all(w_in[t])
        cols, up_cols = pl.ds(t * tile, tile), pl.ds(hidden + t * tile, tile)
        gs[...] = jnp.dot(low[...], w[:, cols], preferred_element_type=f32)
        us[...] = jnp.dot(low[...], w[:, up_cols], preferred_element_type=f32)

        @pl.loop(0, tokens // 16, unroll=2)
        def _(k):
            tok = pl.ds(pl.multiple_of(k * 16, 16), 16)
            g, u = gs[tok, :], us[tok, :]
            sq = g * g
            th = jnp.tanh(g * (scale + (scale * 0.044715) * sq))
            side = 0.5 + 0.5 * th
            gelu = g * side
            slope = side + (0.5 * g) * (1.0 - th * th) * (scale + (3.0 * scale * 0.044715) * sq)
            act[tok, cols] = (gelu * u).astype(bf16)
            pull[tok, cols] = (u * slope).astype(bf16)
            gel[tok, cols] = gelu.astype(bf16)

    wait_all(d_in)
    start_all(late_in + o_in)
    for t in range(width // lane_block):
        c = pl.ds(t * lane_block, lane_block)
        acc[:, c] = jnp.dot(act[...], wd[:, c], preferred_element_type=f32)
    zero = jnp.zeros((8, width), f32)
    wait_all(norm_in)

    def outer_norm(k, loop):
        tok = pl.ds(pl.multiple_of(k * 16, 16), 16)
        n = iota((16, width), 0) + k * 16
        n = n & (span - 1)
        pos = base + (n & (segs - 1)) * seg + lax.shift_right_logical(n, 3)
        limit = jnp.where(k * 16 >= span, info[1], info[0])
        keep = (pos < limit).astype(f32)
        v = n1[tok, :] * gain1[...] + shift1[...] + acc[tok, :] + bias[...]
        centre = v - row_mean(v)
        inv = lax.rsqrt(row_mean(centre * centre) + norm_eps)
        n2 = centre * inv
        out_low[tok, :] = ((n2 * gain2[...] + shift2[...]) * keep).astype(bf16)
        top = cp[tok, :].astype(f32) * keep
        e = top * gain2[...]
        grad = inv * (e - row_mean(e) - n2 * row_mean(e * n2))
        first[tok, :] = grad
        cut = grad.astype(bf16)
        feed[tok, :] = cut
        return (
            loop[0] + fold(cut.astype(f32)),
            loop[1] + fold(top * n2),
            loop[2] + fold(top),
        )

    totals = lax.fori_loop(0, tokens // 16, outer_norm, (zero, zero, zero), unroll=4)
    for k in range(3):
        sums_two[pl.ds(k, 1), :] = jnp.sum(totals[k], axis=0, keepdims=True)

    blocks = 8
    span_d = hidden // blocks
    d_sends = []
    for k in range(blocks):
        if k >= 4:
            d_sends[k - 4].wait()
        which = k if outs == 1 else slots[k]
        c = pl.ds(pl.multiple_of(which * span_d, 128), span_d)
        dd[k % 4] = jnp.dot(act[:, c].T, feed[...], preferred_element_type=f32).astype(bf16)
        per = down_out[0].shape[0]
        dst = down_out[0].at[0, pl.ds(k * span_d, span_d)] if outs == 1 else down_out[k // per].at[k % per]
        d_sends.append(pltpu.make_async_copy(dd.at[k % 4], dst, dd_sems.at[k]))
        d_sends[k].start()
    o, n = iota((span, span), 0), iota((span, span), 1)
    back = (o == (n & (segs - 1)) * seg + lax.shift_right_logical(n, 3)).astype(f32).astype(bf16)
    for r in range(rows):
        layer[r] = jnp.dot(back, out_low[pl.ds(r * span, span), :], preferred_element_type=f32).astype(bf16)
    wait_all(late_in)
    sends = []
    half_tiles = tiles // 2
    for t in range(tiles):
        cols, up_cols = pl.ds(t * tile, tile), pl.ds(hidden + t * tile, tile)
        grad = contract_last(feed[...], wd[cols, :])
        g = (grad * pull[:, cols].astype(f32)).astype(bf16)
        u = (grad * gel[:, cols].astype(f32)).astype(bf16)
        if t >= 2:
            wait_all(sends[t - 2])
        dwg[t % 2] = jnp.dot(low_t[...], g, preferred_element_type=f32).astype(bf16)
        dwu[t % 2] = jnp.dot(low_t[...], u, preferred_element_type=f32).astype(bf16)
        into, at, own = (first_out, 0, t) if t < half_tiles else (second_out, width, t - half_tiles)
        g_at, u_at = at + own * tile, at + (half_tiles + own) * tile
        sends.append(
            send_parts(slots, dwg.at[t % 2], into, dw_sems.at[0, t], None, pl.ds(g_at, tile))
            + send_parts(slots, dwu.at[t % 2], into, dw_sems.at[1, t], None, pl.ds(u_at, tile))
        )
        start_all(sends[t])
        first[...] += contract_last(g, w[:, cols]) + contract_last(u, w[:, up_cols])

    def put(k, src, dst):
        return pltpu.make_async_copy(src, dst, end_sems.at[k])

    def inner_norm(k, loop):
        tok = pl.ds(pl.multiple_of(k * 16, 16), 16)
        top, n = first[tok, :], n1[tok, :]
        e = top * gain1[...]
        grad = s1[tok, 0:1] * (e - row_mean(e) - n * row_mean(e * n))
        acc[tok, :] = grad
        cut = grad.astype(bf16)
        mix[tok, :] = cut
        return (
            loop[0] + fold(cut.astype(f32)),
            loop[1] + fold(top * n),
            loop[2] + fold(top),
        )

    totals = lax.fori_loop(0, tokens // 16, inner_norm, (zero, zero, zero), unroll=4)
    finals = [put(0, acc, pre1_h)]
    finals[0].start()
    for k in range(3):
        sums_one[pl.ds(k, 1), :] = jnp.sum(totals[k], axis=0, keepdims=True)
    dwo[...] = jnp.dot(gated_t[...], mix[...], preferred_element_type=f32).astype(bf16)
    o_sends = send_parts(slots, dwo, second_out, dw_sems.at[2, 0], None, pl.ds(0, width))
    start_all(o_sends)
    wait_all(o_in)
    for t in range(width // lane_block):
        c = pl.ds(t * lane_block, lane_block)
        first[:, c] = contract_last(mix[...], wo[c, :])
    sub = iota((segs, lane_block), 0)
    for r in range(rows):
        factor = factor_of(info, rows, r)
        for t in range(width // lane_block):
            c = pl.ds(t * lane_block, lane_block)
            fade = [jnp.exp(-rate[pl.ds(m, 1), c] * factor) for m in range(modes)]
            far = [jnp.exp(-rate[pl.ds(m, 1), c] * (factor * seg)) for m in range(modes)]

            def step(k, states):
                j = seg - 1 - k
                live = (base + sub * seg + j < info[r]).astype(f32)
                tok = pl.ds(pl.multiple_of(r * span + j * segs, segs), segs)
                grad = first[tok, c] * live
                first[tok, c] = grad
                g = grad * q[r, j, :, c]
                return tuple(f * h + g for f, h in zip(fade, states))

            blank = jnp.zeros((segs, lane_block), f32)
            states = lax.fori_loop(0, seg, step, (blank,) * modes, unroll=4)
            for m in range(modes):
                ends[r, m, :, c] = states[m]
                total = jnp.zeros((1, lane_block), f32)
                for i in reversed(range(segs)):
                    total = far[m] * total + states[m][i : i + 1]
                dev_end[r, pl.ds(m, 1), c] = total
    finals.append(put(1, first, gg_h))
    finals[1].start()
    for copies in [d_sends[-4:]] + sends[-2:] + [o_sends, finals]:
        wait_all(copies)


def feed_core(
    info, where, slots, w_parts, d_parts, o_parts, low, low_t, gated_t, n1, s1, cp, q, vecs, rate, down_shapes, first_shapes, second_shapes,
):
    tokens, width = n1.shape
    rows, seg = q.shape[:2]
    modes, count, outs = rate.shape[0], len(w_parts), len(first_shapes)
    hidden, tile, pieces = down_shapes[0][0] * outs * down_shapes[0][1], hidden_tile, first_shapes[0][0] * outs
    shapes = tuple(down_shapes) + tuple(first_shapes) + tuple(second_shapes)
    return pl.pallas_call(
        lambda *refs: core_kernel(rows, seg * segs, count, outs, *refs),
        out_shape=(vm((rows, seg * segs, width), bf16),)
        + tuple(vm(s, bf16) for s in shapes)
        + (
            vm((tokens, width)),
            vm((tokens, width)),
            vm((rows, modes, segs, width)),
            vm((rows, modes, width)),
            vm((8, width)),
            vm((8, width)),
        ),
        in_specs=smem_spec() * 3 + hbm_specs(2 * count + len(d_parts) + 7) + vmem_specs(2),
        out_specs=tuple(vmem_specs(1) + hbm_specs(3 * outs + 2) + vmem_specs(4)),
        scratch_shapes=[
            pltpu.VMEM((width, 2 * hidden), bf16),
            pltpu.VMEM((hidden, width), bf16),
            pltpu.VMEM((width, width), bf16),
            pltpu.VMEM((tokens, hidden), bf16),
            pltpu.VMEM((tokens, hidden), bf16),
            pltpu.VMEM((tokens, hidden), bf16),
            pltpu.VMEM((tokens, width), bf16),
            pltpu.VMEM((width, tokens), bf16),
            pltpu.VMEM((width, tokens), bf16),
            pltpu.VMEM((tokens, width), f32),
            pltpu.VMEM((tokens, 128), f32),
            pltpu.VMEM((tokens, width), bf16),
            pltpu.VMEM(q.shape, f32),
            pltpu.VMEM((tokens, width), f32),
            pltpu.VMEM((tokens, width), f32),
            pltpu.VMEM((tokens, width), bf16),
            pltpu.VMEM((tokens, width), bf16),
            pltpu.VMEM((tokens, width), bf16),
            pltpu.VMEM((tokens, tile), f32),
            pltpu.VMEM((tokens, tile), f32),
            pltpu.VMEM((4, hidden // 8, width), bf16),
            pltpu.VMEM((2, width, tile), bf16),
            pltpu.VMEM((2, width, tile), bf16),
            pltpu.VMEM((width, width), bf16),
            pltpu.SemaphoreType.DMA((7,)),
            pltpu.SemaphoreType.DMA((2, hidden // tile, count)),
            pltpu.SemaphoreType.DMA((hidden // width, count)),
            pltpu.SemaphoreType.DMA((count,)),
            pltpu.SemaphoreType.DMA((8,)),
            pltpu.SemaphoreType.DMA((3, hidden // tile, pieces)),
            pltpu.SemaphoreType.DMA((2,)),
        ],
        compiler_params=pltpu.CompilerParams(vmem_limit_bytes=vmem_cap),
        cost_estimate=spent(1),
        name="feed_core",
    )(
        info, where, slots, *w_parts, *o_parts, *d_parts, low, low_t, gated_t, n1, s1, cp, q, vecs, rate
    )


def split_rims(rows, seg, at, rim, low, high):
    for r in range(rows):
        for k in range(2):
            rim[pl.ds(2 * r + k, 1), :] = at(r, k, pl.ds(0, 1))
            rim[pl.ds(2 * (rows + r) + k, 1), :] = at(r, seg - 2 + k, pl.ds(segs - 1, 1))
    low[...] = rim[: 2 * rows].astype(bf16)
    high[...] = rim[2 * rows : 4 * rows].astype(bf16)


def source_kernel(rows, span, others, info, *refs):
    gath = refs[:others]
    ends, carry, rate, res, refs = *refs[others : others + 4], refs[others + 4 :]
    streams, refs = refs[:5], refs[5:]
    gm_h, rim_low, rim_high, gres, grate, gg, q, long_out, keys, vals, gm, hist, rim, in_sems, out_sems = refs
    seg = span // segs
    width, modes = q.shape[3], rate.shape[0]
    blocks = width // lane_block
    ins = [
        [
            pltpu.make_async_copy(
                src.at[:, :, :, pl.ds(t * lane_block, lane_block)],
                dst.at[:, :, :, pl.ds(t * lane_block, lane_block)],
                in_sems.at[t, k],
            )
            for k, (src, dst) in enumerate(zip(streams, (gg, q, long_out, keys, vals)))
        ]
        for t in range(blocks)
    ]
    sends = [
        [
            pltpu.make_async_copy(
                gm.at[:, :, :, pl.ds(b * width + t * lane_block, lane_block)],
                gm_h.at[:, pl.ds(2, seg), :, pl.ds(b * width + t * lane_block, lane_block)],
                out_sems.at[t, b],
            )
            for b in range(3)
        ]
        for t in range(blocks)
    ]
    for t in range(blocks):
        start_all(ins[t])
    base = info[2 * rows] * span
    sub = iota((segs, lane_block), 0)
    for t in range(blocks):
        wait_all(ins[t])
        c = pl.ds(t * lane_block, lane_block)
        sum_res = [jnp.zeros((1, lane_block), f32) for _ in range(modes)]
        sum_rate = [jnp.zeros((1, lane_block), f32) for _ in range(modes)]
        for r in range(rows):
            factor = factor_of(info, rows, r)
            fade, mix, start, root, ebb = [], [], [], [], []
            for m in range(modes):
                d = rate[pl.ds(m, 1), c] * factor
                fade.append(jnp.exp(-d))
                ebb.append(jnp.exp(-2.0 * d))
                root.append(jnp.sqrt(1.0 - ebb[m]))
                mix.append(res[pl.ds(m, 1), c] * root[m])
                far = jnp.exp(-d * seg)
                cur = carry_in([g[r, pl.ds(m, 1), c] for g in gath], jnp.exp(-d * span))
                tile = jnp.zeros((segs, lane_block), f32)
                end = ends[r, m, :, c]
                for i in reversed(range(segs)):
                    tile = jnp.where(sub == i, cur, tile)
                    cur = far * cur + end[i : i + 1]
                start.append(tile)

            def ahead(j, loop):
                states, sums = loop
                live = (base + sub * seg + j < info[r]).astype(f32)
                src = keys[r, j, :, c] * vals[r, j, :, c] * live
                g = gg[r, j, :, c] * q[r, j, :, c]
                past = tuple(f * h for f, h in zip(fade, states))
                for m in range(modes):
                    hist[m, j] = past[m]
                states = tuple(p + src for p in past)
                return (states, tuple(s + g * h for s, h in zip(sums, states)))

            zero = jnp.zeros((segs, lane_block), f32)
            init = tuple(carry[r, m, :, c] for m in range(modes))
            _, with_state = lax.fori_loop(0, seg, ahead, (init, (zero,) * modes), unroll=4)

            def behind(k, loop):
                states, sums = loop
                j = seg - 1 - k
                live = (base + sub * seg + j < info[r]).astype(f32)
                grad = gg[r, j, :, c]
                g = grad * q[r, j, :, c]
                states = tuple(f * h + g for f, h in zip(fade, states))
                gs = mix[0] * states[0]
                for m in range(1, modes):
                    gs = gs + mix[m] * states[m]
                gs = gs * live
                for b, part in enumerate(
                    (grad * long_out[r, j, :, c], gs * vals[r, j, :, c], gs * keys[r, j, :, c])
                ):
                    gm[r, j, :, pl.ds(b * width + t * lane_block, lane_block)] = part.astype(bf16).astype(f32)
                return (states, tuple(s + h * hist[m, j] for m, (s, h) in enumerate(zip(sums, states))))

            _, with_lag = lax.fori_loop(0, seg, behind, (tuple(start), (zero,) * modes), unroll=4)
            for m in range(modes):
                u = jnp.sum(with_state[m], axis=0, keepdims=True)
                v = jnp.sum(with_lag[m], axis=0, keepdims=True)
                sum_res[m] = sum_res[m] + root[m] * u
                sum_rate[m] = sum_rate[m] + factor * res[pl.ds(m, 1), c] * (ebb[m] / root[m] * u - root[m] * v)
        for m in range(modes):
            gres[pl.ds(m, 1), c] = sum_res[m]
            grate[pl.ds(m, 1), c] = sum_rate[m]
        start_all(sends[t])
    split_rims(rows, seg, lambda r, j, i: gm[r, j, i, :], rim, rim_low, rim_high)
    for t in range(blocks):
        wait_all(sends[t])


def mixer_source(info, gath, ends, carry, gg, q, long_out, keys, vals, rate, res):
    rows, seg, _, width = q.shape
    modes = rate.shape[0]
    return pl.pallas_call(
        lambda *refs: source_kernel(rows, seg * segs, len(gath), *refs),
        out_shape=(
            vm((rows, seg + 4, segs, 3 * width)),
            vm((2 * rows, 3 * width), bf16),
            vm((2 * rows, 3 * width), bf16),
            vm((modes, width)),
            vm((modes, width)),
        ),
        in_specs=smem_spec() + vmem_specs(4 + len(gath)) + hbm_specs(5),
        out_specs=tuple(hbm_specs(1) + vmem_specs(4)),
        scratch_shapes=[pltpu.VMEM(q.shape, f32)] * 5
        + [
            pltpu.VMEM((rows, seg, segs, 3 * width), f32),
            pltpu.VMEM((modes, seg, segs, lane_block), f32),
            pltpu.VMEM((4 * rows, 3 * width), f32),
            pltpu.SemaphoreType.DMA((width // lane_block, 5)),
            pltpu.SemaphoreType.DMA((width // lane_block, 3)),
        ],
        compiler_params=pltpu.CompilerParams(vmem_limit_bytes=vmem_cap),
        cost_estimate=spent(1),
        name="mixer_source",
    )(info, *gath, ends, carry, rate, res, gg, q, long_out, keys, vals)


def taps_blocks(rows, span, seq_count, info, gm, halo, ext, st, ct, gp, put, gsc, ready, done):
    seg = span // segs
    width = ct.shape[1]
    place = info[2 * rows]
    base = place * span
    sub = iota((segs, lane_block), 0)
    in_low = 1.0 - (place == 0).astype(f32) * (sub == 0).astype(f32)
    in_high = 1.0 - (place == seq_count - 1).astype(f32) * (sub == segs - 1).astype(f32)
    zero = jnp.zeros((segs, lane_block), f32)
    for block in range(3):
        for t in range(width // lane_block):
            ready(block * (width // lane_block) + t)
            for r in range(rows):
                fill_edges(gm, r, seg, halo, (block * width + t * lane_block, lane_block))
            c = pl.ds(block * width + t * lane_block, lane_block)
            lanes = pl.ds(t * lane_block, lane_block)
            sums = tuple(zero for _ in range(4))
            csums = tuple(zero for _ in range(3))
            for r in range(rows):

                def tap3(e):
                    return (
                        st[pl.ds(0, 1), c] * ext[r, e - 1, :, c]
                        + st[pl.ds(1, 1), c] * ext[r, e, :, c]
                        + st[pl.ds(2, 1), c] * ext[r, e + 1, :, c]
                    )

                def grad_at(e):
                    if block != 1:
                        return gm[r, e, :, c]
                    return (
                        ct[pl.ds(0, 1), lanes] * gm[r, e + 1, :, c]
                        + ct[pl.ds(1, 1), lanes] * gm[r, e, :, c]
                        + ct[pl.ds(2, 1), lanes] * gm[r, e - 1, :, c]
                    )

                def step(j, loop):
                    prev, cur, kp_prev, kp_cur, sums, csums = loop
                    nxt = grad_at(j + 3)
                    if block == 1:
                        nxt = jnp.where(j == seg - 1, nxt * in_high, nxt)
                        kp_next = tap3(j + 3)
                        kp_next = jnp.where(j == seg - 1, kp_next * in_high, kp_next)
                        own = gm[r, j + 2, :, c]
                        csums = tuple(s + own * k for s, k in zip(csums, (kp_prev, kp_cur, kp_next)))
                    else:
                        kp_next = kp_cur
                    live = (base + sub * seg + j < info[r]).astype(f32)
                    full = (
                        st[pl.ds(0, 1), c] * nxt + st[pl.ds(1, 1), c] * cur + st[pl.ds(2, 1), c] * prev
                    ) * live
                    full = full.astype(bf16).astype(f32)
                    gsc[r, j] = full
                    sums = (
                        sums[0] + cur * ext[r, j + 1, :, c],
                        sums[1] + cur * ext[r, j + 2, :, c],
                        sums[2] + cur * ext[r, j + 3, :, c],
                        sums[3] + full,
                    )
                    return (cur, nxt, kp_cur, kp_next, sums, csums)

                if block == 1:
                    start = (grad_at(1) * in_low, grad_at(2), tap3(1) * in_low, tap3(2), sums, csums)
                else:
                    start = (grad_at(1), grad_at(2), zero, zero, sums, csums)
                _, _, _, _, sums, csums = lax.fori_loop(0, seg, step, start, unroll=8)
                gp[pl.ds(r * span, span), c] = gsc[r].reshape(span, lane_block).astype(bf16)
            for k in range(3):
                put("short", k, block, lanes, jnp.sum(sums[k], axis=0, keepdims=True))
            put("bias", 0, block, lanes, jnp.sum(sums[3], axis=0, keepdims=True))
            if block == 1:
                for k in range(3):
                    put("cond", k, block, lanes, jnp.sum(csums[k], axis=0, keepdims=True))
        done(block)


row_bias, row_short, row_cond, row_res, row_rate, row_one, row_two, small_rows = 0, 3, 12, 15, 19, 23, 26, 32


def small_put(small):
    def put(kind, k, block, lanes, value):
        row = {"bias": row_bias + block, "short": row_short + 3 * k + block, "cond": row_cond + k}[kind]
        small[pl.ds(row, 1), lanes] = value

    return put


def taps_kernel(rows, span, seq_count, count, outs, info, where, slots, *refs):
    parts, refs = refs[:count], refs[count:]
    gm_h, ext_h, xpt_h, pre1_h, before, after, st, ct, gres, grate, sums_one, sums_two = refs[:12]
    hidden_grad, small = refs[12:14]
    dws, refs = refs[14 : 14 + outs], refs[14 + outs :]
    gsc, gm, ext, xpt, pre1, gp, halo, w, dw, low, stream_sems, in_sems, sems, out_sems = refs
    width = ct.shape[1]
    groups = 3 * width // lane_block
    streams = [
        [
            pltpu.make_async_copy(
                src.at[:, :, :, pl.ds(n * lane_block, lane_block)],
                dst.at[:, :, :, pl.ds(n * lane_block, lane_block)],
                stream_sems.at[k, n],
            )
            for k, (src, dst) in enumerate(((gm_h, gm), (ext_h, ext)))
        ]
        for n in range(groups)
    ]
    late = [pltpu.make_async_copy(xpt_h, xpt, in_sems.at[0]), pltpu.make_async_copy(pre1_h, pre1, in_sems.at[1])]
    copies = fetch_parts(where, parts, w, sems)
    start_all(streams[0] + streams[1])

    def ready(n):
        wait_all(streams[n])
        if n + 2 < groups:
            start_all(streams[n + 2])
        if n == 0:
            late[0].start()
        if n == groups // 2:
            start_all(copies + late[1:])

    small[...] = jnp.zeros_like(small)
    modes = gres.shape[0]
    small[pl.ds(row_res, modes), :] = gres[...]
    small[pl.ds(row_rate, modes), :] = grate[...]
    small[pl.ds(row_one, 3), :] = sums_one[pl.ds(0, 3), :]
    small[pl.ds(row_two, 3), :] = sums_two[pl.ds(0, 3), :]
    join_rims(rows, before, after, halo)
    sends = []

    def done(block):
        c = pl.ds(block * width, width)
        if block == 0:
            late[0].wait()
        dw[:, c] = jnp.dot(xpt[...], gp[:, c], preferred_element_type=f32).astype(bf16)
        sends.extend(send_parts(slots, dw, dws, out_sems.at[block], c))
        start_all(sends[-outs * dws[0].shape[0] :])

    taps_blocks(
        rows, span, seq_count, info, gm, halo, ext, st, ct, gp, small_put(small), gsc,
        ready, done,
    )
    wait_all(copies + late[1:])
    low[...] = (contract_last(gp[...], w[...]) + pre1[...]).astype(bf16)
    o, n = iota((span, span), 0), iota((span, span), 1)
    seg = span // segs
    back = (o == (n & (segs - 1)) * seg + lax.shift_right_logical(n, 3)).astype(f32).astype(bf16)
    for r in range(rows):
        moved = jnp.dot(back, low[pl.ds(r * span, span), :], preferred_element_type=f32)
        hidden_grad[r] = moved.astype(bf16)
    wait_all(sends)


def mixer_taps(
    info, where, slots, gm, parts, before, after, ext, st, ct, xpt, pre1, gres, grate, sums_one, sums_two,
    seq_count, dw_shapes,
):
    rows, padded, _, wide = ext.shape
    seg, width = padded - 4, wide // 3
    tokens = rows * seg * segs
    count, outs = len(parts), len(dw_shapes)
    return pl.pallas_call(
        lambda *refs: taps_kernel(rows, seg * segs, seq_count, count, outs, *refs),
        out_shape=(vm((rows, seg * segs, width), bf16), vm((small_rows, width)))
        + tuple(vm(s, bf16) for s in dw_shapes),
        in_specs=smem_spec() * 3 + hbm_specs(count + 4) + vmem_specs(8),
        out_specs=tuple(vmem_specs(2)) + tuple(any_specs(outs)),
        scratch_shapes=[
            pltpu.VMEM((rows, seg, segs, lane_block), f32),
            pltpu.VMEM(gm.shape, f32),
            pltpu.VMEM(ext.shape, f32),
            pltpu.VMEM(xpt.shape, bf16),
            pltpu.VMEM(pre1.shape, f32),
            pltpu.VMEM((tokens, wide), bf16),
            pltpu.VMEM((16, wide), f32),
            pltpu.VMEM((width, wide), bf16),
            pltpu.VMEM((width, wide), bf16),
            pltpu.VMEM((tokens, width), bf16),
            pltpu.SemaphoreType.DMA((2, wide // lane_block)),
            pltpu.SemaphoreType.DMA((2,)),
            pltpu.SemaphoreType.DMA((count,)),
            pltpu.SemaphoreType.DMA((3, outs * dw_shapes[0][0])),
        ],
        compiler_params=pltpu.CompilerParams(vmem_limit_bytes=vmem_cap),
        cost_estimate=spent(1),
        name="mixer_taps",
    )(
        info, where, slots, *parts, gm, ext, xpt, pre1, before, after, st, ct, gres, grate, sums_one, sums_two
    )


def chip_pairs(count):
    first = [(d, d ^ (2 if d % 2 == 0 else 4)) for d in range(count)]
    second = [(d, d ^ (4 if d % 2 == 0 else 2)) for d in range(count)]
    core = [(d, d ^ 1) for d in range(count)]
    return core, first, second


def tie(value, *needs):
    return lax.optimization_barrier((value, needs))[0]


def cross(block, pairs):
    return lax.ppermute(block, "dp", pairs)


def shard_order(me):
    even = (me & 1) == 0
    f = jnp.where(even, 2, 4)
    g = jnp.where(even, 4, 2)
    near = [me, me ^ f, me ^ g, me ^ 6]
    far = [me ^ 1, me ^ 1 ^ g, me ^ 1 ^ f, me ^ 7]
    return jnp.stack(near + far).astype(jnp.int32)


def slot_order(me):
    even = (me & 1) == 0
    f = jnp.where(even, 2, 4)
    g = jnp.where(even, 4, 2)
    mine = [me, me ^ g, me ^ f, me ^ 6]
    theirs = [me ^ 1, me ^ 1 ^ f, me ^ 1 ^ g, me ^ 7]
    return jnp.stack(mine + theirs).astype(jnp.int32)


class Gather:
    def __init__(self, shard, name):
        self.shard, self.name = shard, name
        self.core, self.first, self.second = chip_pairs(8)

    def one(self, *needs):
        with jax.named_scope(self.name + "_one"):
            self.p1 = cross(tie(self.shard, *needs), self.first)
        return self.p1

    def two(self, *needs):
        with jax.named_scope(self.name + "_two"):
            self.p2 = cross(tie(self.shard, *needs), self.second)
        return self.p2

    def three(self, *needs):
        with jax.named_scope(self.name + "_three"):
            self.p3 = cross(tie(self.p1, *needs), self.second)
        return self.p3

    def share(self, early=(), late=()):
        near = [self.shard, self.p1, self.p2, self.p3]
        with jax.named_scope(self.name + "_core"):
            sent = [tie(p, *early) for p in near[:3]] + [tie(near[3], *late)]
            self.parts = near + [cross(p, self.core) for p in sent]
        return self.parts


class Scatter:
    steps = 6

    def __init__(self, mine, theirs, name):
        self.mine, self.theirs, self.name, self.at = mine, theirs, name, 0
        self.core, self.first, self.second = chip_pairs(8)
        self.odd = lax.axis_index("seq") & 1
        self.near = [(i, i ^ 1) for i in range(4)]

    def step(self, *needs):
        self.at += 1
        with jax.named_scope(f"{self.name}_s{self.at}"):
            return getattr(self, f"step{self.at}")(needs)

    def step1(self, needs):
        self.sent = tie(self.theirs, *needs)
        self.got = cross(self.sent, self.core)
        return self.got

    def step2(self, needs):
        got = tie(self.got, *needs)
        self.sent = (self.mine[2:].astype(f32) + got[2:].astype(f32)).astype(bf16)
        self.got1 = cross(self.sent, self.first)
        return self.got1

    def step3(self, needs):
        got1 = tie(self.got1, *needs)
        send = self.mine[1].astype(f32) + self.got[1].astype(f32) + got1[1].astype(f32)
        self.sent = send.astype(bf16)
        self.got2 = cross(self.sent, self.second)
        return self.got2

    def own_half(self, got2, high):
        depth, wide = got2.shape[0] // 2, got2.shape[1]

        def cut(block):
            if block.ndim == 2:
                return lax.dynamic_slice(block, (high * depth, 0), (depth, wide)).astype(f32)
            return lax.dynamic_slice(block, (0, high * depth, 0), (1, depth, wide))[0].astype(f32)

        return cut(self.mine) + cut(self.got) + cut(self.got1) + cut(got2)

    def step4(self, needs):
        self.sent = self.own_half(tie(self.got2, *needs), 1 - self.odd).astype(bf16)
        self.h1 = lax.ppermute(self.sent, "seq", self.near)
        return self.h1

    def step5(self, needs):
        part = self.own_half(self.got2, self.odd) + tie(self.h1, *needs).astype(f32)
        self.part = self.sent = part.astype(bf16)
        self.h2 = lax.ppermute(self.part, "seq", [(i, i ^ 2) for i in range(4)])
        return self.h2

    def step6(self, needs):
        self.total = (self.part.astype(f32) + tie(self.h2, *needs).astype(f32)).astype(bf16)
        self.sent = self.total
        self.h3 = lax.ppermute(self.total, "seq", self.near)
        return self.h3

    def result(self):
        odd = self.odd == 1
        low = jnp.where(odd, self.h3, self.total)
        return jnp.concatenate([low, jnp.where(odd, self.total, self.h3)]).astype(f32)


class Total:
    steps = 5

    def __init__(self, flat, name):
        self.flat, self.name, self.at = flat, name, 0

    def step(self, *needs):
        axis, count, bit = (("dp", 8, 1), ("dp", 8, 2), ("dp", 8, 4), ("seq", 4, 1), ("seq", 4, 2))[self.at]
        self.at += 1
        with jax.named_scope(f"{self.name}_s{self.at}"):
            flat = self.sent = tie(self.flat, *needs)
            got = lax.ppermute(flat, axis, [(d, d ^ bit) for d in range(count)])
            self.flat = flat + got
        return got

    def result(self):
        return self.flat


def advance(last, *flows):
    for f in flows:
        f.step(last)
        last = f.sent
    return last


def local(
    hidden_in,
    seq_len,
    bucket,
    in_weight,
    in_bias,
    short_taps,
    cond_taps,
    mode_residue,
    mode_rate,
    out_weight,
    out_bias,
    norm1_gain,
    norm1_bias,
    gate_weight,
    up_weight,
    down_weight,
    down_bias,
    norm2_gain,
    norm2_bias,
    out_cotangent,
):
    rows, span, width = hidden_in.shape
    tokens, seg = rows * span, span // segs
    dp_count, seq_count = lax.axis_size("dp"), lax.axis_size("seq")
    me, place = lax.axis_index("dp"), lax.axis_index("seq")
    info = jnp.concatenate([seq_len, bucket, place[None]]).astype(jnp.int32)
    chips = dp_count == 8 and seq_count == 4
    up_line = [(i, i + 1) for i in range(seq_count - 1)]
    down_line = [(i + 1, i) for i in range(seq_count - 1)]

    def rims(low, high):
        return lax.ppermute(high, "seq", up_line), lax.ppermute(low, "seq", down_line)

    def dw_shapes(depth, wide):
        return ((4, depth, wide),) * 2 if chips else ((1, depth * dp_count, wide),)

    line_in = in_bias[None]
    vecs = jnp.stack([out_bias, norm1_gain, norm1_bias, down_bias, norm2_gain, norm2_bias])

    def states_of(block, sign):
        return [
            lax.ppermute(block, "seq", [(i, i + sign * k) for i in range(seq_count) if 0 <= i + sign * k < seq_count])
            for k in range(1, seq_count)
        ]

    hidden = gate_weight.shape[1]
    depth = gate_weight.shape[0]
    half = hidden // 2
    before, after = rims(
        hidden_in[:, :2].reshape(2 * rows, width), hidden_in[:, span - 2 :].reshape(2 * rows, width)
    )
    shard_io = jnp.concatenate([in_weight, out_weight], axis=1)
    d_parts = ()
    if chips:
        downs = [down_weight[k * depth : (k + 1) * depth] for k in range(hidden // width)]
        shard_f = jnp.concatenate([gate_weight, up_weight, *downs], axis=1)
        w_io, w_f = Gather(shard_io, "w_in_out"), Gather(shard_f, "w_feed_down")
        w_io.one()
        w_io.two()
        w_io.three(w_io.p2, before, after, shard_f, info)
        io_parts = w_io.share((w_io.p1,))
        w_f.one(w_io.p3)
        w_f.two(w_io.p3)
    else:
        shard_f = jnp.concatenate([gate_weight, up_weight], axis=1)
        io_parts, f_parts, d_parts = (
            [lax.all_gather(shard, "dp", axis=0, tiled=True)] for shard in (shard_io, shard_f, down_weight)
        )
    one = jnp.zeros((1,), jnp.int32)
    where = shard_order(me) if chips else one
    slots = slot_order(me) if chips else one

    xp, xpt, cp, ext, q, keys, vals, ends, dev_end = mixer_enter(
        info, where, hidden_in, out_cotangent, before, after, line_in, short_taps, cond_taps, mode_rate,
        io_parts, seq_count,
    )
    gath = states_of(dev_end, 1)
    if chips:
        w_f.three(gath, w_f.p2, vecs)
    long_out, gated_t, carry, n1, s1, low, low_t = mixer_settle(
        info, where, gath, ends, q, keys, vals, mode_rate, mode_residue, xp,
        vecs, io_parts,
    )
    if chips:
        f_parts = w_f.share((gath,), (low,))
    layer_out, *grads, pre1, gg, back_ends, back_dev, sums_two, sums_one = feed_core(
        info, where, slots, f_parts, d_parts, io_parts, low, low_t, gated_t, n1, s1, cp, q, vecs, mode_rate,
        dw_shapes(*down_weight.shape), dw_shapes(depth, hidden), dw_shapes(depth, width + hidden),
    )
    gg = gg.reshape(q.shape)
    back_gath = states_of(back_dev, -1)
    wait = ()
    if chips:
        s_d, s_a, s_b = (
            Scatter(*grads[2 * k : 2 * k + 2], name) for k, name in enumerate(("g_down", "g_feed", "g_out_feed"))
        )
        s_d.step()
        s_a.step(back_gath)
        s_b.step(back_gath)
        wait = advance(back_gath[0], s_d)
    gm, rim_low, rim_high, g_res, g_rate = mixer_source(
        tie(info, wait), back_gath, back_ends, carry, gg, q, long_out, keys, vals, mode_rate, mode_residue
    )
    before, after = rims(rim_low, rim_high)
    if chips:
        wait = advance(rim_low, s_d, s_a)
    grad_hidden, small, *g_in = mixer_taps(
        tie(info, wait), where, slots, gm, io_parts, before, after, ext, short_taps, cond_taps,
        xpt, pre1, g_res, g_rate, sums_one, sums_two, seq_count, dw_shapes(depth, 3 * width),
    )

    if chips:
        s_in = Scatter(*g_in, "g_in")
        s_small = Total(small, "g_small")
        s_in.step()
        order = (
            s_b, s_d, s_a, s_in, s_d, s_d, s_a, s_b, s_in, s_small, s_a, s_b, s_small, s_in, s_a, s_small, s_b,
            s_in, s_small, s_b, s_small, s_in,
        )
        advance(small, *order)
        flow = (s_in, s_small, s_d, s_a, s_b)
        share_in, small, share_down, share_a, share_b = (f.result() for f in flow)
    else:

        def share(grad):
            own = lax.psum_scatter(grad[0], "dp", scatter_dimension=0, tiled=True)
            return lax.psum(own, "seq").astype(f32)

        share_in, share_down, share_a, share_b = map(share, (*g_in, *grads))
        small = lax.psum(small, ("dp", "seq"))
    share_out = share_b[:, :width]
    share_gate = jnp.concatenate([share_a[:, :half], share_b[:, width : width + half]], axis=1)
    share_up = jnp.concatenate([share_a[:, half:], share_b[:, width + half :]], axis=1)
    modes = mode_rate.shape[0]
    return (
        layer_out, grad_hidden, share_in,
        small[row_bias : row_bias + 3].reshape(3 * width),
        small[row_short : row_short + 9].reshape(3, 3 * width),
        small[row_cond : row_cond + 3],
        small[row_res : row_res + modes],
        small[row_rate : row_rate + modes],
        share_out, small[row_one], small[row_one + 1], small[row_one + 2],
        share_gate, share_up, share_down, small[row_two], small[row_two + 1], small[row_two + 2],
    )


def solution(mesh):
    split, weight, full = P("dp", "seq", None), P("dp", None), P()
    in_specs = (
        split, P("dp"), P("dp"), weight, full, full, full, full, full, weight,
        full, full, full, weight, weight, weight, full, full, full, split,
    )
    out_specs = (
        split, split, weight, full, full, full, full, full, weight, full,
        full, full, weight, weight, weight, full, full, full,
    )
    return jax.shard_map(local, mesh=mesh, in_specs=in_specs, out_specs=out_specs, check_vma=False)
```

```python
import jax
import jax.numpy as jnp
from jax import lax
from jax.experimental import pallas as pl
from jax.experimental.pallas import tpu as pltpu
from jax.sharding import PartitionSpec as P

norm_eps = 1e-05
f32 = jnp.float32
bf16 = jnp.bfloat16
segs = 8
lane_block = 256
vmem_cap = 60 * 1024 * 1024


def iota(shape, dim):
    return lax.broadcasted_iota(jnp.int32, shape, dim)


def factor_of(info, rows, r):
    b = info[rows + r]
    return jnp.where(b == 0, 4.0, jnp.where(b == 1, 2.0, 1.0)).astype(f32)


def order_matrix(span):
    seg = span // segs
    o, n = iota((span, span), 0), iota((span, span), 1)
    return (n == (o & (segs - 1)) * seg + lax.shift_right_logical(o, 3)).astype(f32).astype(bf16)


def fill_edges(ext, r, seg, halo, cols):
    n = cols[1]
    c = pl.ds(cols[0], n)
    sub = iota((segs, n), 0)
    for h, (dst, src, shift, edge) in enumerate(
        ((0, seg, 1, 0), (1, seg + 1, 1, 0), (seg + 2, 2, segs - 1, segs - 1), (seg + 3, 3, segs - 1, segs - 1))
    ):
        rolled = pltpu.roll(ext[r, src, :, c], shift, 0)
        ext[r, dst, :, c] = jnp.where(sub == edge, halo[pl.ds(4 * r + h, 1), c], rolled)


def fetch_parts(where, parts, full, sems, at=0, cols=None):
    depth, wide = parts[0].shape[0], full.shape[1] if cols is None else cols.size
    copies = []
    for k, part in enumerate(parts):
        src = part if part.shape[1] == wide else part.at[:, pl.ds(at, wide)]
        dst = full.at[pl.ds(pl.multiple_of(where[k] * depth, 8), depth)]
        if cols is not None:
            dst = full.at[pl.ds(pl.multiple_of(where[k] * depth, 8), depth), cols]
        copies.append(pltpu.make_async_copy(src, dst, sems.at[k]))
    return copies


def start_all(copies):
    for copy in copies:
        copy.start()


def wait_all(copies):
    for copy in copies:
        copy.wait()


def send_parts(where, full, outs, sems, cols=None, into=None):
    per, depth = outs[0].shape[0], outs[0].shape[1]
    copies = []
    for k in range(per * len(outs)):
        rows_of = pl.ds(pl.multiple_of(where[k] * depth, 8), depth)
        src, dst = full.at[rows_of], outs[k // per].at[k % per]
        if cols is not None:
            src, dst = full.at[rows_of, cols], outs[k // per].at[k % per, :, cols]
        if into is not None:
            dst = outs[k // per].at[k % per, :, into]
        copies.append(pltpu.make_async_copy(src, dst, sems.at[k]))
    return copies


def join_rims(rows, before, after, rim):
    rim[...] = jnp.zeros_like(rim)
    low, high = before[...].astype(f32), after[...].astype(f32)
    for r in range(rows):
        for k in range(2):
            rim[pl.ds(4 * r + k, 1), :] = low[2 * r + k : 2 * r + k + 1]
            rim[pl.ds(4 * r + 2 + k, 1), :] = high[2 * r + k : 2 * r + k + 1]


def enter_kernel(rows, span, seq_count, count, info, where, x, cot, before, after, bias, st, ct, rate, *refs):
    parts, refs = refs[:count], refs[count:]
    xp, xpt, cp, ext, q, keys, vals, ends, dev_end, mask, hal, xh, w, sems = refs
    copies = fetch_parts(where, parts, w, sems)
    start_all(copies)
    width = x.shape[2]
    seg = span // segs
    place = info[2 * rows]
    base = place * span
    order = order_matrix(span)
    for r in range(rows):
        moved = jnp.dot(order, x[r], preferred_element_type=f32).astype(bf16)
        xp[pl.ds(r * span, span), :] = moved
        xpt[:, pl.ds(r * span, span)] = moved.T
        cp[pl.ds(r * span, span), :] = jnp.dot(order, cot[r], preferred_element_type=f32).astype(bf16)
        n = iota((span, 128), 0)
        pos = base + (n & (segs - 1)) * seg + lax.shift_right_logical(n, 3)
        mask[pl.ds(r * span, span), :] = (pos < info[r]).astype(f32)
    join_rims(rows, before, after, xh)
    edge_rows = xh[...].astype(bf16)
    hn = iota((16, 128), 0)
    hk = hn & 3
    hpos = base + jnp.where(hk < 2, hk - 2, span + hk - 2)
    hlim = jnp.where(lax.shift_right_logical(hn, 2) == 0, info[0], info[1])
    hmask = ((hpos >= 0) & (hpos < hlim)).astype(f32)
    wait_all(copies)

    @pl.loop(0, 3 * width // lane_block)
    def _(t):
        cols = pl.ds(pl.multiple_of(t * lane_block, lane_block), lane_block)
        part = jnp.dot(xp[...], w[:, cols], preferred_element_type=f32) + bias[:, cols]
        rim = jnp.dot(edge_rows, w[:, cols], preferred_element_type=f32) + bias[:, cols]
        for s in range(lane_block // 128):
            sub = slice(s * 128, (s + 1) * 128)
            scol = pl.ds(pl.multiple_of(t * lane_block + s * 128, 128), 128)
            low = (part[:, sub] * mask[...]).astype(bf16).astype(f32)
            for r in range(rows):
                ext[r, pl.ds(2, seg), :, scol] = low[r * span : (r + 1) * span].reshape(seg, segs, 128)
            hal[:, scol] = (rim[:, sub] * hmask).astype(bf16).astype(f32)

    sub = iota((segs, lane_block), 0)
    first = (place == 0).astype(f32)
    last = (place == seq_count - 1).astype(f32)
    in_low = 1.0 - first * (sub == 0).astype(f32)
    in_high = 1.0 - last * (sub == segs - 1).astype(f32)
    for r in range(rows):
        factor = factor_of(info, rows, r)
        for t in range(3 * width // lane_block):
            fill_edges(ext, r, seg, hal, (t * lane_block, lane_block))
        for t in range(width // lane_block):
            cq = pl.ds(t * lane_block, lane_block)
            ck = pl.ds(width + t * lane_block, lane_block)
            cv = pl.ds(2 * width + t * lane_block, lane_block)
            modes = rate.shape[0]
            fade = [jnp.exp(-rate[pl.ds(m, 1), cq] * factor) for m in range(modes)]
            far = [jnp.exp(-rate[pl.ds(m, 1), cq] * (factor * seg)) for m in range(modes)]

            def tap3(cols, e):
                return (
                    st[pl.ds(0, 1), cols] * ext[r, e - 1, :, cols]
                    + st[pl.ds(1, 1), cols] * ext[r, e, :, cols]
                    + st[pl.ds(2, 1), cols] * ext[r, e + 1, :, cols]
                )

            def step(j, carry):
                kp_prev, kp_cur, states = carry
                kp_next = tap3(ck, j + 3)
                kp_next = jnp.where(j == seg - 1, kp_next * in_high, kp_next)
                key = (
                    ct[pl.ds(0, 1), cq] * kp_prev
                    + ct[pl.ds(1, 1), cq] * kp_cur
                    + ct[pl.ds(2, 1), cq] * kp_next
                )
                val = tap3(cv, j + 2)
                q[r, j, :, cq] = tap3(cq, j + 2)
                keys[r, j, :, cq] = key
                vals[r, j, :, cq] = val
                live = (base + sub * seg + j < info[r]).astype(f32)
                src = key * val * live
                return (kp_cur, kp_next, tuple(f * h + src for f, h in zip(fade, states)))

            zero = jnp.zeros((segs, lane_block), f32)
            start = (tap3(ck, 1) * in_low, tap3(ck, 2), (zero,) * modes)
            _, _, states = lax.fori_loop(0, seg, step, start, unroll=4)
            for m in range(modes):
                ends[r, m, :, cq] = states[m]
                total = jnp.zeros((1, lane_block), f32)
                for i in range(segs):
                    total = far[m] * total + states[m][i : i + 1]
                dev_end[r, pl.ds(m, 1), cq] = total


def vm(shape, dtype=f32):
    return jax.ShapeDtypeStruct(shape, dtype)


def vmem_specs(n):
    return [pl.BlockSpec(memory_space=pltpu.VMEM)] * n


def smem_spec():
    return [pl.BlockSpec(memory_space=pltpu.SMEM)]


def spent(us):
    return pl.CostEstimate(flops=int(us * 1.1e9), bytes_accessed=1_000_000, transcendentals=0)


def any_specs(n):
    return [pl.BlockSpec(memory_space=pl.ANY)] * n


def hbm_specs(n):
    return [pl.BlockSpec(memory_space=pltpu.HBM)] * n


def mixer_enter(info, where, hidden, cot, before, after, bias, st, ct, rate, parts, seq_count):
    rows, span, width = hidden.shape
    seg, modes, tokens = span // segs, rate.shape[0], rows * span
    body = (rows, seg, segs, width)
    return pl.pallas_call(
        lambda *refs: enter_kernel(rows, span, seq_count, len(parts), *refs),
        out_shape=(
            vm((tokens, width), bf16),
            vm((width, tokens), bf16),
            vm((tokens, width), bf16),
            vm((rows, seg + 4, segs, 3 * width)),
            vm(body),
            vm(body),
            vm(body),
            vm((rows, modes, segs, width)),
            vm((rows, modes, width)),
        ),
        in_specs=smem_spec() * 2 + vmem_specs(8) + hbm_specs(len(parts)),
        out_specs=tuple(vmem_specs(9)),
        scratch_shapes=[
            pltpu.VMEM((tokens, 128), f32),
            pltpu.VMEM((16, 3 * width), f32),
            pltpu.VMEM((16, width), f32),
            pltpu.VMEM((width, 3 * width), bf16),
            pltpu.SemaphoreType.DMA((len(parts),)),
        ],
        compiler_params=pltpu.CompilerParams(vmem_limit_bytes=vmem_cap),
        cost_estimate=spent(1),
        name="mixer_enter",
    )(info, where, hidden, cot, before, after, bias, st, ct, rate, *parts)


def carry_in(parts, fade_span):
    total = parts[0]
    scale = fade_span
    for p in parts[1:]:
        total = total + scale * p
        scale = scale * fade_span
    return total


def settle_kernel(rows, span, others, count, info, where, *refs):
    gath, refs = refs[:others], refs[others:]
    parts, refs = refs[:count], refs[count:]
    ends, q, keys, vals, rate, res, xp, vecs, long_out, gated_t, carry_out, n1, s1, low, low_t, gsc, wo, sems = refs
    ob, gain, shift = (vecs.at[pl.ds(k, 1)] for k in range(3))
    copies = fetch_parts(where, parts, wo, sems, parts[0].shape[1] - wo.shape[1])
    start_all(copies)
    seg = span // segs
    width = q.shape[3]
    modes = rate.shape[0]
    base = info[2 * rows] * span
    sub = iota((segs, lane_block), 0)
    for r in range(rows):
        factor = factor_of(info, rows, r)
        for t in range(width // lane_block):
            c = pl.ds(t * lane_block, lane_block)
            fade, mix, start = [], [], []
            for m in range(modes):
                d = rate[pl.ds(m, 1), c] * factor
                fade.append(jnp.exp(-d))
                mix.append(res[pl.ds(m, 1), c] * jnp.sqrt(1.0 - jnp.exp(-2.0 * d)))
                far = jnp.exp(-d * seg)
                cur = carry_in([g[r, pl.ds(m, 1), c] for g in gath], jnp.exp(-d * span))
                tile = jnp.zeros((segs, lane_block), f32)
                end = ends[r, m, :, c]
                for i in range(segs):
                    tile = jnp.where(sub == i, cur, tile)
                    cur = far * cur + end[i : i + 1]
                carry_out[r, m, :, c] = tile
                start.append(tile)

            def step(j, states):
                live = (base + sub * seg + j < info[r]).astype(f32)
                src = keys[r, j, :, c] * vals[r, j, :, c] * live
                states = tuple(f * h + src for f, h in zip(fade, states))
                out = mix[0] * states[0]
                for m in range(1, modes):
                    out = out + mix[m] * states[m]
                long_out[r, j, :, c] = out
                gsc[r, j, :, c] = q[r, j, :, c] * out * live
                return states

            lax.fori_loop(0, seg, step, tuple(start), unroll=4)
    wait_all(copies)
    for r in range(rows):
        tok = pl.ds(r * span, span)
        cut = gsc[r].reshape(span, width).astype(bf16)
        gated_t[:, tok] = cut.T
        n1[tok, :] = xp[tok, :].astype(f32) + jnp.dot(cut, wo[...], preferred_element_type=f32) + ob[...]

    @pl.loop(0, rows * span // 16, unroll=4)
    def _(k):
        tok = pl.ds(pl.multiple_of(k * 16, 16), 16)
        v = n1[tok, :]
        centre = v - jnp.mean(v, axis=-1, keepdims=True)
        inv = lax.rsqrt(jnp.mean(centre * centre, axis=-1, keepdims=True) + norm_eps)
        n = centre * inv
        n1[tok, :] = n
        s1[tok, :] = jnp.broadcast_to(inv, (16, 128))
        low[tok, :] = (n * gain[...] + shift[...]).astype(bf16)

    low_t[...] = low[...].T


def mixer_settle(info, where, gath, ends, q, keys, vals, rate, res, xp, vecs, parts):
    rows, seg, _, width = q.shape
    span = seg * segs
    tokens, modes = rows * span, rate.shape[0]
    return pl.pallas_call(
        lambda *refs: settle_kernel(rows, span, len(gath), len(parts), *refs),
        out_shape=(
            vm(q.shape),
            vm((width, tokens), bf16),
            vm(ends.shape),
            vm((tokens, width)),
            vm((tokens, 128)),
            vm((tokens, width), bf16),
            vm((width, tokens), bf16),
        ),
        in_specs=smem_spec() * 2 + vmem_specs(len(gath)) + hbm_specs(len(parts)) + vmem_specs(8),
        out_specs=tuple(vmem_specs(7)),
        scratch_shapes=[
            pltpu.VMEM(q.shape, f32),
            pltpu.VMEM((width, width), bf16),
            pltpu.SemaphoreType.DMA((len(parts),)),
        ],
        compiler_params=pltpu.CompilerParams(vmem_limit_bytes=vmem_cap),
        cost_estimate=spent(1),
        name="mixer_settle",
    )(info, where, *gath, *parts, ends, q, keys, vals, rate, res, xp, vecs)


def row_mean(v):
    return jnp.mean(v, axis=-1, keepdims=True)


def fold(v):
    return v[:8] + v[8:]


def contract_last(a, b):
    return lax.dot_general(a, b, (((1,), (1,)), ((), ())), preferred_element_type=f32)


hidden_tile = 512


def core_kernel(rows, span, count, outs, info, where, slots, *refs):
    w_parts, o_parts, refs = refs[:count], refs[count : 2 * count], refs[2 * count :]
    if outs == 1:
        d_parts, refs = refs[:1], refs[1:]
    low_h, low_th, gated_th, n1_h, s1_h, cp_h, q_h, vecs, rate, layer = refs[:10]
    refs = refs[10:]
    gain1, shift1, bias, gain2, shift2 = (vecs.at[pl.ds(k, 1)] for k in range(1, 6))
    down_out, first_out, second_out, refs = refs[:outs], refs[outs : 2 * outs], refs[2 * outs : 3 * outs], refs[3 * outs :]
    pre1_h, gg_h, ends, dev_end, sums_two, sums_one, w, wd, wo, act, pull, gel, low, low_t, gated_t = refs[:15]
    n1, s1, cp, q, acc, first, feed, out_low, mix, gs, us, dd, dwg, dwu, dwo = refs[15:30]
    in_sems, w_sems, d_sems, o_sems, dd_sems, dw_sems, end_sems = refs[30:]
    hidden, width = wd.shape
    tile, seg, modes = hidden_tile, span // segs, rate.shape[0]
    tiles, tokens = hidden // tile, rows * span
    base = info[2 * rows] * span

    def bring(k, src, dst):
        return pltpu.make_async_copy(src, dst, in_sems.at[k])

    w_in = [
        [
            copy
            for k, at in enumerate((t * tile, hidden + t * tile))
            for copy in fetch_parts(where, w_parts, w, w_sems.at[k, t], at, pl.ds(at, tile))
        ]
        for t in range(tiles)
    ]
    if outs == 1:
        d_in = fetch_parts(where, d_parts, wd, d_sems.at[0])
    else:
        depth = w_parts[0].shape[0]
        d_in = [
            pltpu.make_async_copy(
                part.at[:, pl.ds(2 * hidden + j * width, width)],
                wd.at[pl.ds(pl.multiple_of(where[k] * (hidden // count) + j * depth, 8), depth)],
                d_sems.at[j, k],
            )
            for k, part in enumerate(w_parts)
            for j in range(hidden // count // depth)
        ]
    o_in = fetch_parts(where, o_parts, wo, o_sems, o_parts[0].shape[1] - width)
    low_in = bring(0, low_h, low)
    norm_in = [bring(1, n1_h, n1), bring(2, cp_h, cp)]
    late_in = [bring(3, low_th, low_t), bring(4, s1_h, s1), bring(5, q_h, q), bring(6, gated_th, gated_t)]
    start_all([low_in] + w_in[0] + w_in[1])
    low_in.wait()
    scale = 0.7978845608028654
    for t in range(tiles):
        if t + 2 < tiles:
            start_all(w_in[t + 2])
        if t == 1:
            start_all(d_in)
        if t == 3:
            start_all(norm_in)
        wait_all(w_in[t])
        cols, up_cols = pl.ds(t * tile, tile), pl.ds(hidden + t * tile, tile)
        gs[...] = jnp.dot(low[...], w[:, cols], preferred_element_type=f32)
        us[...] = jnp.dot(low[...], w[:, up_cols], preferred_element_type=f32)

        @pl.loop(0, tokens // 16, unroll=2)
        def _(k):
            tok = pl.ds(pl.multiple_of(k * 16, 16), 16)
            g, u = gs[tok, :], us[tok, :]
            sq = g * g
            th = jnp.tanh(g * (scale + (scale * 0.044715) * sq))
            side = 0.5 + 0.5 * th
            gelu = g * side
            slope = side + (0.5 * g) * (1.0 - th * th) * (scale + (3.0 * scale * 0.044715) * sq)
            act[tok, cols] = (gelu * u).astype(bf16)
            pull[tok, cols] = (u * slope).astype(bf16)
            gel[tok, cols] = gelu.astype(bf16)

    wait_all(d_in)
    start_all(late_in + o_in)
    for t in range(width // lane_block):
        c = pl.ds(t * lane_block, lane_block)
        acc[:, c] = jnp.dot(act[...], wd[:, c], preferred_element_type=f32)
    zero = jnp.zeros((8, width), f32)
    wait_all(norm_in)

    def outer_norm(k, loop):
        tok = pl.ds(pl.multiple_of(k * 16, 16), 16)
        n = iota((16, width), 0) + k * 16
        n = n & (span - 1)
        pos = base + (n & (segs - 1)) * seg + lax.shift_right_logical(n, 3)
        limit = jnp.where(k * 16 >= span, info[1], info[0])
        keep = (pos < limit).astype(f32)
        v = n1[tok, :] * gain1[...] + shift1[...] + acc[tok, :] + bias[...]
        centre = v - row_mean(v)
        inv = lax.rsqrt(row_mean(centre * centre) + norm_eps)
        n2 = centre * inv
        out_low[tok, :] = ((n2 * gain2[...] + shift2[...]) * keep).astype(bf16)
        top = cp[tok, :].astype(f32) * keep
        e = top * gain2[...]
        grad = inv * (e - row_mean(e) - n2 * row_mean(e * n2))
        first[tok, :] = grad
        cut = grad.astype(bf16)
        feed[tok, :] = cut
        return (
            loop[0] + fold(cut.astype(f32)),
            loop[1] + fold(top * n2),
            loop[2] + fold(top),
        )

    totals = lax.fori_loop(0, tokens // 16, outer_norm, (zero, zero, zero), unroll=4)
    for k in range(3):
        sums_two[pl.ds(k, 1), :] = jnp.sum(totals[k], axis=0, keepdims=True)

    blocks = 8
    span_d = hidden // blocks
    d_sends = []
    for k in range(blocks):
        if k >= 4:
            d_sends[k - 4].wait()
        which = k if outs == 1 else slots[k]
        c = pl.ds(pl.multiple_of(which * span_d, 128), span_d)
        dd[k % 4] = jnp.dot(act[:, c].T, feed[...], preferred_element_type=f32).astype(bf16)
        per = down_out[0].shape[0]
        dst = down_out[0].at[0, pl.ds(k * span_d, span_d)] if outs == 1 else down_out[k // per].at[k % per]
        d_sends.append(pltpu.make_async_copy(dd.at[k % 4], dst, dd_sems.at[k]))
        d_sends[k].start()
    o, n = iota((span, span), 0), iota((span, span), 1)
    back = (o == (n & (segs - 1)) * seg + lax.shift_right_logical(n, 3)).astype(f32).astype(bf16)
    for r in range(rows):
        layer[r] = jnp.dot(back, out_low[pl.ds(r * span, span), :], preferred_element_type=f32).astype(bf16)
    wait_all(late_in)
    sends = []
    half_tiles = tiles // 2
    for t in range(tiles):
        cols, up_cols = pl.ds(t * tile, tile), pl.ds(hidden + t * tile, tile)
        grad = contract_last(feed[...], wd[cols, :])
        g = (grad * pull[:, cols].astype(f32)).astype(bf16)
        u = (grad * gel[:, cols].astype(f32)).astype(bf16)
        if t >= 2:
            wait_all(sends[t - 2])
        dwg[t % 2] = jnp.dot(low_t[...], g, preferred_element_type=f32).astype(bf16)
        dwu[t % 2] = jnp.dot(low_t[...], u, preferred_element_type=f32).astype(bf16)
        into, at, own = (first_out, 0, t) if t < half_tiles else (second_out, width, t - half_tiles)
        g_at, u_at = at + own * tile, at + (half_tiles + own) * tile
        sends.append(
            send_parts(slots, dwg.at[t % 2], into, dw_sems.at[0, t], None, pl.ds(g_at, tile))
            + send_parts(slots, dwu.at[t % 2], into, dw_sems.at[1, t], None, pl.ds(u_at, tile))
        )
        start_all(sends[t])
        first[...] += contract_last(g, w[:, cols]) + contract_last(u, w[:, up_cols])

    def put(k, src, dst):
        return pltpu.make_async_copy(src, dst, end_sems.at[k])

    def inner_norm(k, loop):
        tok = pl.ds(pl.multiple_of(k * 16, 16), 16)
        top, n = first[tok, :], n1[tok, :]
        e = top * gain1[...]
        grad = s1[tok, 0:1] * (e - row_mean(e) - n * row_mean(e * n))
        acc[tok, :] = grad
        cut = grad.astype(bf16)
        mix[tok, :] = cut
        return (
            loop[0] + fold(cut.astype(f32)),
            loop[1] + fold(top * n),
            loop[2] + fold(top),
        )

    totals = lax.fori_loop(0, tokens // 16, inner_norm, (zero, zero, zero), unroll=4)
    finals = [put(0, acc, pre1_h)]
    finals[0].start()
    for k in range(3):
        sums_one[pl.ds(k, 1), :] = jnp.sum(totals[k], axis=0, keepdims=True)
    dwo[...] = jnp.dot(gated_t[...], mix[...], preferred_element_type=f32).astype(bf16)
    o_sends = send_parts(slots, dwo, second_out, dw_sems.at[2, 0], None, pl.ds(0, width))
    start_all(o_sends)
    wait_all(o_in)
    for t in range(width // lane_block):
        c = pl.ds(t * lane_block, lane_block)
        first[:, c] = contract_last(mix[...], wo[c, :])
    sub = iota((segs, lane_block), 0)
    for r in range(rows):
        factor = factor_of(info, rows, r)
        for t in range(width // lane_block):
            c = pl.ds(t * lane_block, lane_block)
            fade = [jnp.exp(-rate[pl.ds(m, 1), c] * factor) for m in range(modes)]
            far = [jnp.exp(-rate[pl.ds(m, 1), c] * (factor * seg)) for m in range(modes)]

            def step(k, states):
                j = seg - 1 - k
                live = (base + sub * seg + j < info[r]).astype(f32)
                tok = pl.ds(pl.multiple_of(r * span + j * segs, segs), segs)
                grad = first[tok, c] * live
                first[tok, c] = grad
                g = grad * q[r, j, :, c]
                return tuple(f * h + g for f, h in zip(fade, states))

            blank = jnp.zeros((segs, lane_block), f32)
            states = lax.fori_loop(0, seg, step, (blank,) * modes, unroll=4)
            for m in range(modes):
                ends[r, m, :, c] = states[m]
                total = jnp.zeros((1, lane_block), f32)
                for i in reversed(range(segs)):
                    total = far[m] * total + states[m][i : i + 1]
                dev_end[r, pl.ds(m, 1), c] = total
    finals.append(put(1, first, gg_h))
    finals[1].start()
    for copies in [d_sends[-4:]] + sends[-2:] + [o_sends, finals]:
        wait_all(copies)


def feed_core(
    info, where, slots, w_parts, d_parts, o_parts, low, low_t, gated_t, n1, s1, cp, q, vecs, rate, down_shapes, first_shapes, second_shapes,
):
    tokens, width = n1.shape
    rows, seg = q.shape[:2]
    modes, count, outs = rate.shape[0], len(w_parts), len(first_shapes)
    hidden, tile, pieces = down_shapes[0][0] * outs * down_shapes[0][1], hidden_tile, first_shapes[0][0] * outs
    shapes = tuple(down_shapes) + tuple(first_shapes) + tuple(second_shapes)
    return pl.pallas_call(
        lambda *refs: core_kernel(rows, seg * segs, count, outs, *refs),
        out_shape=(vm((rows, seg * segs, width), bf16),)
        + tuple(vm(s, bf16) for s in shapes)
        + (
            vm((tokens, width)),
            vm((tokens, width)),
            vm((rows, modes, segs, width)),
            vm((rows, modes, width)),
            vm((8, width)),
            vm((8, width)),
        ),
        in_specs=smem_spec() * 3 + hbm_specs(2 * count + len(d_parts) + 7) + vmem_specs(2),
        out_specs=tuple(vmem_specs(1) + hbm_specs(3 * outs + 2) + vmem_specs(4)),
        scratch_shapes=[
            pltpu.VMEM((width, 2 * hidden), bf16),
            pltpu.VMEM((hidden, width), bf16),
            pltpu.VMEM((width, width), bf16),
            pltpu.VMEM((tokens, hidden), bf16),
            pltpu.VMEM((tokens, hidden), bf16),
            pltpu.VMEM((tokens, hidden), bf16),
            pltpu.VMEM((tokens, width), bf16),
            pltpu.VMEM((width, tokens), bf16),
            pltpu.VMEM((width, tokens), bf16),
            pltpu.VMEM((tokens, width), f32),
            pltpu.VMEM((tokens, 128), f32),
            pltpu.VMEM((tokens, width), bf16),
            pltpu.VMEM(q.shape, f32),
            pltpu.VMEM((tokens, width), f32),
            pltpu.VMEM((tokens, width), f32),
            pltpu.VMEM((tokens, width), bf16),
            pltpu.VMEM((tokens, width), bf16),
            pltpu.VMEM((tokens, width), bf16),
            pltpu.VMEM((tokens, tile), f32),
            pltpu.VMEM((tokens, tile), f32),
            pltpu.VMEM((4, hidden // 8, width), bf16),
            pltpu.VMEM((2, width, tile), bf16),
            pltpu.VMEM((2, width, tile), bf16),
            pltpu.VMEM((width, width), bf16),
            pltpu.SemaphoreType.DMA((7,)),
            pltpu.SemaphoreType.DMA((2, hidden // tile, count)),
            pltpu.SemaphoreType.DMA((hidden // width, count)),
            pltpu.SemaphoreType.DMA((count,)),
            pltpu.SemaphoreType.DMA((8,)),
            pltpu.SemaphoreType.DMA((3, hidden // tile, pieces)),
            pltpu.SemaphoreType.DMA((2,)),
        ],
        compiler_params=pltpu.CompilerParams(vmem_limit_bytes=vmem_cap),
        cost_estimate=spent(1),
        name="feed_core",
    )(
        info, where, slots, *w_parts, *o_parts, *d_parts, low, low_t, gated_t, n1, s1, cp, q, vecs, rate
    )


def split_rims(rows, seg, at, rim, low, high):
    for r in range(rows):
        for k in range(2):
            rim[pl.ds(2 * r + k, 1), :] = at(r, k, pl.ds(0, 1))
            rim[pl.ds(2 * (rows + r) + k, 1), :] = at(r, seg - 2 + k, pl.ds(segs - 1, 1))
    low[...] = rim[: 2 * rows].astype(bf16)
    high[...] = rim[2 * rows : 4 * rows].astype(bf16)


def source_kernel(rows, span, others, info, *refs):
    gath = refs[:others]
    ends, carry, rate, res, refs = *refs[others : others + 4], refs[others + 4 :]
    streams, refs = refs[:5], refs[5:]
    gm_h, rim_low, rim_high, gres, grate, gg, q, long_out, keys, vals, gm, hist, rim, in_sems, out_sems = refs
    seg = span // segs
    width, modes = q.shape[3], rate.shape[0]
    blocks = width // lane_block
    ins = [
        [
            pltpu.make_async_copy(
                src.at[:, :, :, pl.ds(t * lane_block, lane_block)],
                dst.at[:, :, :, pl.ds(t * lane_block, lane_block)],
                in_sems.at[t, k],
            )
            for k, (src, dst) in enumerate(zip(streams, (gg, q, long_out, keys, vals)))
        ]
        for t in range(blocks)
    ]
    sends = [
        [
            pltpu.make_async_copy(
                gm.at[:, :, :, pl.ds(b * width + t * lane_block, lane_block)],
                gm_h.at[:, pl.ds(2, seg), :, pl.ds(b * width + t * lane_block, lane_block)],
                out_sems.at[t, b],
            )
            for b in range(3)
        ]
        for t in range(blocks)
    ]
    for t in range(blocks):
        start_all(ins[t])
    base = info[2 * rows] * span
    sub = iota((segs, lane_block), 0)
    for t in range(blocks):
        wait_all(ins[t])
        c = pl.ds(t * lane_block, lane_block)
        sum_res = [jnp.zeros((1, lane_block), f32) for _ in range(modes)]
        sum_rate = [jnp.zeros((1, lane_block), f32) for _ in range(modes)]
        for r in range(rows):
            factor = factor_of(info, rows, r)
            fade, mix, start, root, ebb = [], [], [], [], []
            for m in range(modes):
                d = rate[pl.ds(m, 1), c] * factor
                fade.append(jnp.exp(-d))
                ebb.append(jnp.exp(-2.0 * d))
                root.append(jnp.sqrt(1.0 - ebb[m]))
                mix.append(res[pl.ds(m, 1), c] * root[m])
                far = jnp.exp(-d * seg)
                cur = carry_in([g[r, pl.ds(m, 1), c] for g in gath], jnp.exp(-d * span))
                tile = jnp.zeros((segs, lane_block), f32)
                end = ends[r, m, :, c]
                for i in reversed(range(segs)):
                    tile = jnp.where(sub == i, cur, tile)
                    cur = far * cur + end[i : i + 1]
                start.append(tile)

            def ahead(j, loop):
                states, sums = loop
                live = (base + sub * seg + j < info[r]).astype(f32)
                src = keys[r, j, :, c] * vals[r, j, :, c] * live
                g = gg[r, j, :, c] * q[r, j, :, c]
                past = tuple(f * h for f, h in zip(fade, states))
                for m in range(modes):
                    hist[m, j] = past[m]
                states = tuple(p + src for p in past)
                return (states, tuple(s + g * h for s, h in zip(sums, states)))

            zero = jnp.zeros((segs, lane_block), f32)
            init = tuple(carry[r, m, :, c] for m in range(modes))
            _, with_state = lax.fori_loop(0, seg, ahead, (init, (zero,) * modes), unroll=4)

            def behind(k, loop):
                states, sums = loop
                j = seg - 1 - k
                live = (base + sub * seg + j < info[r]).astype(f32)
                grad = gg[r, j, :, c]
                g = grad * q[r, j, :, c]
                states = tuple(f * h + g for f, h in zip(fade, states))
                gs = mix[0] * states[0]
                for m in range(1, modes):
                    gs = gs + mix[m] * states[m]
                gs = gs * live
                for b, part in enumerate(
                    (grad * long_out[r, j, :, c], gs * vals[r, j, :, c], gs * keys[r, j, :, c])
                ):
                    gm[r, j, :, pl.ds(b * width + t * lane_block, lane_block)] = part.astype(bf16).astype(f32)
                return (states, tuple(s + h * hist[m, j] for m, (s, h) in enumerate(zip(sums, states))))

            _, with_lag = lax.fori_loop(0, seg, behind, (tuple(start), (zero,) * modes), unroll=4)
            for m in range(modes):
                u = jnp.sum(with_state[m], axis=0, keepdims=True)
                v = jnp.sum(with_lag[m], axis=0, keepdims=True)
                sum_res[m] = sum_res[m] + root[m] * u
                sum_rate[m] = sum_rate[m] + factor * res[pl.ds(m, 1), c] * (ebb[m] / root[m] * u - root[m] * v)
        for m in range(modes):
            gres[pl.ds(m, 1), c] = sum_res[m]
            grate[pl.ds(m, 1), c] = sum_rate[m]
        start_all(sends[t])
    split_rims(rows, seg, lambda r, j, i: gm[r, j, i, :], rim, rim_low, rim_high)
    for t in range(blocks):
        wait_all(sends[t])


def mixer_source(info, gath, ends, carry, gg, q, long_out, keys, vals, rate, res):
    rows, seg, _, width = q.shape
    modes = rate.shape[0]
    return pl.pallas_call(
        lambda *refs: source_kernel(rows, seg * segs, len(gath), *refs),
        out_shape=(
            vm((rows, seg + 4, segs, 3 * width)),
            vm((2 * rows, 3 * width), bf16),
            vm((2 * rows, 3 * width), bf16),
            vm((modes, width)),
            vm((modes, width)),
        ),
        in_specs=smem_spec() + vmem_specs(4 + len(gath)) + hbm_specs(5),
        out_specs=tuple(hbm_specs(1) + vmem_specs(4)),
        scratch_shapes=[pltpu.VMEM(q.shape, f32)] * 5
        + [
            pltpu.VMEM((rows, seg, segs, 3 * width), f32),
            pltpu.VMEM((modes, seg, segs, lane_block), f32),
            pltpu.VMEM((4 * rows, 3 * width), f32),
            pltpu.SemaphoreType.DMA((width // lane_block, 5)),
            pltpu.SemaphoreType.DMA((width // lane_block, 3)),
        ],
        compiler_params=pltpu.CompilerParams(vmem_limit_bytes=vmem_cap),
        cost_estimate=spent(1),
        name="mixer_source",
    )(info, *gath, ends, carry, rate, res, gg, q, long_out, keys, vals)


def taps_blocks(rows, span, seq_count, info, gm, halo, ext, st, ct, gp, put, gsc, ready, done):
    seg = span // segs
    width = ct.shape[1]
    place = info[2 * rows]
    base = place * span
    sub = iota((segs, lane_block), 0)
    in_low = 1.0 - (place == 0).astype(f32) * (sub == 0).astype(f32)
    in_high = 1.0 - (place == seq_count - 1).astype(f32) * (sub == segs - 1).astype(f32)
    zero = jnp.zeros((segs, lane_block), f32)
    for block in range(3):
        for t in range(width // lane_block):
            ready(block * (width // lane_block) + t)
            for r in range(rows):
                fill_edges(gm, r, seg, halo, (block * width + t * lane_block, lane_block))
            c = pl.ds(block * width + t * lane_block, lane_block)
            lanes = pl.ds(t * lane_block, lane_block)
            sums = tuple(zero for _ in range(4))
            csums = tuple(zero for _ in range(3))
            for r in range(rows):

                def tap3(e):
                    return (
                        st[pl.ds(0, 1), c] * ext[r, e - 1, :, c]
                        + st[pl.ds(1, 1), c] * ext[r, e, :, c]
                        + st[pl.ds(2, 1), c] * ext[r, e + 1, :, c]
                    )

                def grad_at(e):
                    if block != 1:
                        return gm[r, e, :, c]
                    return (
                        ct[pl.ds(0, 1), lanes] * gm[r, e + 1, :, c]
                        + ct[pl.ds(1, 1), lanes] * gm[r, e, :, c]
                        + ct[pl.ds(2, 1), lanes] * gm[r, e - 1, :, c]
                    )

                def step(j, loop):
                    prev, cur, kp_prev, kp_cur, sums, csums = loop
                    nxt = grad_at(j + 3)
                    if block == 1:
                        nxt = jnp.where(j == seg - 1, nxt * in_high, nxt)
                        kp_next = tap3(j + 3)
                        kp_next = jnp.where(j == seg - 1, kp_next * in_high, kp_next)
                        own = gm[r, j + 2, :, c]
                        csums = tuple(s + own * k for s, k in zip(csums, (kp_prev, kp_cur, kp_next)))
                    else:
                        kp_next = kp_cur
                    live = (base + sub * seg + j < info[r]).astype(f32)
                    full = (
                        st[pl.ds(0, 1), c] * nxt + st[pl.ds(1, 1), c] * cur + st[pl.ds(2, 1), c] * prev
                    ) * live
                    full = full.astype(bf16).astype(f32)
                    gsc[r, j] = full
                    sums = (
                        sums[0] + cur * ext[r, j + 1, :, c],
                        sums[1] + cur * ext[r, j + 2, :, c],
                        sums[2] + cur * ext[r, j + 3, :, c],
                        sums[3] + full,
                    )
                    return (cur, nxt, kp_cur, kp_next, sums, csums)

                if block == 1:
                    start = (grad_at(1) * in_low, grad_at(2), tap3(1) * in_low, tap3(2), sums, csums)
                else:
                    start = (grad_at(1), grad_at(2), zero, zero, sums, csums)
                _, _, _, _, sums, csums = lax.fori_loop(0, seg, step, start, unroll=8)
                gp[pl.ds(r * span, span), c] = gsc[r].reshape(span, lane_block).astype(bf16)
            for k in range(3):
                put("short", k, block, lanes, jnp.sum(sums[k], axis=0, keepdims=True))
            put("bias", 0, block, lanes, jnp.sum(sums[3], axis=0, keepdims=True))
            if block == 1:
                for k in range(3):
                    put("cond", k, block, lanes, jnp.sum(csums[k], axis=0, keepdims=True))
        done(block)


row_bias, row_short, row_cond, row_res, row_rate, row_one, row_two, small_rows = 0, 3, 12, 15, 19, 23, 26, 32


def small_put(small):
    def put(kind, k, block, lanes, value):
        row = {"bias": row_bias + block, "short": row_short + 3 * k + block, "cond": row_cond + k}[kind]
        small[pl.ds(row, 1), lanes] = value

    return put


def taps_kernel(rows, span, seq_count, count, outs, info, where, slots, *refs):
    parts, refs = refs[:count], refs[count:]
    gm_h, ext_h, xpt_h, pre1_h, before, after, st, ct, gres, grate, sums_one, sums_two = refs[:12]
    hidden_grad, small = refs[12:14]
    dws, refs = refs[14 : 14 + outs], refs[14 + outs :]
    gsc, gm, ext, xpt, pre1, gp, halo, w, dw, low, stream_sems, in_sems, sems, out_sems = refs
    width = ct.shape[1]
    groups = 3 * width // lane_block
    streams = [
        [
            pltpu.make_async_copy(
                src.at[:, :, :, pl.ds(n * lane_block, lane_block)],
                dst.at[:, :, :, pl.ds(n * lane_block, lane_block)],
                stream_sems.at[k, n],
            )
            for k, (src, dst) in enumerate(((gm_h, gm), (ext_h, ext)))
        ]
        for n in range(groups)
    ]
    late = [pltpu.make_async_copy(xpt_h, xpt, in_sems.at[0]), pltpu.make_async_copy(pre1_h, pre1, in_sems.at[1])]
    copies = fetch_parts(where, parts, w, sems)
    start_all(streams[0] + streams[1])

    def ready(n):
        wait_all(streams[n])
        if n + 2 < groups:
            start_all(streams[n + 2])
        if n == 0:
            late[0].start()
        if n == groups // 2:
            start_all(copies + late[1:])

    small[...] = jnp.zeros_like(small)
    modes = gres.shape[0]
    small[pl.ds(row_res, modes), :] = gres[...]
    small[pl.ds(row_rate, modes), :] = grate[...]
    small[pl.ds(row_one, 3), :] = sums_one[pl.ds(0, 3), :]
    small[pl.ds(row_two, 3), :] = sums_two[pl.ds(0, 3), :]
    join_rims(rows, before, after, halo)
    sends = []

    def done(block):
        c = pl.ds(block * width, width)
        if block == 0:
            late[0].wait()
        dw[:, c] = jnp.dot(xpt[...], gp[:, c], preferred_element_type=f32).astype(bf16)
        sends.extend(send_parts(slots, dw, dws, out_sems.at[block], c))
        start_all(sends[-outs * dws[0].shape[0] :])

    taps_blocks(
        rows, span, seq_count, info, gm, halo, ext, st, ct, gp, small_put(small), gsc,
        ready, done,
    )
    wait_all(copies + late[1:])
    low[...] = (contract_last(gp[...], w[...]) + pre1[...]).astype(bf16)
    o, n = iota((span, span), 0), iota((span, span), 1)
    seg = span // segs
    back = (o == (n & (segs - 1)) * seg + lax.shift_right_logical(n, 3)).astype(f32).astype(bf16)
    for r in range(rows):
        moved = jnp.dot(back, low[pl.ds(r * span, span), :], preferred_element_type=f32)
        hidden_grad[r] = moved.astype(bf16)
    wait_all(sends)


def mixer_taps(
    info, where, slots, gm, parts, before, after, ext, st, ct, xpt, pre1, gres, grate, sums_one, sums_two,
    seq_count, dw_shapes,
):
    rows, padded, _, wide = ext.shape
    seg, width = padded - 4, wide // 3
    tokens = rows * seg * segs
    count, outs = len(parts), len(dw_shapes)
    return pl.pallas_call(
        lambda *refs: taps_kernel(rows, seg * segs, seq_count, count, outs, *refs),
        out_shape=(vm((rows, seg * segs, width), bf16), vm((small_rows, width)))
        + tuple(vm(s, bf16) for s in dw_shapes),
        in_specs=smem_spec() * 3 + hbm_specs(count + 4) + vmem_specs(8),
        out_specs=tuple(vmem_specs(2)) + tuple(any_specs(outs)),
        scratch_shapes=[
            pltpu.VMEM((rows, seg, segs, lane_block), f32),
            pltpu.VMEM(gm.shape, f32),
            pltpu.VMEM(ext.shape, f32),
            pltpu.VMEM(xpt.shape, bf16),
            pltpu.VMEM(pre1.shape, f32),
            pltpu.VMEM((tokens, wide), bf16),
            pltpu.VMEM((16, wide), f32),
            pltpu.VMEM((width, wide), bf16),
            pltpu.VMEM((width, wide), bf16),
            pltpu.VMEM((tokens, width), bf16),
            pltpu.SemaphoreType.DMA((2, wide // lane_block)),
            pltpu.SemaphoreType.DMA((2,)),
            pltpu.SemaphoreType.DMA((count,)),
            pltpu.SemaphoreType.DMA((3, outs * dw_shapes[0][0])),
        ],
        compiler_params=pltpu.CompilerParams(vmem_limit_bytes=vmem_cap),
        cost_estimate=spent(1),
        name="mixer_taps",
    )(
        info, where, slots, *parts, gm, ext, xpt, pre1, before, after, st, ct, gres, grate, sums_one, sums_two
    )


def chip_pairs(count):
    first = [(d, d ^ (2 if d % 2 == 0 else 4)) for d in range(count)]
    second = [(d, d ^ (4 if d % 2 == 0 else 2)) for d in range(count)]
    core = [(d, d ^ 1) for d in range(count)]
    return core, first, second


def tie(value, *needs):
    return lax.optimization_barrier((value, needs))[0]


def cross(block, pairs):
    return lax.ppermute(block, "dp", pairs)


def shard_order(me):
    even = (me & 1) == 0
    f = jnp.where(even, 2, 4)
    g = jnp.where(even, 4, 2)
    near = [me, me ^ f, me ^ g, me ^ 6]
    far = [me ^ 1, me ^ 1 ^ g, me ^ 1 ^ f, me ^ 7]
    return jnp.stack(near + far).astype(jnp.int32)


def slot_order(me):
    even = (me & 1) == 0
    f = jnp.where(even, 2, 4)
    g = jnp.where(even, 4, 2)
    mine = [me, me ^ g, me ^ f, me ^ 6]
    theirs = [me ^ 1, me ^ 1 ^ f, me ^ 1 ^ g, me ^ 7]
    return jnp.stack(mine + theirs).astype(jnp.int32)


class Gather:
    def __init__(self, shard, name):
        self.shard, self.name = shard, name
        self.core, self.first, self.second = chip_pairs(8)

    def one(self, *needs):
        with jax.named_scope(self.name + "_one"):
            self.p1 = cross(tie(self.shard, *needs), self.first)
        return self.p1

    def two(self, *needs):
        with jax.named_scope(self.name + "_two"):
            self.p2 = cross(tie(self.shard, *needs), self.second)
        return self.p2

    def three(self, *needs):
        with jax.named_scope(self.name + "_three"):
            self.p3 = cross(tie(self.p1, *needs), self.second)
        return self.p3

    def share(self, early=(), late=()):
        near = [self.shard, self.p1, self.p2, self.p3]
        with jax.named_scope(self.name + "_core"):
            sent = [tie(p, *early) for p in near[:3]] + [tie(near[3], *late)]
            self.parts = near + [cross(p, self.core) for p in sent]
        return self.parts


class Scatter:
    steps = 6

    def __init__(self, mine, theirs, name):
        self.mine, self.theirs, self.name, self.at = mine, theirs, name, 0
        self.core, self.first, self.second = chip_pairs(8)
        self.odd = lax.axis_index("seq") & 1
        self.near = [(i, i ^ 1) for i in range(4)]

    def step(self, *needs):
        self.at += 1
        with jax.named_scope(f"{self.name}_s{self.at}"):
            return getattr(self, f"step{self.at}")(needs)

    def step1(self, needs):
        self.sent = tie(self.theirs, *needs)
        self.got = cross(self.sent, self.core)
        return self.got

    def step2(self, needs):
        got = tie(self.got, *needs)
        self.sent = (self.mine[2:].astype(f32) + got[2:].astype(f32)).astype(bf16)
        self.got1 = cross(self.sent, self.first)
        return self.got1

    def step3(self, needs):
        got1 = tie(self.got1, *needs)
        send = self.mine[1].astype(f32) + self.got[1].astype(f32) + got1[1].astype(f32)
        self.sent = send.astype(bf16)
        self.got2 = cross(self.sent, self.second)
        return self.got2

    def own_half(self, got2, high):
        depth, wide = got2.shape[0] // 2, got2.shape[1]

        def cut(block):
            if block.ndim == 2:
                return lax.dynamic_slice(block, (high * depth, 0), (depth, wide)).astype(f32)
            return lax.dynamic_slice(block, (0, high * depth, 0), (1, depth, wide))[0].astype(f32)

        return cut(self.mine) + cut(self.got) + cut(self.got1) + cut(got2)

    def step4(self, needs):
        self.sent = self.own_half(tie(self.got2, *needs), 1 - self.odd).astype(bf16)
        self.h1 = lax.ppermute(self.sent, "seq", self.near)
        return self.h1

    def step5(self, needs):
        part = self.own_half(self.got2, self.odd) + tie(self.h1, *needs).astype(f32)
        self.part = self.sent = part.astype(bf16)
        self.h2 = lax.ppermute(self.part, "seq", [(i, i ^ 2) for i in range(4)])
        return self.h2

    def step6(self, needs):
        self.total = (self.part.astype(f32) + tie(self.h2, *needs).astype(f32)).astype(bf16)
        self.sent = self.total
        self.h3 = lax.ppermute(self.total, "seq", self.near)
        return self.h3

    def result(self):
        odd = self.odd == 1
        low = jnp.where(odd, self.h3, self.total)
        return jnp.concatenate([low, jnp.where(odd, self.total, self.h3)]).astype(f32)


class Total:
    steps = 5

    def __init__(self, flat, name):
        self.flat, self.name, self.at = flat, name, 0

    def step(self, *needs):
        axis, count, bit = (("dp", 8, 1), ("dp", 8, 2), ("dp", 8, 4), ("seq", 4, 1), ("seq", 4, 2))[self.at]
        self.at += 1
        with jax.named_scope(f"{self.name}_s{self.at}"):
            flat = self.sent = tie(self.flat, *needs)
            got = lax.ppermute(flat, axis, [(d, d ^ bit) for d in range(count)])
            self.flat = flat + got
        return got

    def result(self):
        return self.flat


def advance(last, *flows):
    for f in flows:
        f.step(last)
        last = f.sent
    return last


def local(
    hidden_in,
    seq_len,
    bucket,
    in_weight,
    in_bias,
    short_taps,
    cond_taps,
    mode_residue,
    mode_rate,
    out_weight,
    out_bias,
    norm1_gain,
    norm1_bias,
    gate_weight,
    up_weight,
    down_weight,
    down_bias,
    norm2_gain,
    norm2_bias,
    out_cotangent,
):
    rows, span, width = hidden_in.shape
    tokens, seg = rows * span, span // segs
    dp_count, seq_count = lax.axis_size("dp"), lax.axis_size("seq")
    me, place = lax.axis_index("dp"), lax.axis_index("seq")
    info = jnp.concatenate([seq_len, bucket, place[None]]).astype(jnp.int32)
    chips = dp_count == 8 and seq_count == 4
    up_line = [(i, i + 1) for i in range(seq_count - 1)]
    down_line = [(i + 1, i) for i in range(seq_count - 1)]

    def rims(low, high):
        return lax.ppermute(high, "seq", up_line), lax.ppermute(low, "seq", down_line)

    def dw_shapes(depth, wide):
        return ((4, depth, wide),) * 2 if chips else ((1, depth * dp_count, wide),)

    line_in = in_bias[None]
    vecs = jnp.stack([out_bias, norm1_gain, norm1_bias, down_bias, norm2_gain, norm2_bias])

    def states_of(block, sign):
        return [
            lax.ppermute(block, "seq", [(i, i + sign * k) for i in range(seq_count) if 0 <= i + sign * k < seq_count])
            for k in range(1, seq_count)
        ]

    hidden = gate_weight.shape[1]
    depth = gate_weight.shape[0]
    half = hidden // 2
    before, after = rims(
        hidden_in[:, :2].reshape(2 * rows, width), hidden_in[:, span - 2 :].reshape(2 * rows, width)
    )
    shard_io = jnp.concatenate([in_weight, out_weight], axis=1)
    d_parts = ()
    if chips:
        downs = [down_weight[k * depth : (k + 1) * depth] for k in range(hidden // width)]
        shard_f = jnp.concatenate([gate_weight, up_weight, *downs], axis=1)
        w_io, w_f = Gather(shard_io, "w_in_out"), Gather(shard_f, "w_feed_down")
        w_io.one()
        w_io.two()
        w_io.three(w_io.p2, before, after, shard_f, info)
        io_parts = w_io.share((w_io.p1,))
        w_f.one(w_io.p3)
        w_f.two(w_io.p3)
    else:
        shard_f = jnp.concatenate([gate_weight, up_weight], axis=1)
        io_parts, f_parts, d_parts = (
            [lax.all_gather(shard, "dp", axis=0, tiled=True)] for shard in (shard_io, shard_f, down_weight)
        )
    one = jnp.zeros((1,), jnp.int32)
    where = shard_order(me) if chips else one
    slots = slot_order(me) if chips else one

    xp, xpt, cp, ext, q, keys, vals, ends, dev_end = mixer_enter(
        info, where, hidden_in, out_cotangent, before, after, line_in, short_taps, cond_taps, mode_rate,
        io_parts, seq_count,
    )
    gath = states_of(dev_end, 1)
    if chips:
        w_f.three(gath, w_f.p2, vecs)
    long_out, gated_t, carry, n1, s1, low, low_t = mixer_settle(
        info, where, gath, ends, q, keys, vals, mode_rate, mode_residue, xp,
        vecs, io_parts,
    )
    if chips:
        f_parts = w_f.share((gath,), (low,))
    layer_out, *grads, pre1, gg, back_ends, back_dev, sums_two, sums_one = feed_core(
        info, where, slots, f_parts, d_parts, io_parts, low, low_t, gated_t, n1, s1, cp, q, vecs, mode_rate,
        dw_shapes(*down_weight.shape), dw_shapes(depth, hidden), dw_shapes(depth, width + hidden),
    )
    gg = gg.reshape(q.shape)
    back_gath = states_of(back_dev, -1)
    wait = ()
    if chips:
        s_d, s_a, s_b = (
            Scatter(*grads[2 * k : 2 * k + 2], name) for k, name in enumerate(("g_down", "g_feed", "g_out_feed"))
        )
        s_d.step()
        s_a.step(back_gath)
        s_b.step(back_gath)
        wait = advance(back_gath[0], s_d)
    gm, rim_low, rim_high, g_res, g_rate = mixer_source(
        tie(info, wait), back_gath, back_ends, carry, gg, q, long_out, keys, vals, mode_rate, mode_residue
    )
    before, after = rims(rim_low, rim_high)
    if chips:
        wait = advance(rim_low, s_d, s_a)
    grad_hidden, small, *g_in = mixer_taps(
        tie(info, wait), where, slots, gm, io_parts, before, after, ext, short_taps, cond_taps,
        xpt, pre1, g_res, g_rate, sums_one, sums_two, seq_count, dw_shapes(depth, 3 * width),
    )

    if chips:
        s_in = Scatter(*g_in, "g_in")
        s_small = Total(small, "g_small")
        s_in.step()
        order = (
            s_b, s_d, s_a, s_in, s_d, s_small, s_d, s_a, s_small, s_b, s_in, s_small, s_a, s_b, s_small, s_in,
            s_a, s_small, s_b, s_in, s_b, s_in,
        )
        advance(small, *order)
        flow = (s_in, s_small, s_d, s_a, s_b)
        share_in, small, share_down, share_a, share_b = (f.result() for f in flow)
    else:

        def share(grad):
            own = lax.psum_scatter(grad[0], "dp", scatter_dimension=0, tiled=True)
            return lax.psum(own, "seq").astype(f32)

        share_in, share_down, share_a, share_b = map(share, (*g_in, *grads))
        small = lax.psum(small, ("dp", "seq"))
    share_out = share_b[:, :width]
    share_gate = jnp.concatenate([share_a[:, :half], share_b[:, width : width + half]], axis=1)
    share_up = jnp.concatenate([share_a[:, half:], share_b[:, width + half :]], axis=1)
    modes = mode_rate.shape[0]
    return (
        layer_out, grad_hidden, share_in,
        small[row_bias : row_bias + 3].reshape(3 * width),
        small[row_short : row_short + 9].reshape(3, 3 * width),
        small[row_cond : row_cond + 3],
        small[row_res : row_res + modes],
        small[row_rate : row_rate + modes],
        share_out, small[row_one], small[row_one + 1], small[row_one + 2],
        share_gate, share_up, share_down, small[row_two], small[row_two + 1], small[row_two + 2],
    )


def solution(mesh):
    split, weight, full = P("dp", "seq", None), P("dp", None), P()
    in_specs = (
        split, P("dp"), P("dp"), weight, full, full, full, full, full, weight,
        full, full, full, weight, weight, weight, full, full, full, split,
    )
    out_specs = (
        split, split, weight, full, full, full, full, full, weight, full,
        full, full, weight, weight, weight, full, full, full,
    )
    return jax.shard_map(local, mesh=mesh, in_specs=in_specs, out_specs=out_specs, check_vma=False)
```
